32 devices in a mesh: dp: 8 (over z, x), pipe: 4 (over y, core).
Axes of the slice: x: 2, y: 2, z: 4, core: 2. Of those that a mesh axis runs over, the one named last changes fastest.
Arguments:
- tokens: bfloat16 [18816, 768], P('dp'), may hold values from -6 to 6
- cotangent: bfloat16 [18816, 768], P('dp'), may hold values from -6 to 6
- norm_gain: float32 [4, 768], P('pipe'), may hold values from 0.5 to 1.5
- norm_shift: float32 [4, 768], P('pipe'), may hold values from -1.5 to 1.5
- w_first: bfloat16 [4, 768, 3072], P('pipe'), may hold values from -1.5 to 1.5
- b_first: float32 [4, 3072], P('pipe'), may hold values from -1.5 to 1.5
- w_second: bfloat16 [4, 3072, 768], P('pipe'), may hold values from -0.109375 to 0.109375
- b_second: float32 [4, 768], P('pipe'), may hold values from -1.5 to 1.5
Outputs:
- layer_output: bfloat16 [18816, 768], P(('dp', 'pipe'))
- input_grad: bfloat16 [18816, 768], P(('dp', 'pipe'))
- grad_norm_gain: float32 [4, 768], P('pipe', 'dp')
- grad_norm_shift: float32 [4, 768], P('pipe', 'dp')
- grad_w_first: float32 [4, 768, 3072], P('pipe', 'dp')
- grad_b_first: float32 [4, 3072], P('pipe', 'dp')
- grad_w_second: float32 [4, 3072, 768], P('pipe', None, 'dp')
- grad_b_second: float32 [4, 768], P('pipe', 'dp')
The draws below stay inside these ranges and needn't reach their ends.
All inputs are finite; a program needn't handle non-finite values.
Results may differ from the reference program's by a relative error of at most 0.023.
Values may be sent and summed in bfloat16 or wider, within the bound.
A program may use at most 704 MiB of HBM per device.

```python
import jax
import jax.numpy as jnp
from jax import lax

D = 768
FF = 3072
HEADS = 24
HEAD_DIM = 32
PATCHES = 49
SECTIONS = 4
MICRO_ROWS = 588
TOKENS = 18816


def draw_w_first(key, part):
    key = jax.random.fold_in(key, 11)
    shape = (SECTIONS, D, FF)
    base = jnp.clip(jax.random.normal(key, shape, jnp.float32), -4.0, 4.0) * D ** (-0.5)
    column = lax.broadcasted_iota(jnp.int32, shape, 2)
    section_num = lax.broadcasted_iota(jnp.int32, shape, 0)
    boost = jnp.where((column >= 3 * D) & (section_num % 2 == 0), 3.0, 1.0)
    return (base * boost).astype(jnp.bfloat16)


def raised(values, key, source, target, parts, factor):
    def block_of(dim):
        return (jnp.arange(values.shape[dim]) // (values.shape[dim] // parts)).reshape((-1,) + (1,) * (values.ndim - 1 - dim))

    first = jax.random.permutation(key, parts)[block_of(target)]
    second = (block_of(target) + parts // 2) % parts
    return jnp.where((block_of(source) == first) | (block_of(source) == second), factor * values, values)


def block_scale(stream_key, shape, shards, low, largest):
    gain, own = 1.0, jax.random.fold_in(stream_key, 6)
    for axis_at, parts in shards:
        draws = jnp.exp(jax.random.uniform(jax.random.fold_in(own, axis_at), (parts,), jnp.float32, low / len(shards), largest / len(shards)))
        gain = gain * jnp.repeat(draws, shape[axis_at] // parts).reshape([-1 if axis == axis_at else 1 for axis in range(len(shape))])
    return gain


def bell_draw(key, dims, spread, reach, pieces=(), held_as=jnp.bfloat16):
    values = jax.random.normal(key, dims, jnp.float32) * spread
    if len(pieces) > 0:
        values = block_scale(key, dims, pieces, -0.22, 0.18) * values
    return jnp.clip(values, min=-reach, max=reach).astype(held_as)


def noise_with(stream_key, dims, deviation, reach, split, heavy, kind=jnp.bfloat16):
    values = deviation * jax.random.normal(stream_key, dims, jnp.float32)
    if split:
        values = values * block_scale(stream_key, dims, split, -0.22, 0.18)
    return jnp.clip(raised(values, jax.random.fold_in(stream_key, 3), *heavy), -reach, reach).astype(kind)


def setup_inputs(seed: int = 0) -> dict:
    streams_of = jax.random.split(jax.random.key(seed), 9)
    tokens = noise_with(streams_of[0], (TOKENS, D), 1.0, 6.0, ((0, 8),), (0, 1, 8, 2.0))
    cotangent = noise_with(streams_of[1], (TOKENS, D), 1.0, 6.0, ((0, 8),), (0, 1, 8, 2.0))
    norm_gain = jnp.clip(1.0 + 0.1 * jax.random.normal(streams_of[2], (SECTIONS, D), jnp.float32), 0.5, 1.5)
    norm_shift = bell_draw(streams_of[3], (SECTIONS, D), 0.3, 1.5, ((0, 4),), jnp.float32)
    w_first = draw_w_first(jax.random.fold_in(streams_of[8], 71), 0)
    b_first = bell_draw(streams_of[5], (SECTIONS, FF), 0.3, 1.5, ((0, 4),), jnp.float32)
    w_second = bell_draw(streams_of[6], (SECTIONS, FF, D), FF ** -0.5, 0.109375, ((0, 4),))
    b_second = bell_draw(streams_of[7], (SECTIONS, D), 0.3, 1.5, ((0, 4),), jnp.float32)
    return {"tokens": tokens, "cotangent": cotangent, "norm_gain": norm_gain, "norm_shift": norm_shift, "w_first": w_first, "b_first": b_first, "w_second": w_second, "b_second": b_second}


NORM_EPS = 1e-05
PRECISE = lax.Precision.HIGHEST

@jax.custom_vjp
def low(v):
    return lax.optimization_barrier(v.astype(jnp.bfloat16)).astype(jnp.float32)

@jax.custom_vjp
def low_back(v):
    return v

def low_keep(v):
    return (low(v), None)

def low_pass(kept, grad):
    return (grad,)

def back_keep(v):
    return (v, None)

def back_low(kept, grad):
    return (low(grad),)
low.defvjp(low_keep, low_pass)
low_back.defvjp(back_keep, back_low)

def matmul(former, latter):
    return jnp.dot(former, latter, precision=PRECISE, preferred_element_type=jnp.float32)

def layer_norm(values, gain_vec, shift_vec):
    center = values - lax.optimization_barrier(jnp.mean(values, -1, keepdims=True))
    variance = lax.optimization_barrier(jnp.mean(center * center, -1, keepdims=True))
    return center * lax.rsqrt(variance + NORM_EPS) * gain_vec + shift_vec

def attention_section(values, gain_vec, shift_vec, w_in, b_in, spatial):
    count = values.shape[0]
    images = count // PATCHES
    normed = low(layer_norm(values, gain_vec, shift_vec))
    projected = low(low_back(matmul(normed, w_in[:, :3 * D]) + b_in[:3 * D]))
    projected = projected.reshape(images, PATCHES, 3, HEADS, HEAD_DIM)
    queries = projected[:, :, 0]
    key_rows = projected[:, :, 1]
    value_rows = projected[:, :, 2]
    score_scale = HEAD_DIM ** (-0.5)
    if spatial:
        scores = jnp.einsum('bnhd,bmhd->bhnm', queries, key_rows, precision=PRECISE)
        attn_probs = jax.nn.softmax(low_back(scores * score_scale), axis=-1)
        attended = jnp.einsum('bhnm,bmhd->bnhd', low(attn_probs), value_rows, precision=PRECISE)
    else:
        scores = jnp.einsum('bnhc,bnhe->bhce', queries, key_rows, precision=PRECISE)
        attn_probs = jax.nn.softmax(low_back(scores * score_scale), axis=-1)
        attended = jnp.einsum('bhce,bnhe->bnhc', low(attn_probs), value_rows, precision=PRECISE)
    attended = low(low_back(attended.reshape(count, D)))
    branch = low_back(matmul(attended, w_in[:, 3 * D:]) + b_in[3 * D:])
    return values + branch

def mlp_section(values, gain_vec, shift_vec, w_in, b_in, w_out, b_out):
    normed = low(layer_norm(values, gain_vec, shift_vec))
    hidden = low_back(matmul(normed, w_in) + b_in)
    active = low(jax.nn.gelu(hidden, approximate=False))
    branch = low_back(matmul(active, w_out) + b_out)
    return values + branch

def forward_block(block_rows, params):
    gain_stack, shift_stack, w_in, b_in, w_out, b_out = params
    values = block_rows
    for section_num in range(SECTIONS):
        if section_num % 2 == 0:
            values = attention_section(values, gain_stack[section_num], shift_stack[section_num], w_in[section_num], b_in[section_num], section_num == 0)
        else:
            values = mlp_section(values, gain_stack[section_num], shift_stack[section_num], w_in[section_num], b_in[section_num], w_out[section_num], b_out[section_num])
        if section_num < SECTIONS - 1:
            values = low_back(low(values))
    return low(values)

def forward_all(inputs, params):
    blocks = inputs.reshape(-1, MICRO_ROWS, D)
    checked = jax.checkpoint(forward_block)

    def one_block(block_rows):
        return checked(block_rows, params)
    outputs = lax.map(one_block, blocks)
    return outputs.reshape(-1, D)

def reference(tokens, cotangent, norm_gain, norm_shift, w_first, b_first, w_second, b_second):
    params = (norm_gain.astype(jnp.float32), norm_shift.astype(jnp.float32), w_first.astype(jnp.float32), b_first.astype(jnp.float32), w_second.astype(jnp.float32), b_second.astype(jnp.float32))
    inputs = tokens.astype(jnp.float32)
    outputs, pullback = jax.vjp(forward_all, inputs, params)
    grad_in, grad_params = pullback(cotangent.astype(jnp.float32))
    return (outputs.astype(jnp.bfloat16), grad_in.astype(jnp.bfloat16), grad_params[0], grad_params[1], grad_params[2], grad_params[3], grad_params[4], grad_params[5])
```

```python
import functools

import jax
import jax.experimental.pallas as pl
import jax.experimental.pallas.tpu as pltpu
import jax.numpy as jnp
from jax import lax
from jax.sharding import PartitionSpec as P

D = 768
FF = 3072
PATCHES = 49
PAD = 64
EPS = 1e-05
SCALE = 32 ** (-0.5)
MICROS = 4
MEMBERS = 8
BLOCK = D // MEMBERS
WIDE = 384
MESH = pl.DeviceIdType.MESH
BF = jnp.bfloat16
F32 = jnp.float32


def dot(a, b, ca, cb):
    return lax.dot_general(a, b, (((ca,), (cb,)), ((), ())), preferred_element_type=F32)


def gelu_pair(h):
    t = 1.0 / (1.0 + 0.3275911 * 0.7071067811865476 * jnp.abs(h))
    poly = t * (0.127414796 + t * (-0.142248368 + t * (0.7107068705 + t * (-0.7265760135 + t * 0.5307027145))))
    bell = jnp.exp(-0.5 * h * h)
    tail = poly * bell
    cdf = jnp.where(h >= 0, 1.0 - tail, tail)
    return h * cdf, cdf + h * (0.3989422804014327 * bell)


def norm_parts(x):
    center = x - jnp.mean(x, -1, keepdims=True)
    inverse = lax.rsqrt(jnp.mean(center * center, -1, keepdims=True) + EPS)
    return center * inverse, inverse


def head_masks(width):
    lane = lax.broadcasted_iota(jnp.int32, (1, width), 1) // 32
    return [lane == h for h in range(width // 32)]


def spread(block, masks):
    return jnp.concatenate([jnp.where(m, block, jnp.zeros_like(block)) for m in masks], 0)


def gather_heads(stacked, masks):
    total = None
    for h, m in enumerate(masks):
        part = jnp.where(m, stacked[PAD * h : PAD * (h + 1)], 0.0)
        total = part if total is None else total + part
    return total


def window_forward(q, k, v):
    eight, four = head_masks(256), head_masks(128)
    scores = dot(k, spread(q, eight), 1, 1)
    row = lax.broadcasted_iota(jnp.int32, (PAD, 1), 0)
    scores = jnp.where(row < PATCHES, scores, -1e30)
    top = jnp.max(scores, 0, keepdims=True)
    e = jnp.exp((scores - top) * SCALE)
    probs = (e * (1.0 / jnp.sum(e, 0, keepdims=True))).astype(BF)
    halves = []
    for a in range(2):
        stacked = dot(probs[:, 256 * a : 256 * (a + 1)], v[:, 128 * a : 128 * (a + 1)], 0, 0)
        halves.append(gather_heads(stacked, four))
    return probs, jnp.concatenate(halves, 1)


def window_backward(q, k, v, probs, d_att):
    eight, four = head_masks(256), head_masks(128)
    d_wide = spread(d_att, eight)
    d_probs = dot(v, d_wide, 1, 1)
    p = probs.astype(F32)
    d_scores = p * (d_probs - jnp.sum(p * d_probs, 0, keepdims=True))
    d_scores = d_scores.astype(BF)
    d_v = dot(probs, d_wide, 1, 0)
    d_k = dot(d_scores, spread(q, eight), 1, 0) * SCALE
    halves = []
    for a in range(2):
        stacked = dot(d_scores[:, 256 * a : 256 * (a + 1)], k[:, 128 * a : 128 * (a + 1)], 0, 0)
        halves.append(gather_heads(stacked, four))
    return jnp.concatenate(halves, 1) * SCALE, d_k, d_v


def channel_forward(q, k, v):
    scores = dot(q, k, 0, 0)
    r = lax.broadcasted_iota(jnp.int32, (128, 128), 0) // 32
    c = lax.broadcasted_iota(jnp.int32, (128, 128), 1) // 32
    scores = jnp.where(r == c, scores, -1e30)
    e = jnp.exp((scores - jnp.max(scores, 1, keepdims=True)) * SCALE)
    probs = (e * (1.0 / jnp.sum(e, 1, keepdims=True))).astype(BF)
    return probs, dot(v, probs, 1, 1)


def channel_backward(q, k, v, probs, d_att):
    d_probs = dot(d_att, v, 0, 0)
    p = probs.astype(F32)
    d_scores = (p * (d_probs - jnp.sum(p * d_probs, 1, keepdims=True))).astype(BF)
    d_v = dot(d_att, probs, 1, 0)
    d_q = dot(k, d_scores, 1, 1) * SCALE
    d_k = dot(q, d_scores, 1, 0) * SCALE
    return d_q, d_k, d_v


def sections_kernel(
    micros, rows, real,
    x_ref, par_ref, w1_ref, w2_ref,
    lo_ref, ig_ref, left_ref, right_ref, small_ref,
    w1, w2, par, xs, arr, snd, fin, mid, slope, qkv, probs_w, probs_c,
    att_in, normed_a, att_low, normed_f, act, d_proj, g_mid, d_att, wide_tmp, acc, tmp,
    w_local, w_send, w_recv, x_sem, s_send, s_recv, f_send, f_recv, f_local, o_sem, keep_sem,
):
    dp, pipe = lax.axis_index("dp"), lax.axis_index("pipe")
    y, core = pipe // 2, pipe % 2
    sibling = (dp, 2 * y + 1 - core)
    across = (dp, 2 * (1 - y) + core)
    images = real // PATCHES
    half = micros // 2

    barrier = pltpu.get_barrier_semaphore()
    pl.semaphore_signal(barrier, inc=1, device_id=sibling, device_id_type=MESH)
    pl.semaphore_signal(barrier, inc=1, device_id=across, device_id_type=MESH)

    own_x = pltpu.make_async_copy(x_ref, xs, x_sem)
    own_x.start()
    own_1 = pltpu.make_async_copy(w1_ref, w1.at[core], w_local.at[0])
    own_1.start()
    own_2 = pltpu.make_async_copy(w2_ref, w2, w_local.at[1])
    own_p = pltpu.make_async_copy(par_ref, par.at[core], w_local.at[2])
    own_p.start()
    pl.semaphore_wait(barrier, 2)

    def to_sibling(src, dst, n):
        return pltpu.make_async_remote_copy(
            src_ref=src, dst_ref=dst, send_sem=w_send.at[n], recv_sem=w_recv.at[n],
            device_id=sibling, device_id_type=MESH,
        )

    send_p = to_sibling(par_ref, par.at[core], 2)
    send_1 = to_sibling(w1_ref, w1.at[core], 0)
    send_2 = to_sibling(w2_ref, w2, 1)
    send_p.start()
    send_1.start()

    @pl.when(core == 1)
    def _():
        send_2.start()
        own_2.start()

    small_ref[...] = jnp.zeros_like(small_ref)
    tmp[pl.ds(rows, tmp.shape[0] - rows), :] = jnp.zeros((tmp.shape[0] - rows, 3 * D), F32)
    own_x.wait()
    own_p.wait()
    to_sibling(par_ref, par.at[1 - core], 2).wait_recv()

    @pl.when(core == 0)
    def _():
        own_1.wait()

    @pl.when(core == 1)
    def _():
        to_sibling(w1_ref, w1.at[1 - core], 0).wait_recv()

    def feed_weights():
        @pl.when(core == 1)
        def _():
            own_1.wait()
            own_2.wait()

        @pl.when(core == 0)
        def _():
            to_sibling(w1_ref, w1.at[1 - core], 0).wait_recv()
            to_sibling(w2_ref, w2, 1).wait_recv()

    def out_rows(m):
        return pl.ds(pl.multiple_of(m * rows, 16), rows)

    def put_left(n, m, src):
        return pltpu.make_async_copy(src, left_ref.at[n, out_rows(m)], o_sem.at[n])

    def put_right(n, m, src, start):
        return pltpu.make_async_copy(
            src, right_ref.at[out_rows(m), pl.ds(start, src.shape[-1])], o_sem.at[4 + n]
        )

    kept_start = ((0, normed_f), (2, normed_a), (3, att_low))

    def wait_left(m, n, src):
        @pl.when(m > 0)
        def _():
            put_left(n, m, src).wait()

    def wait_right(m, n, src, start):
        @pl.when(m > 0)
        def _():
            put_right(n, m, src, start).wait()

    row = lax.broadcasted_iota(jnp.int32, (PAD, 1), 0)

    def stage(src, dst, first, cols):
        for i in range(images):
            for c in range(0, cols, D):
                part = src[PATCHES * i : PATCHES * i + PAD, c : c + D]
                dst[first + i, :, c : c + D] = jnp.where(row < PATCHES, part, 0.0).astype(BF)

    def attention_forward(m, x_in, spatial):
        x = x_in[m].astype(F32)
        scaled, _ = norm_parts(x)
        wait_left(m, 2, normed_a)
        normed_a[...] = (scaled * par[0, 1:2, :D] + par[0, 1:2, D : 2 * D]).astype(BF)
        put_left(2, m, normed_a).start()
        for c in range(0, 3 * D, D):
            tmp[0:rows, c : c + D] = dot(normed_a[...], w1[0, :, c : c + D], 1, 0) + par[0, 0:1, c : c + D]
        first = m * images if spatial else 0
        stage(tmp, qkv, first, 3 * D)

        def one_image(i, carry):
            if spatial:
                for g in range(3):
                    s = 256 * g
                    p, a = window_forward(
                        qkv[first + i, :, s : s + 256],
                        qkv[first + i, :, D + s : D + s + 256],
                        qkv[first + i, :, 2 * D + s : 2 * D + s + 256],
                    )
                    probs_w[first + i, :, 512 * g : 512 * (g + 1)] = p
                    att_in[i, :, s : s + 256] = a
            else:
                for g in range(6):
                    s = 128 * g
                    p, a = channel_forward(
                        qkv[first + i, :, s : s + 128],
                        qkv[first + i, :, D + s : D + s + 128],
                        qkv[first + i, :, 2 * D + s : 2 * D + s + 128],
                    )
                    probs_c[i, s : s + 128, :] = p
                    att_in[i, :, s : s + 128] = a
            return carry

        lax.fori_loop(0, images, one_image, 0)
        for i in range(images):
            acc[PATCHES * i : PATCHES * i + PAD, :] = att_in[i]
        acc[real:rows, :] = jnp.zeros((rows - real, D), F32)
        wait_left(m, 3, att_low)
        att_low[...] = acc[0:rows, :].astype(BF)
        put_left(3, m, att_low).start()
        branch = dot(att_low[...], w1[0, :, 3 * D :], 1, 0) + par[0, 0:1, 3 * D :]
        mid[m] = (x + branch).astype(BF)

    def feed_forward(m, dst):
        x = mid[m].astype(F32)
        scaled, _ = norm_parts(x)
        wait_left(m, 0, normed_f)
        normed_f[...] = (scaled * par[1, 1:2, :D] + par[1, 1:2, D : 2 * D]).astype(BF)
        put_left(0, m, normed_f).start()
        wait_right(m, 0, act, FF)
        acc[0:rows, :] = x + par[1, 1:2, 2 * D : 3 * D]
        for c in range(0, FF, D):
            hidden = dot(normed_f[...], w1[1, :, c : c + D], 1, 0) + par[1, 0:1, c : c + D]
            value, diff = gelu_pair(hidden)
            act[:, c : c + D] = value.astype(BF)
            slope[m, :, c : c + D] = diff.astype(BF)
            acc[0:rows, :] += dot(act[:, c : c + D], w2[c : c + D, :], 1, 0)
        put_right(0, m, act, FF).start()
        dst[m] = acc[0:rows, :].astype(BF)

    def norm_back(d_normed, x, gain, at):
        scaled, inverse = norm_parts(x)
        small_ref[at : at + 1, :D] += jnp.sum(d_normed * scaled, 0, keepdims=True)
        small_ref[at : at + 1, D : 2 * D] += jnp.sum(d_normed, 0, keepdims=True)
        d_scaled = d_normed * gain
        mean = jnp.mean(d_scaled, -1, keepdims=True)
        cross = jnp.mean(d_scaled * scaled, -1, keepdims=True)
        return inverse * (d_scaled - mean - scaled * cross)

    def keep_gout(m, g_in):
        return pltpu.make_async_copy(g_in.at[m], left_ref.at[1, out_rows(m)], keep_sem.at[0, m])

    def keep_hidden(m):
        return pltpu.make_async_copy(slope.at[m], right_ref.at[out_rows(m), pl.ds(0, FF)], keep_sem.at[1, m])

    def feed_backward(m, g_in):
        keep_gout(m, g_in).start()
        small_ref[3:4, 2 * D : 3 * D] += jnp.sum(g_in[m].astype(F32), 0, keepdims=True)
        for c in range(0, FF, D):
            d_act = dot(g_in[m], w2[c : c + D, :], 1, 1)
            d_hid = (d_act * slope[m, :, c : c + D].astype(F32)).astype(BF)
            slope[m, :, c : c + D] = d_hid
            small_ref[2:3, c : c + D] += jnp.sum(d_hid.astype(F32), 0, keepdims=True)
            back = dot(d_hid, w1[1, :, c : c + D], 1, 1)
            if c == 0:
                acc[0:rows, :] = back
            else:
                acc[0:rows, :] += back
        keep_hidden(m).start()
        back = norm_back(acc[0:rows, :], mid[m].astype(F32), par[1, 1:2, :D], 3)
        wait_right(m, 2, g_mid, 3 * FF - D)
        g_mid[...] = (g_in[m].astype(F32) + back).astype(BF)
        put_right(2, m, g_mid, 3 * FF - D).start()

    def attention_backward(m, x_in, dst, spatial):
        g = g_mid[...]
        small_ref[0:1, 3 * D :] += jnp.sum(g.astype(F32), 0, keepdims=True)
        acc[0:rows, :] = dot(g, w1[0, :, 3 * D :], 1, 1)
        stage(acc, d_att, 0, D)
        first = m * images if spatial else 0

        def one_image(i, carry):
            if spatial:
                for n in range(3):
                    s = 256 * n
                    d_q, d_k, d_v = window_backward(
                        qkv[first + i, :, s : s + 256],
                        qkv[first + i, :, D + s : D + s + 256],
                        qkv[first + i, :, 2 * D + s : 2 * D + s + 256],
                        probs_w[first + i, :, 512 * n : 512 * (n + 1)],
                        d_att[i, :, s : s + 256],
                    )
                    wide_tmp[i, :, s : s + 256] = d_q
                    wide_tmp[i, :, D + s : D + s + 256] = d_k
                    wide_tmp[i, :, 2 * D + s : 2 * D + s + 256] = d_v
            else:
                for n in range(6):
                    s = 128 * n
                    d_q, d_k, d_v = channel_backward(
                        qkv[first + i, :, s : s + 128],
                        qkv[first + i, :, D + s : D + s + 128],
                        qkv[first + i, :, 2 * D + s : 2 * D + s + 128],
                        probs_c[i, s : s + 128, :],
                        d_att[i, :, s : s + 128],
                    )
                    wide_tmp[i, :, s : s + 128] = d_q
                    wide_tmp[i, :, D + s : D + s + 128] = d_k
                    wide_tmp[i, :, 2 * D + s : 2 * D + s + 128] = d_v
            return carry

        lax.fori_loop(0, images, one_image, 0)
        for i in range(images):
            for c in range(0, 3 * D, D):
                tmp[PATCHES * i : PATCHES * i + PAD, c : c + D] = wide_tmp[i, :, c : c + D]
        tmp[real:rows, :] = jnp.zeros((rows - real, 3 * D), F32)
        wait_right(m, 1, d_proj, 2 * FF)
        d_proj[...] = tmp[0:rows, :].astype(BF)
        put_right(1, m, d_proj, 2 * FF).start()
        small_ref[0:1, : 3 * D] += jnp.sum(d_proj[...].astype(F32), 0, keepdims=True)
        d_normed = dot(d_proj[...], w1[0, :, : 3 * D], 1, 1)
        back = norm_back(d_normed, x_in[m].astype(F32), par[0, 1:2, :D], 1)
        dst[m] = (g.astype(F32) + back).astype(BF)

    def hop(m):
        return pltpu.make_async_remote_copy(
            src_ref=snd.at[m], dst_ref=arr.at[m], send_sem=s_send.at[m], recv_sem=s_recv.at[m],
            device_id=across, device_id_type=MESH,
        )

    def final_hop(m, ref, slot):
        return pltpu.make_async_remote_copy(
            src_ref=fin.at[m], dst_ref=ref.at[slot], send_sem=f_send.at[slot], recv_sem=f_recv.at[slot],
            device_id=across, device_id_type=MESH,
        )

    def final_own(m, ref, slot):
        return pltpu.make_async_copy(fin.at[m], ref.at[slot], f_local.at[slot])

    @pl.when(y == 0)
    def _():
        def forward(m, carry):
            attention_forward(m, xs, True)

            @pl.when(m == 0)
            def _():
                feed_weights()

            feed_forward(m, snd)
            hop(m).start()
            return carry

        lax.fori_loop(0, micros, forward, 0)

        def backward(m, carry):
            hop(m).wait_recv()
            feed_backward(m, arr)
            attention_backward(m, xs, fin, True)

            @pl.when(m < half)
            def _():
                final_hop(m, ig_ref, m).start()

            @pl.when(m >= half)
            def _():
                final_own(m, ig_ref, m - half).start()

            return carry

        lax.fori_loop(0, micros, backward, 0)

        def finish(n, carry):
            final_hop(n, ig_ref, n).wait_send()
            final_hop(n, lo_ref, n).wait_recv()
            final_own(n, ig_ref, n).wait()
            return carry

        lax.fori_loop(0, half, finish, 0)

        def kept(m, carry):
            keep_gout(m, arr).wait()
            return carry

        lax.fori_loop(0, micros, kept, 0)

    @pl.when(y == 1)
    def _():
        def both(m, carry):
            hop(m).wait_recv()
            attention_forward(m, arr, False)

            @pl.when(m == 0)
            def _():
                feed_weights()

            feed_forward(m, fin)

            @pl.when(m < half)
            def _():
                final_own(m, lo_ref, m).start()

            feed_backward(m, xs)
            attention_backward(m, arr, snd, False)
            hop(m).start()

            @pl.when(m >= half)
            def _():
                final_hop(m, lo_ref, m - half).start()

            return carry

        lax.fori_loop(0, micros, both, 0)

        def finish(n, carry):
            final_hop(n, lo_ref, n).wait_send()
            final_hop(n, ig_ref, n).wait_recv()
            final_own(n, lo_ref, n).wait()
            return carry

        lax.fori_loop(0, half, finish, 0)

        def kept(m, carry):
            keep_gout(m, xs).wait()
            return carry

        lax.fori_loop(0, micros, kept, 0)

    def sent(m, carry):
        hop(m).wait_send()
        keep_hidden(m).wait()
        return carry

    lax.fori_loop(0, micros, sent, 0)
    last = micros - 1
    put_left(0, last, normed_f).wait()
    put_left(2, last, normed_a).wait()
    put_left(3, last, att_low).wait()
    put_right(0, last, act, FF).wait()
    put_right(1, last, d_proj, 2 * FF).wait()
    put_right(2, last, g_mid, 3 * FF - D).wait()
    send_p.wait_send()
    send_1.wait_send()

    @pl.when(core == 1)
    def _():
        send_2.wait_send()


def run_sections(x, par, w1, w2, micros, rows, real):
    images = real // PATCHES
    half = micros // 2
    tall = (PATCHES * (images - 1) + PAD + 7) // 8 * 8
    tall = max(tall, rows)
    hbm = pl.BlockSpec(memory_space=pl.ANY)
    vmem = pl.BlockSpec(memory_space=pltpu.VMEM)
    dma = pltpu.SemaphoreType.DMA
    scratch = [
        pltpu.VMEM((2, D, FF), BF),
        pltpu.VMEM((FF, D), BF),
        pltpu.VMEM((2, 8, FF), F32),
        pltpu.VMEM((micros, rows, D), BF),
        pltpu.VMEM((micros, rows, D), BF),
        pltpu.VMEM((micros, rows, D), BF),
        pltpu.VMEM((micros, rows, D), BF),
        pltpu.VMEM((micros, rows, D), BF),
        pltpu.VMEM((micros, rows, FF), BF),
        pltpu.VMEM((micros * images, PAD, 3 * D), BF),
        pltpu.VMEM((micros * images, PAD, 3 * 512), BF),
        pltpu.VMEM((images, D, 128), BF),
        pltpu.VMEM((images, PAD, D), F32),
        pltpu.VMEM((rows, D), BF),
        pltpu.VMEM((rows, D), BF),
        pltpu.VMEM((rows, D), BF),
        pltpu.VMEM((rows, FF), BF),
        pltpu.VMEM((rows, 3 * D), BF),
        pltpu.VMEM((rows, D), BF),
        pltpu.VMEM((images, PAD, D), BF),
        pltpu.VMEM((images, PAD, 3 * D), F32),
        pltpu.VMEM((tall, D), F32),
        pltpu.VMEM((tall, 3 * D), F32),
        dma((3,)), dma((3,)), dma((3,)), dma(()),
        dma((micros,)), dma((micros,)), dma((half,)), dma((half,)), dma((half,)),
        dma((7,)), dma((2, micros)),
    ]
    out_shape = (
        jax.ShapeDtypeStruct((half, rows, D), BF),
        jax.ShapeDtypeStruct((half, rows, D), BF),
        jax.ShapeDtypeStruct((4, micros * rows, D), BF),
        jax.ShapeDtypeStruct((micros * rows, 3 * FF), BF),
        jax.ShapeDtypeStruct((8, FF), F32),
    )
    flops = 2 * 6 * 3 * D * D * 4 * micros * rows
    return pl.pallas_call(
        functools.partial(sections_kernel, micros, rows, real),
        out_shape=out_shape,
        in_specs=[hbm, vmem, hbm, hbm],
        out_specs=(hbm, hbm, hbm, hbm, vmem),
        scratch_shapes=scratch,
        compiler_params=pltpu.CompilerParams(
            collective_id=0, has_side_effects=True, vmem_limit_bytes=63 * 2**20
        ),
        cost_estimate=pl.CostEstimate(flops=flops, bytes_accessed=60_000_000, transcendentals=0),
        name="sections",
    )(x, par, w1, w2)


LAG_SUM, LAG_Z, LAG_OUT = 1, 4, 7
RING = 4


def weights_kernel(
    inner, left_ref, right_ref, out_ref,
    left, ring, part, sib, from_x, from_z,
    l_sem, r_sem, c_send, c_recv, x_send, x_recv, z_send, z_recv,
):
    dp, pipe = lax.axis_index("dp"), lax.axis_index("pipe")
    y, core = pipe // 2, pipe % 2
    outer, rest = dp // inner, dp % inner
    z, x = outer // 2, outer % 2
    lines = MEMBERS // 2
    per = FF // WIDE
    steps = 3 * per

    def at(zz, xx):
        return ((zz * 2 + xx) * inner + rest, pipe)

    sibling = (dp, 2 * y + 1 - core)
    x_peer = at(z, 1 - x)

    barrier = pltpu.get_barrier_semaphore()
    pl.semaphore_signal(barrier, inc=1, device_id=sibling, device_id_type=MESH)
    pl.semaphore_signal(barrier, inc=1, device_id=x_peer, device_id_type=MESH)
    for i in range(1, lines):
        pl.semaphore_signal(barrier, inc=1, device_id=at((z + i) % lines, x), device_id_type=MESH)

    def load_left(n):
        return pltpu.make_async_copy(left_ref.at[n], left.at[n], l_sem.at[n])

    def load_right(k):
        cols = pl.ds(pl.multiple_of(k * WIDE, 128), WIDE)
        return pltpu.make_async_copy(right_ref.at[:, cols], ring.at[k % RING], r_sem.at[k % RING])

    load_left(0).start()
    load_right(0).start()
    load_left(1).start()
    for k in range(1, RING - 1):
        load_right(k).start()
    load_left(2).start()
    load_left(3).start()
    pl.semaphore_wait(barrier, 1 + lines)

    def owner(k):
        is_attn = k // (2 * per)
        return 1 - is_attn, k - is_attn * 2 * per

    def to_sibling(k, j):
        return pltpu.make_async_remote_copy(
            src_ref=part.at[k], dst_ref=sib.at[j], send_sem=c_send.at[k], recv_sem=c_recv.at[j],
            device_id=sibling, device_id_type=MESH,
        )

    def to_x(k, j):
        return pltpu.make_async_remote_copy(
            src_ref=part.at[k, :, 1 - x], dst_ref=from_x.at[j], send_sem=x_send.at[j], recv_sem=x_recv.at[j],
            device_id=x_peer, device_id_type=MESH,
        )

    def to_z(k, j, zz):
        return pltpu.make_async_remote_copy(
            src_ref=part.at[k, zz, x], dst_ref=from_z.at[j, z], send_sem=z_send.at[j, zz],
            recv_sem=z_recv.at[j, z], device_id=at(zz, x), device_id_type=MESH,
        )

    def arrived_z(k, j, zz):
        return pltpu.make_async_remote_copy(
            src_ref=part.at[k, zz, x], dst_ref=from_z.at[j, zz], send_sem=z_send.at[j, zz],
            recv_sem=z_recv.at[j, zz], device_id=at(zz, x), device_id_type=MESH,
        )

    load_left(0).wait()

    def step(s, carry):
        @pl.when(s < steps)
        def _():
            k = s
            for n in range(1, 4):
                edge = (per, 2 * per, 3 * per - D // WIDE)[n - 1]

                @pl.when(k == edge)
                def _():
                    load_left(n).wait()

            load_right(k).wait()

            @pl.when(k + RING - 1 < steps)
            def _():
                load_right(k + RING - 1).start()

            which = k // per + k // (3 * per - D // WIDE)
            product = dot(left[which], ring[k % RING], 0, 0)
            part[k] = product.astype(BF).reshape(lines, 2, BLOCK, WIDE)
            own, j = owner(k)

            @pl.when(own != core)
            def _():
                to_sibling(k, j).start()

        k1 = s - LAG_SUM

        @pl.when((k1 >= 0) & (k1 < steps))
        def _():
            own, j = owner(k1)

            @pl.when(own == core)
            def _():
                to_sibling(k1, j).wait_recv()
                part[k1] = (part[k1].astype(F32) + sib[j].astype(F32)).astype(BF)
                to_x(k1, j).start()

        k2 = s - LAG_Z

        @pl.when((k2 >= 0) & (k2 < steps))
        def _():
            own, j = owner(k2)

            @pl.when(own == core)
            def _():
                to_x(k2, j).wait_recv()
                part[k2, :, x] = (part[k2, :, x].astype(F32) + from_x[j].astype(F32)).astype(BF)
                for i in range(1, lines):
                    to_z(k2, j, (z + i) % lines).start()

        k3 = s - LAG_OUT

        @pl.when((k3 >= 0) & (k3 < steps))
        def _():
            own, j = owner(k3)

            @pl.when(own == core)
            def _():
                total = part[k3, z, x].astype(F32)
                for i in range(1, lines):
                    zz = (z + i) % lines
                    arrived_z(k3, j, zz).wait_recv()
                    total += from_z[j, zz].astype(F32)
                out_ref[j // per, :, pl.ds(pl.multiple_of((j % per) * WIDE, 128), WIDE)] = total

        return carry

    lax.fori_loop(0, steps + LAG_OUT, step, 0)

    def drain(k, carry):
        own, j = owner(k)

        @pl.when(own != core)
        def _():
            to_sibling(k, j).wait_send()

        @pl.when(own == core)
        def _():
            to_x(k, j).wait_send()
            for i in range(1, lines):
                to_z(k, j, (z + i) % lines).wait_send()

        return carry

    lax.fori_loop(0, steps, drain, 0)


def reduce_weights(left, right, inner):
    count = left.shape[1]
    lines = MEMBERS // 2
    per = FF // WIDE
    hbm = pl.BlockSpec(memory_space=pl.ANY)
    vmem = pl.BlockSpec(memory_space=pltpu.VMEM)
    dma = pltpu.SemaphoreType.DMA
    return pl.pallas_call(
        functools.partial(weights_kernel, inner),
        out_shape=jax.ShapeDtypeStruct((2, BLOCK, FF), F32),
        in_specs=[hbm, hbm],
        out_specs=vmem,
        scratch_shapes=[
            pltpu.VMEM((4, count, D), BF),
            pltpu.VMEM((RING, count, WIDE), BF),
            pltpu.VMEM((3 * per, lines, 2, BLOCK, WIDE), BF),
            pltpu.VMEM((2 * per, lines, 2, BLOCK, WIDE), BF),
            pltpu.VMEM((2 * per, lines, BLOCK, WIDE), BF),
            pltpu.VMEM((2 * per, lines, BLOCK, WIDE), BF),
            dma((4,)), dma((RING,)), dma((3 * per,)), dma((2 * per,)), dma((2 * per,)), dma((2 * per,)),
            dma((2 * per, lines)), dma((2 * per, lines)),
        ],
        compiler_params=pltpu.CompilerParams(
            collective_id=1, has_side_effects=True, vmem_limit_bytes=63 * 2**20
        ),
        cost_estimate=pl.CostEstimate(
            flops=2 * 3 * D * FF * count, bytes_accessed=40_000_000, transcendentals=0
        ),
        name="weights",
    )(left, right)


def on_device(tokens, cotangent, norm_gain, norm_shift, w_first, b_first, w_second, b_second):
    pipe = lax.axis_index("pipe")
    dp = lax.axis_index("dp")
    groups = lax.axis_size("dp")
    y, core = pipe // 2, pipe % 2
    inner = groups // MEMBERS
    share = tokens.shape[0] // 4
    micros = MICROS
    real = 2 * share // micros
    rows = (real + 15) // 16 * 16

    def own_rows(whole):
        parts = whole.reshape(2, 2, share, D)
        picked = lax.dynamic_index_in_dim(parts, core, 1, keepdims=False)
        return picked[::-1].reshape(micros, real, D)

    x = jnp.where(y == 0, own_rows(tokens), own_rows(cotangent))
    x = jnp.pad(x, ((0, 0), (0, rows - real), (0, 0)))
    line = jnp.concatenate([norm_gain, norm_shift, b_second, jnp.zeros((1, FF - 3 * D), F32)], 1)
    par = jnp.concatenate([b_first, line, jnp.zeros((6, FF), F32)], 0)
    lo, ig, left, right, small = run_sections(x, par, w_first[0], w_second[0], micros, rows, real)
    layer_out = lo[:, :real].reshape(share, D)
    input_grad = ig[:, :real].reshape(share, D)
    grads = reduce_weights(left, right, inner)

    pairs = small[:4].reshape(2, 2, FF)
    mine = lax.dynamic_index_in_dim(pairs, core, 0, keepdims=False)
    other = lax.dynamic_index_in_dim(pairs, 1 - core, 0, keepdims=False)
    swap = [(i, i + 1 - 2 * (i % 2)) for i in range(4)]
    mine = mine + lax.ppermute(other, "pipe", swap)
    mine = lax.psum(mine, "dp")

    def piece(vec):
        size = vec.shape[0] // groups
        return lax.dynamic_slice_in_dim(vec, dp * size, size, 0)[None]

    if inner > 1:
        members = [[o * inner + i for i in range(inner)] for o in range(MEMBERS)]
        grads = lax.psum_scatter(
            grads, "dp", scatter_dimension=1, axis_index_groups=members, tiled=True
        )
    g_first = grads[0][None]
    g_second = jnp.where(core == 1, grads[1], 0.0).T[None]
    return (
        layer_out,
        input_grad,
        piece(mine[1, :D]),
        piece(mine[1, D : 2 * D]),
        g_first,
        piece(mine[0]),
        g_second,
        piece(mine[1, 2 * D : 3 * D]),
    )


def solution(mesh):
    in_specs = (
        P("dp", None), P("dp", None), P("pipe", None), P("pipe", None),
        P("pipe", None, None), P("pipe", None), P("pipe", None, None), P("pipe", None),
    )
    out_specs = (
        P(("dp", "pipe"), None), P(("dp", "pipe"), None), P("pipe", "dp"), P("pipe", "dp"),
        P("pipe", "dp", None), P("pipe", "dp"), P("pipe", None, "dp"), P("pipe", "dp"),
    )
    return jax.shard_map(
        on_device, mesh=mesh, in_specs=in_specs, out_specs=out_specs, check_vma=False
    )
```

```python
import functools

import jax
import jax.experimental.pallas as pl
import jax.experimental.pallas.tpu as pltpu
import jax.numpy as jnp
from jax import lax
from jax.sharding import PartitionSpec as P

D = 768
FF = 3072
PATCHES = 49
PAD = 64
EPS = 1e-05
SCALE = 32 ** (-0.5)
MICROS = 8
MEMBERS = 8
BLOCK = D // MEMBERS
WIDE = 384
MESH = pl.DeviceIdType.MESH
BF = jnp.bfloat16
F32 = jnp.float32


def dot(a, b, ca, cb):
    return lax.dot_general(a, b, (((ca,), (cb,)), ((), ())), preferred_element_type=F32)


def gelu_pair(h):
    t = 1.0 / (1.0 + 0.3275911 * 0.7071067811865476 * jnp.abs(h))
    poly = t * (0.127414796 + t * (-0.142248368 + t * (0.7107068705 + t * (-0.7265760135 + t * 0.5307027145))))
    bell = jnp.exp(-0.5 * h * h)
    tail = poly * bell
    cdf = jnp.where(h >= 0, 1.0 - tail, tail)
    return h * cdf, cdf + h * (0.3989422804014327 * bell)


def norm_parts(x):
    center = x - jnp.mean(x, -1, keepdims=True)
    inverse = lax.rsqrt(jnp.mean(center * center, -1, keepdims=True) + EPS)
    return center * inverse, inverse


def head_masks(width):
    lane = lax.broadcasted_iota(jnp.int32, (1, width), 1) // 32
    return [lane == h for h in range(width // 32)]


def spread(block, masks):
    return jnp.concatenate([jnp.where(m, block, jnp.zeros_like(block)) for m in masks], 0)


def gather_heads(stacked, masks):
    total = None
    for h, m in enumerate(masks):
        part = jnp.where(m, stacked[PAD * h : PAD * (h + 1)], 0.0)
        total = part if total is None else total + part
    return total


def window_forward(q, k, v):
    eight, four = head_masks(256), head_masks(128)
    row = lax.broadcasted_iota(jnp.int32, (PAD, 1), 0)
    scores = [
        dot(k[:, s : s + 256], spread(q[:, s : s + 256], eight), 1, 1) for s in range(0, D, 256)
    ]
    probs = []
    for block in scores:
        block = jnp.where(row < PATCHES, block, -1e30)
        e = jnp.exp((block - jnp.max(block, 0, keepdims=True)) * SCALE)
        probs.append((e * (1.0 / jnp.sum(e, 0, keepdims=True))).astype(BF))
    parts = []
    for n in range(D // 128):
        cols = slice(256 * (n % 2), 256 * (n % 2) + 256)
        parts.append(dot(probs[n // 2][:, cols], v[:, 128 * n : 128 * n + 128], 0, 0))
    parts = [gather_heads(part, four) for part in parts]
    return jnp.concatenate(probs, 1), jnp.concatenate(parts, 1)


def window_backward(q, k, v, probs, d_att):
    eight, four = head_masks(256), head_masks(128)
    starts = range(0, D, 256)
    wide = [spread(d_att[:, s : s + 256], eight) for s in starts]
    d_probs = [dot(v[:, s : s + 256], wide[n], 1, 1) for n, s in enumerate(starts)]
    d_v = [dot(probs[:, 2 * s : 2 * s + 512], wide[n], 1, 0) for n, s in enumerate(starts)]
    d_scores = []
    for n, s in enumerate(starts):
        p = probs[:, 2 * s : 2 * s + 512].astype(F32)
        product = p * d_probs[n]
        d_scores.append((product - p * jnp.sum(product, 0, keepdims=True)).astype(BF))
    d_k = [
        dot(d_scores[n], spread(q[:, s : s + 256], eight), 1, 0) * SCALE for n, s in enumerate(starts)
    ]
    d_q = []
    for n in range(D // 128):
        cols = slice(256 * (n % 2), 256 * (n % 2) + 256)
        d_q.append(dot(d_scores[n // 2][:, cols], k[:, 128 * n : 128 * n + 128], 0, 0))
    d_q = [gather_heads(part, four) * SCALE for part in d_q]
    return jnp.concatenate(d_q, 1), jnp.concatenate(d_k, 1), jnp.concatenate(d_v, 1)


def compress(block, masks):
    total = None
    for h, m in enumerate(masks):
        part = jnp.where(m, block[32 * h : 32 * h + 32], 0.0)
        total = part if total is None else total + part
    return total


def diagonal(block, masks):
    return jnp.concatenate([jnp.where(m, block, jnp.zeros_like(block)) for m in masks], 0)


def channel_forward(q, k, v):
    four = head_masks(128)
    starts = range(0, D, 128)
    scores = [dot(k[:, s : s + 128], q[:, s : s + 128], 0, 0) for s in starts]
    scores = jnp.concatenate([compress(block, four) for block in scores], 1)
    e = jnp.exp((scores - jnp.max(scores, 0, keepdims=True)) * SCALE)
    probs = (e * (1.0 / jnp.sum(e, 0, keepdims=True))).astype(BF)
    parts = [dot(v[:, s : s + 128], diagonal(probs[:, s : s + 128], four), 1, 0) for s in starts]
    return probs, jnp.concatenate(parts, 1)


def channel_backward(q, k, v, probs, d_att):
    four = head_masks(128)
    starts = range(0, D, 128)
    d_probs = [dot(v[:, s : s + 128], d_att[:, s : s + 128], 0, 0) for s in starts]
    d_v = [dot(d_att[:, s : s + 128], diagonal(probs[:, s : s + 128], four), 1, 1) for s in starts]
    d_probs = jnp.concatenate([compress(block, four) for block in d_probs], 1)
    p = probs.astype(F32)
    product = p * d_probs
    d_scores = (product - p * jnp.sum(product, 0, keepdims=True)).astype(BF)
    blocks = [diagonal(d_scores[:, s : s + 128], four) for s in starts]
    d_q = [dot(k[:, s : s + 128], blocks[n], 1, 0) * SCALE for n, s in enumerate(starts)]
    d_k = [dot(q[:, s : s + 128], blocks[n], 1, 1) * SCALE for n, s in enumerate(starts)]
    return jnp.concatenate(d_q, 1), jnp.concatenate(d_k, 1), jnp.concatenate(d_v, 1)


def sections_kernel(
    micros, rows, real,
    tok_ref, cot_ref, par, w1_ref, w2_ref,
    lo_ref, ig_ref, left_ref, right_ref, small_ref,
    w1, w2, big, probs, x_in, g_in, v_out, g_out, raw, normed, att_low, wide, acc, tmp, att_in, d_att, d_split,
    w_sem, raw_sem, v_send, v_recv, g_send, g_recv, f_send, f_recv, k_sem, kg_sem, kh_sem,
):
    dp, role = lax.axis_index("dp"), lax.axis_index("pipe")
    images = real // PATCHES
    share = micros // 4
    slab = raw.shape[1]
    total = tok_ref.shape[0]

    barrier = pltpu.get_barrier_semaphore()
    for n in range(1, 4):
        pl.semaphore_signal(barrier, inc=1, device_id=(dp, (role + n) % 4), device_id_type=MESH)

    load_1 = pltpu.make_async_copy(w1_ref, w1, w_sem.at[0])
    load_2 = pltpu.make_async_copy(w2_ref, w2, w_sem.at[1])
    load_1.start()

    def owner(m):
        return (m // share + 2) % 4

    def first_row(m):
        return owner(m) * (share * real) + (m % share) * real

    def slab_start(m):
        return pl.multiple_of(jnp.minimum(first_row(m) // 16 * 16, total - slab), 16)

    def load_slab(ref, m):
        return pltpu.make_async_copy(ref.at[pl.ds(slab_start(m), slab)], raw.at[m % 2], raw_sem.at[m % 2])

    def take_slab(ref, m, dst):
        load_slab(ref, m).wait()
        shift = first_row(m) - slab_start(m)
        moved = pltpu.roll(raw[m % 2].astype(F32), slab - shift, 0)[:rows]
        row = lax.broadcasted_iota(jnp.int32, (rows, 1), 0)
        dst[m] = jnp.where(row < real, moved, 0.0).astype(BF)

        @pl.when(m + 2 < micros)
        def _():
            load_slab(ref, m + 2).start()

    small_ref[...] = jnp.zeros_like(small_ref)

    def out_rows(m):
        return pl.ds(pl.multiple_of(m * rows, 16), rows)

    def keep_left(n, m, src):
        return pltpu.make_async_copy(src, left_ref.at[n, out_rows(m)], k_sem.at[n])

    def keep_wide(m, start, size):
        return pltpu.make_async_copy(
            wide.at[:, pl.ds(0, size)], right_ref.at[out_rows(m), pl.ds(start, size)], k_sem.at[2]
        )

    def again(m, copy):
        @pl.when(m > 0)
        def _():
            copy.wait()

    def keep_gout_left(m):
        return pltpu.make_async_copy(g_in.at[m], left_ref.at[1, out_rows(m)], kg_sem.at[m])

    def keep_gout_right(m):
        return pltpu.make_async_copy(g_in.at[m], right_ref.at[out_rows(m), pl.ds(3 * D, D)], kg_sem.at[m])

    def keep_hidden(m):
        return pltpu.make_async_copy(
            big.at[m, pl.ds(0, rows)], right_ref.at[out_rows(m), pl.ds(0, FF)], kh_sem.at[m]
        )

    def next_hop(m):
        return pltpu.make_async_remote_copy(
            src_ref=v_out.at[m % 2], dst_ref=x_in.at[m], send_sem=v_send.at[m], recv_sem=v_recv.at[m],
            device_id=(dp, (role + 1) % 4), device_id_type=MESH,
        )

    def back_hop(m):
        return pltpu.make_async_remote_copy(
            src_ref=g_out.at[m % 2], dst_ref=g_in.at[m], send_sem=g_send.at[m], recv_sem=g_recv.at[m],
            device_id=(dp, (role + 3) % 4), device_id_type=MESH,
        )

    def result_hop(n, src, ref, m):
        return pltpu.make_async_remote_copy(
            src_ref=src.at[m % 2], dst_ref=ref.at[m % share], send_sem=f_send.at[m],
            recv_sem=f_recv.at[n, m % share], device_id=(dp, owner(m)), device_id_type=MESH,
        )

    def result_here(src, ref, m):
        return pltpu.make_async_copy(src.at[m % 2], ref.at[m % share], f_send.at[m])

    def result_start(n, src, ref, m):
        @pl.when(owner(m) == role)
        def _():
            result_here(src, ref, m).start()

        @pl.when(owner(m) != role)
        def _():
            result_hop(n, src, ref, m).start()

    def result_wait(n, src, ref, m):
        @pl.when(owner(m) == role)
        def _():
            result_here(src, ref, m).wait()

        @pl.when(owner(m) != role)
        def _():
            result_hop(n, src, ref, m).wait_send()

    bias = par[0:1, :]
    gain, shift_row, bias_out = par[1:2, :D], par[1:2, D : 2 * D], par[1:2, 2 * D : 3 * D]
    image_row = lax.broadcasted_iota(jnp.int32, (PAD, 1), 0)

    def norm_forward(m, x):
        scaled, _ = norm_parts(x)
        again(m, keep_left(0, m, normed))
        normed[...] = (scaled * gain + shift_row).astype(BF)
        keep_left(0, m, normed).start()

    def norm_back(d_normed, m):
        scaled, inverse = norm_parts(x_in[m].astype(F32))
        small_ref[0:1, :] += jnp.sum(d_normed * scaled, 0, keepdims=True)
        small_ref[1:2, :] += jnp.sum(d_normed, 0, keepdims=True)
        d_scaled = d_normed * gain
        mean = jnp.mean(d_scaled, -1, keepdims=True)
        cross = jnp.mean(d_scaled * scaled, -1, keepdims=True)
        return (g_in[m].astype(F32) + inverse * (d_scaled - mean - scaled * cross)).astype(BF)

    def cut(src, n, c):
        part = src[PATCHES * n : PATCHES * n + PAD, c : c + D]
        return jnp.where(image_row < PATCHES, part, 0.0).astype(BF)

    def image_at(i):
        return pl.ds(pl.multiple_of(i * PAD, PAD), PAD)

    def attention_forward(m, spatial):
        x = x_in[m].astype(F32)
        norm_forward(m, x)
        for c in range(0, 3 * D, D):
            tmp[0:rows, c : c + D] = dot(normed[...], w1[:, c : c + D], 1, 0) + bias[:, c : c + D]
        for i in range(images):
            for c in range(0, 3 * D, D):
                big[m, PAD * i : PAD * (i + 1), c : c + D] = cut(tmp, i, c)

        def one_image(i, carry):
            q, k, v = (big[m, image_at(i), n * D : (n + 1) * D] for n in range(3))
            if spatial:
                probs[m * images + i], att_in[i] = window_forward(q, k, v)
            else:
                probs[m * images + i, 0:32, 0:D], att_in[i] = channel_forward(q, k, v)
            return carry

        lax.fori_loop(0, images, one_image, 0)
        for i in range(images):
            acc[PATCHES * i : PATCHES * i + PAD, :] = att_in[i]
        acc[real:rows, :] = jnp.zeros((rows - real, D), F32)
        again(m, keep_left(1, m, att_low))
        att_low[...] = acc[0:rows, :].astype(BF)
        keep_left(1, m, att_low).start()
        branch = dot(att_low[...], w1[:, 3 * D :], 1, 0) + bias[:, 3 * D :]
        v_out[m % 2] = (x + branch).astype(BF)

    def attention_backward(m, spatial):
        keep_gout_right(m).start()
        g = g_in[m]
        small_ref[6:7, :] += jnp.sum(g.astype(F32), 0, keepdims=True)
        acc[0:rows, :] = dot(g, w1[:, 3 * D :], 1, 1)
        for i in range(images):
            d_att[i] = cut(acc, i, 0)

        def one_image(i, carry):
            q, k, v = (big[m, image_at(i), n * D : (n + 1) * D] for n in range(3))
            if spatial:
                grads = window_backward(q, k, v, probs[m * images + i], d_att[i])
            else:
                grads = channel_backward(q, k, v, probs[m * images + i, 0:32, 0:D], d_att[i])
            for n in range(3):
                d_split[i, :, n * D : (n + 1) * D] = grads[n].astype(BF)
            return carry

        lax.fori_loop(0, images, one_image, 0)
        for i in range(images):
            for c in range(0, 3 * D, D):
                tmp[PATCHES * i : PATCHES * i + PAD, c : c + D] = d_split[i, :, c : c + D].astype(F32)
        tmp[real:rows, :] = jnp.zeros((rows - real, 3 * D), F32)
        again(m, keep_wide(m, 0, 3 * D))
        for n in range(3):
            part = tmp[0:rows, n * D : (n + 1) * D]
            wide[:, n * D : (n + 1) * D] = part.astype(BF)
            small_ref[3 + n : 4 + n, :] += jnp.sum(part, 0, keepdims=True)
        keep_wide(m, 0, 3 * D).start()
        g_out[m % 2] = norm_back(dot(wide[:, : 3 * D], w1[:, : 3 * D], 1, 1), m)

    def feed_forward(m):
        x = x_in[m].astype(F32)
        norm_forward(m, x)
        again(m, keep_wide(m, FF, FF))
        acc[0:rows, :] = x + bias_out
        for c in range(0, FF, D):
            hidden = dot(normed[...], w1[:, c : c + D], 1, 0) + bias[:, c : c + D]
            value, diff = gelu_pair(hidden)
            wide[:, c : c + D] = value.astype(BF)
            big[m, 0:rows, c : c + D] = diff.astype(BF)
            acc[0:rows, :] += dot(wide[:, c : c + D], w2[c : c + D, :], 1, 0)
        keep_wide(m, FF, FF).start()
        v_out[m % 2] = acc[0:rows, :].astype(BF)

    def feed_backward(m):
        keep_gout_left(m).start()
        small_ref[2:3, :] += jnp.sum(g_in[m].astype(F32), 0, keepdims=True)
        for n in range(FF // D):
            c = n * D
            d_act = dot(g_in[m], w2[c : c + D, :], 1, 1)
            d_hid = (d_act * big[m, 0:rows, c : c + D].astype(F32)).astype(BF)
            big[m, 0:rows, c : c + D] = d_hid
            small_ref[3 + n : 4 + n, :] += jnp.sum(d_hid.astype(F32), 0, keepdims=True)
            back = dot(d_hid, w1[:, c : c + D], 1, 1)
            if n == 0:
                acc[0:rows, :] = back
            else:
                acc[0:rows, :] += back
        keep_hidden(m).start()
        g_out[m % 2] = norm_back(acc[0:rows, :], m)

    def forward(m, run, first, last):
        if first:
            take_slab(tok_ref, m, x_in)
        else:
            next_hop(m).wait_recv()

        @pl.when(m >= 2)
        def _():
            finish_forward(m - 2, last)

        run(m)
        if last is True:
            result_start(0, v_out, lo_ref, m)
        elif last is False:
            next_hop(m).start()
        else:

            @pl.when(last)
            def _():
                result_start(0, v_out, lo_ref, m)

            @pl.when(jnp.logical_not(last))
            def _():
                next_hop(m).start()

    def finish_forward(m, last):
        if last is False:
            next_hop(m).wait_send()
        else:

            @pl.when(last)
            def _():
                result_wait(0, v_out, lo_ref, m)

            @pl.when(jnp.logical_not(last))
            def _():
                next_hop(m).wait_send()

    def backward(m, run, first, last):
        if last is False:
            back_hop(m).wait_recv()
        else:

            @pl.when(last)
            def _():
                take_slab(cot_ref, m, g_in)

            @pl.when(jnp.logical_not(last))
            def _():
                back_hop(m).wait_recv()

        @pl.when(m >= 2)
        def _():
            finish_backward(m - 2, first)

        run(m)
        if first:
            result_start(1, g_out, ig_ref, m)
        else:
            back_hop(m).start()

    def finish_backward(m, first):
        if first:
            result_wait(1, g_out, ig_ref, m)
        else:
            back_hop(m).wait_send()

    def pipeline(run_forward, run_backward, lag, first, last):
        def step(s, carry):
            @pl.when(s < micros)
            def _():
                forward(s, run_forward, first, last)

            @pl.when(s >= lag)
            def _():
                backward(s - lag, run_backward, first, last)

            return carry

        lax.fori_loop(0, micros + lag, step, 0)
        for m in (micros - 2, micros - 1):
            finish_forward(m, last)
            finish_backward(m, first)

    @pl.when(role == 0)
    def _():
        load_slab(tok_ref, 0).start()
        load_slab(tok_ref, 1).start()

    @pl.when(role == 3)
    def _():
        load_slab(cot_ref, 0).start()
        load_slab(cot_ref, 1).start()

    @pl.when(role % 2 == 1)
    def _():
        load_2.start()

    load_1.wait()
    pl.semaphore_wait(barrier, 3)

    @pl.when(role == 0)
    def _():
        tmp[rows:, :] = jnp.zeros((tmp.shape[0] - rows, 3 * D), F32)
        acc[rows:, :] = jnp.zeros((acc.shape[0] - rows, D), F32)
        pipeline(
            functools.partial(attention_forward, spatial=True),
            functools.partial(attention_backward, spatial=True),
            micros, True, False,
        )

    @pl.when(role == 2)
    def _():
        tmp[rows:, :] = jnp.zeros((tmp.shape[0] - rows, 3 * D), F32)
        acc[rows:, :] = jnp.zeros((acc.shape[0] - rows, D), F32)
        pipeline(
            functools.partial(attention_forward, spatial=False),
            functools.partial(attention_backward, spatial=False),
            2, False, False,
        )

    @pl.when(role % 2 == 0)
    def _():
        keep_left(1, micros - 1, att_low).wait()
        keep_wide(micros - 1, 0, 3 * D).wait()

        def kept(m, carry):
            keep_gout_right(m).wait()
            return carry

        lax.fori_loop(0, micros, kept, 0)

    @pl.when(role % 2 == 1)
    def _():
        load_2.wait()
        pipeline(feed_forward, feed_backward, jnp.where(role == 3, 0, micros), False, role == 3)
        keep_wide(micros - 1, FF, FF).wait()

        def kept(m, carry):
            keep_gout_left(m).wait()
            keep_hidden(m).wait()
            return carry

        lax.fori_loop(0, micros, kept, 0)

    keep_left(0, micros - 1, normed).wait()

    def arrived(n, carry):
        @pl.when(role != 3)
        def _():
            result_hop(0, v_out, lo_ref, n).wait_recv()

        @pl.when(role != 0)
        def _():
            result_hop(1, g_out, ig_ref, n).wait_recv()

        return carry

    lax.fori_loop(0, share, arrived, 0)


def run_sections(tokens, cotangent, par, w1, w2, micros, rows, real):
    images = real // PATCHES
    tall = max((PATCHES * (images - 1) + PAD + 7) // 8 * 8, rows)
    share = micros // 4
    slab = min(rows + 16, tokens.shape[0])
    hbm = pl.BlockSpec(memory_space=pl.ANY)
    vmem = pl.BlockSpec(memory_space=pltpu.VMEM)
    dma = pltpu.SemaphoreType.DMA
    scratch = [
        pltpu.VMEM((D, FF), BF),
        pltpu.VMEM((FF, D), BF),
        pltpu.VMEM((micros, max(images * PAD, rows), FF), BF),
        pltpu.VMEM((micros * images, PAD, 3 * 512), BF),
        pltpu.VMEM((micros, rows, D), BF),
        pltpu.VMEM((micros, rows, D), BF),
        pltpu.VMEM((2, rows, D), BF),
        pltpu.VMEM((2, rows, D), BF),
        pltpu.VMEM((2, slab, D), BF),
        pltpu.VMEM((rows, D), BF),
        pltpu.VMEM((rows, D), BF),
        pltpu.VMEM((rows, FF), BF),
        pltpu.VMEM((tall, D), F32),
        pltpu.VMEM((tall, 3 * D), F32),
        pltpu.VMEM((images, PAD, D), F32),
        pltpu.VMEM((images, PAD, D), BF),
        pltpu.VMEM((images, PAD, 3 * D), BF),
        dma((2,)), dma((2,)), dma((micros,)), dma((micros,)), dma((micros,)), dma((micros,)),
        dma((micros,)), dma((2, share)), dma((3,)), dma((micros,)), dma((micros,)),
    ]
    out_shape = (
        jax.ShapeDtypeStruct((share, rows, D), BF),
        jax.ShapeDtypeStruct((share, rows, D), BF),
        jax.ShapeDtypeStruct((2, micros * rows, D), BF),
        jax.ShapeDtypeStruct((micros * rows, 2 * FF), BF),
        jax.ShapeDtypeStruct((8, D), F32),
    )
    return pl.pallas_call(
        functools.partial(sections_kernel, micros, rows, real),
        out_shape=out_shape,
        in_specs=[hbm, hbm, vmem, hbm, hbm],
        out_specs=(hbm, hbm, hbm, hbm, vmem),
        scratch_shapes=scratch,
        compiler_params=pltpu.CompilerParams(
            collective_id=0, has_side_effects=True, vmem_limit_bytes=63 * 2**20
        ),
        cost_estimate=pl.CostEstimate(
            flops=2 * 4 * 2 * D * FF * micros * rows, bytes_accessed=60_000_000, transcendentals=0
        ),
        name="sections",
    )(tokens, cotangent, par, w1, w2)


LAG_X, LAG_Z, LAG_OUT = 0, 3, 6
RING = 4


def weights_kernel(
    inner, real,
    left_ref, right_ref, small, lo_ref, ig_ref,
    first_ref, second_ref, vec_ref, lo_out, ig_out,
    left, ring, part, from_x, from_z, vec_x, vec_z, halves, joined,
    l_sem, r_sem, x_send, x_recv, z_send, z_recv, v_send, v_recv, h_sem,
):
    dp, role = lax.axis_index("dp"), lax.axis_index("pipe")
    feed = role % 2
    outer, rest = dp // inner, dp % inner
    z, x = outer // 2, outer % 2
    lines = MEMBERS // 2
    per = FF // WIDE
    steps = per + per * feed

    def at(zz, xx):
        return ((zz * 2 + xx) * inner + rest, role)

    barrier = pltpu.get_barrier_semaphore()
    pl.semaphore_signal(barrier, inc=1, device_id=at(z, 1 - x), device_id_type=MESH)
    for i in range(1, lines):
        pl.semaphore_signal(barrier, inc=1, device_id=at((z + i) % lines, x), device_id_type=MESH)

    def load_left(n):
        return pltpu.make_async_copy(left_ref.at[n], left.at[n], l_sem.at[n])

    def load_right(k):
        cols = pl.ds(pl.multiple_of(k * WIDE, 128), WIDE)
        return pltpu.make_async_copy(right_ref.at[:, cols], ring.at[k % RING], r_sem.at[k % RING])

    load_left(0).start()
    load_right(0).start()
    for k in range(1, RING - 1):
        load_right(k).start()
    load_left(1).start()
    load_lo = pltpu.make_async_copy(lo_ref, halves.at[0], h_sem.at[0])
    load_ig = pltpu.make_async_copy(ig_ref, halves.at[1], h_sem.at[1])
    load_lo.start()
    load_ig.start()
    pl.semaphore_wait(barrier, lines)

    def to_x(k):
        return pltpu.make_async_remote_copy(
            src_ref=part.at[k, :, 1 - x], dst_ref=from_x.at[k], send_sem=x_send.at[k], recv_sem=x_recv.at[k],
            device_id=at(z, 1 - x), device_id_type=MESH,
        )

    def to_z(k, zz):
        return pltpu.make_async_remote_copy(
            src_ref=part.at[k, zz, x], dst_ref=from_z.at[k, z], send_sem=z_send.at[k, zz],
            recv_sem=z_recv.at[k, z], device_id=at(zz, x), device_id_type=MESH,
        )

    def arrived_z(k, zz):
        return pltpu.make_async_remote_copy(
            src_ref=part.at[k, zz, x], dst_ref=from_z.at[k, zz], send_sem=z_send.at[k, zz],
            recv_sem=z_recv.at[k, zz], device_id=at(zz, x), device_id_type=MESH,
        )

    vec_to_x = pltpu.make_async_remote_copy(
        src_ref=small, dst_ref=vec_x.at[0], send_sem=v_send.at[0], recv_sem=v_recv.at[0],
        device_id=at(z, 1 - x), device_id_type=MESH,
    )

    def vec_to_z(zz):
        return pltpu.make_async_remote_copy(
            src_ref=vec_x.at[1], dst_ref=vec_z.at[z], send_sem=v_send.at[1 + zz], recv_sem=v_recv.at[1 + z],
            device_id=at(zz, x), device_id_type=MESH,
        )

    def vec_arrived(zz):
        return pltpu.make_async_remote_copy(
            src_ref=vec_x.at[1], dst_ref=vec_z.at[zz], send_sem=v_send.at[1 + zz], recv_sem=v_recv.at[1 + zz],
            device_id=at(zz, x), device_id_type=MESH,
        )

    load_left(0).wait()
    edge = jnp.where(feed == 1, per, 3 * D // WIDE)

    def step(s, carry):
        @pl.when(s < steps)
        def _():
            @pl.when(s == edge)
            def _():
                load_left(1).wait()

            load_right(s).wait()

            @pl.when(s + RING - 1 < steps)
            def _():
                load_right(s + RING - 1).start()

            product = dot(left[s // edge], ring[s % RING], 0, 0)
            part[s] = product.astype(BF).reshape(lines, 2, BLOCK, WIDE)
            to_x(s).start()

        k2 = s - LAG_Z

        @pl.when((k2 >= 0) & (k2 < steps))
        def _():
            to_x(k2).wait_recv()
            part[k2, :, x] = (part[k2, :, x].astype(F32) + from_x[k2].astype(F32)).astype(BF)
            for i in range(1, lines):
                to_z(k2, (z + i) % lines).start()

        k3 = s - LAG_OUT

        @pl.when((k3 >= 0) & (k3 < steps))
        def _():
            total = part[k3, z, x].astype(F32)
            for i in range(1, lines):
                zz = (z + i) % lines
                arrived_z(k3, zz).wait_recv()
                total += from_z[k3, zz].astype(F32)
            place = pl.multiple_of((k3 % per) * WIDE, 128)

            @pl.when(k3 < per)
            def _():
                first_ref[:, pl.ds(place, WIDE)] = total

            @pl.when(k3 >= per)
            def _():
                second_ref[pl.ds(place, WIDE), :] = total.T

        @pl.when(s == 0)
        def _():
            vec_to_x.start()

            @pl.when(feed == 0)
            def _():
                second_ref[...] = jnp.zeros_like(second_ref)

        @pl.when(s == 2)
        def _():
            for n, load, dst in ((0, load_lo, lo_out), (1, load_ig, ig_out)):
                load.wait()
                for i in range(halves.shape[1]):
                    joined[real * i : real * (i + 1), :] = halves[n, i, :real].astype(F32)
                dst[...] = joined[: dst.shape[0], :].astype(BF)

        @pl.when(s == 4)
        def _():
            vec_to_x.wait_recv()
            vec_x[1] = small[...] + vec_x[0]
            for i in range(1, lines):
                vec_to_z((z + i) % lines).start()

        return carry

    lax.fori_loop(0, steps + LAG_OUT, step, 0)
    total = vec_x[1]
    for i in range(1, lines):
        zz = (z + i) % lines
        vec_arrived(zz).wait_recv()
        total += vec_z[zz]
        vec_to_z(zz).wait_send()
    vec_ref[...] = total
    vec_to_x.wait_send()

    def drain(k, carry):
        to_x(k).wait_send()
        for i in range(1, lines):
            to_z(k, (z + i) % lines).wait_send()
        return carry

    lax.fori_loop(0, steps, drain, 0)


def reduce_weights(left, right, small, lo, ig, inner, real):
    count = left.shape[1]
    lines = MEMBERS // 2
    per = FF // WIDE
    share = lo.shape[0]
    hbm = pl.BlockSpec(memory_space=pl.ANY)
    vmem = pl.BlockSpec(memory_space=pltpu.VMEM)
    dma = pltpu.SemaphoreType.DMA
    return pl.pallas_call(
        functools.partial(weights_kernel, inner, real),
        out_shape=(
            jax.ShapeDtypeStruct((BLOCK, FF), F32),
            jax.ShapeDtypeStruct((FF, BLOCK), F32),
            jax.ShapeDtypeStruct((8, D), F32),
            jax.ShapeDtypeStruct((share * real, D), BF),
            jax.ShapeDtypeStruct((share * real, D), BF),
        ),
        in_specs=[hbm, hbm, vmem, hbm, hbm],
        out_specs=(vmem, vmem, vmem, vmem, vmem),
        scratch_shapes=[
            pltpu.VMEM((2, count, D), BF),
            pltpu.VMEM((RING, count, WIDE), BF),
            pltpu.VMEM((2 * per, lines, 2, BLOCK, WIDE), BF),
            pltpu.VMEM((2 * per, lines, BLOCK, WIDE), BF),
            pltpu.VMEM((2 * per, lines, BLOCK, WIDE), BF),
            pltpu.VMEM((2, 8, D), F32),
            pltpu.VMEM((lines, 8, D), F32),
            pltpu.VMEM((2,) + lo.shape, BF),
            pltpu.VMEM(((share * real + 7) // 8 * 8, D), F32),
            dma((2,)), dma((RING,)), dma((2 * per,)), dma((2 * per,)),
            dma((2 * per, lines)), dma((2 * per, lines)), dma((1 + lines,)), dma((1 + lines,)), dma((2,)),
        ],
        compiler_params=pltpu.CompilerParams(
            collective_id=1, has_side_effects=True, vmem_limit_bytes=63 * 2**20
        ),
        cost_estimate=pl.CostEstimate(
            flops=2 * 2 * D * FF * count, bytes_accessed=40_000_000, transcendentals=0
        ),
        name="weights",
    )(left, right, small, lo, ig)


def on_device(tokens, cotangent, norm_gain, norm_shift, w_first, b_first, w_second, b_second):
    dp = lax.axis_index("dp")
    groups = lax.axis_size("dp")
    inner = groups // MEMBERS
    micros = MICROS
    real = tokens.shape[0] // micros
    rows = (real + 15) // 16 * 16
    line = jnp.concatenate([norm_gain, norm_shift, b_second, jnp.zeros((1, FF - 3 * D), F32)], 1)
    par = jnp.concatenate([b_first, line, jnp.zeros((6, FF), F32)], 0)
    lo, ig, left, right, small = run_sections(
        tokens, cotangent, par, w_first[0], w_second[0], micros, rows, real
    )
    g_first, g_second, vec, layer_out, input_grad = reduce_weights(left, right, small, lo, ig, inner, real)

    if inner > 1:
        members = [[o * inner + i for i in range(inner)] for o in range(MEMBERS)]

        def over_members(part, dim):
            return lax.psum_scatter(
                part, "dp", scatter_dimension=dim, axis_index_groups=members, tiled=True
            )

        g_first = over_members(g_first, 0)
        g_second = over_members(g_second, 1)
        vec = lax.psum(vec, "dp", axis_index_groups=members)

    def piece(vec):
        size = vec.shape[0] // groups
        return lax.dynamic_slice_in_dim(vec, dp * size, size, 0)[None]

    return (
        layer_out,
        input_grad,
        piece(vec[0]),
        piece(vec[1]),
        g_first[None],
        piece(vec[3:7].reshape(FF)),
        g_second[None],
        piece(vec[2]),
    )


def solution(mesh):
    in_specs = (
        P("dp", None), P("dp", None), P("pipe", None), P("pipe", None),
        P("pipe", None, None), P("pipe", None), P("pipe", None, None), P("pipe", None),
    )
    out_specs = (
        P(("dp", "pipe"), None), P(("dp", "pipe"), None), P("pipe", "dp"), P("pipe", "dp"),
        P("pipe", "dp", None), P("pipe", "dp"), P("pipe", None, "dp"), P("pipe", "dp"),
    )
    return jax.shard_map(
        on_device, mesh=mesh, in_specs=in_specs, out_specs=out_specs, check_vma=False
    )
```

```python
import functools

import jax
import jax.experimental.pallas as pl
import jax.experimental.pallas.tpu as pltpu
import jax.numpy as jnp
from jax import lax
from jax.sharding import PartitionSpec as P

D = 768
FF = 3072
PATCHES = 49
PAD = 64
EPS = 1e-05
SCALE = 32 ** (-0.5)
MICROS = 8
MEMBERS = 8
BLOCK = D // MEMBERS
CHUNK = 512
GROUPS = {True: 3, False: 6}
WIDE = 384
MESH = pl.DeviceIdType.MESH
BF = jnp.bfloat16
F32 = jnp.float32


def dot(a, b, ca, cb):
    return lax.dot_general(a, b, (((ca,), (cb,)), ((), ())), preferred_element_type=F32)


def gelu_pair(h):
    cdf = 0.5 + 0.5 * lax.erf(h * 0.7071067811865476)
    bell = jnp.exp(-0.5 * h * h)
    return h * cdf, cdf + h * (0.3989422804014327 * bell)


def norm_parts(x):
    center = x - jnp.mean(x, -1, keepdims=True)
    inverse = lax.rsqrt(jnp.mean(center * center, -1, keepdims=True) + EPS)
    return center * inverse, inverse


def head_masks(width):
    lane = lax.broadcasted_iota(jnp.int32, (1, width), 1) // 32
    return [lane == h for h in range(width // 32)]


def spread(block, masks):
    return jnp.concatenate([jnp.where(m, block, jnp.zeros_like(block)) for m in masks], 0)


def gather_heads(stacked, masks):
    total = None
    for h, m in enumerate(masks):
        part = jnp.where(m, stacked[PAD * h : PAD * (h + 1)], 0.0)
        total = part if total is None else total + part
    return total


def spread_turned(block):
    turned = block.T
    twice = jnp.concatenate([turned, turned], 1)
    lane = lax.broadcasted_iota(jnp.int32, (1, 2 * PAD), 1) // PAD
    none = jnp.zeros((32, 2 * PAD), block.dtype)
    rows = []
    for h in range(8):
        part = jnp.where(lane == h % 2, twice[32 * h : 32 * (h + 1)], none)
        rows.append(jnp.concatenate([part if c == h // 2 else none for c in range(4)], 1))
    return jnp.concatenate(rows, 0)


WIDE_STARTS = range(0, D, 256)
STARTS = range(0, D, 128)


def heads_apart(stacked, values):
    four = head_masks(128)
    parts = []
    for n, s in enumerate(STARTS):
        cols = slice(256 * (n % 2), 256 * (n % 2) + 256)
        parts.append(gather_heads(dot(stacked[n // 2][:, cols], values[:, s : s + 128], 0, 0), four))
    return parts


def window_forward(qs, ks, vs):
    every = range(len(qs))
    row = lax.broadcasted_iota(jnp.int32, (PAD, 1), 0)
    scores = [
        [dot(ks[i][:, s : s + 256], spread_turned(qs[i][:, s : s + 256]), 1, 0) for s in WIDE_STARTS]
        for i in every
    ]
    probs = []
    for i in every:
        blocks = []
        for block in scores[i]:
            block = jnp.where(row < PATCHES, block, -1e30)
            e = jnp.exp((block - jnp.max(block, 0, keepdims=True)) * SCALE)
            blocks.append((e * (1.0 / jnp.sum(e, 0, keepdims=True))).astype(BF))
        probs.append(blocks)
    parts = [jnp.concatenate(heads_apart(probs[i], vs[i]), 1) for i in every]
    return [jnp.concatenate(blocks, 1) for blocks in probs], parts


def window_backward(qs, ks, vs, probs, d_atts):
    eight = head_masks(256)
    every = range(len(qs))
    d_probs = [
        [dot(vs[i][:, s : s + 256], spread_turned(d_atts[i][:, s : s + 256]), 1, 0) for s in WIDE_STARTS]
        for i in every
    ]
    d_v = [
        [dot(probs[i][:, 2 * s : 2 * s + 512], spread(d_atts[i][:, s : s + 256], eight), 1, 0) for s in WIDE_STARTS]
        for i in every
    ]
    d_scores = []
    for i in every:
        blocks = []
        for n, s in enumerate(WIDE_STARTS):
            p = probs[i][:, 2 * s : 2 * s + 512].astype(F32)
            product = p * d_probs[i][n]
            blocks.append((product - p * jnp.sum(product, 0, keepdims=True)).astype(BF))
        d_scores.append(blocks)
    d_k = [
        [dot(d_scores[i][n], spread(qs[i][:, s : s + 256], eight), 1, 0) * SCALE for n, s in enumerate(WIDE_STARTS)]
        for i in every
    ]
    d_q = [[part * SCALE for part in heads_apart(d_scores[i], ks[i])] for i in every]
    return [[jnp.concatenate(parts[i], 1) for parts in (d_q, d_k, d_v)] for i in every]


def compress(block, masks):
    total = None
    for h, m in enumerate(masks):
        part = jnp.where(m, block[32 * h : 32 * h + 32], 0.0)
        total = part if total is None else total + part
    return total


def diagonal_turned(block):
    turned = jnp.concatenate([block.T] * 4, 1)
    r = lax.broadcasted_iota(jnp.int32, (128, 128), 0) // 32
    c = lax.broadcasted_iota(jnp.int32, (128, 128), 1) // 32
    return jnp.where(r == c, turned, jnp.zeros_like(turned))


def channel_forward(qs, ks, vs):
    four = head_masks(128)
    every = range(len(qs))
    scores = [[dot(ks[i][:, s : s + 128], qs[i][:, s : s + 128], 0, 0) for s in STARTS] for i in every]
    scores = [jnp.concatenate([compress(block, four) for block in scores[i]], 1) for i in every]
    es = [jnp.exp((block - jnp.max(block, 0, keepdims=True)) * SCALE) for block in scores]
    probs = [(e * (1.0 / jnp.sum(e, 0, keepdims=True))).astype(BF) for e in es]
    parts = [
        jnp.concatenate([dot(vs[i][:, s : s + 128], spread(probs[i][:, s : s + 128], four), 1, 0) for s in STARTS], 1)
        for i in every
    ]
    return probs, parts


def channel_backward(qs, ks, vs, probs, d_atts):
    four = head_masks(128)
    every = range(len(qs))
    d_probs = [[dot(vs[i][:, s : s + 128], d_atts[i][:, s : s + 128], 0, 0) for s in STARTS] for i in every]
    d_v = [
        [dot(d_atts[i][:, s : s + 128], diagonal_turned(probs[i][:, s : s + 128]), 1, 0) for s in STARTS]
        for i in every
    ]
    d_scores = []
    for i in every:
        block = jnp.concatenate([compress(block, four) for block in d_probs[i]], 1)
        p = probs[i].astype(F32)
        product = p * block
        d_scores.append((product - p * jnp.sum(product, 0, keepdims=True)).astype(BF))
    d_q = [
        [dot(ks[i][:, s : s + 128], spread(d_scores[i][:, s : s + 128], four), 1, 0) * SCALE for s in STARTS]
        for i in every
    ]
    d_k = [
        [dot(qs[i][:, s : s + 128], diagonal_turned(d_scores[i][:, s : s + 128]), 1, 0) * SCALE for s in STARTS]
        for i in every
    ]
    return [[jnp.concatenate(parts[i], 1) for parts in (d_q, d_k, d_v)] for i in every]


def sections_kernel(
    micros, rows, real,
    tok_ref, cot_ref, par, w1_ref, w2_ref,
    lo_ref, ig_ref, left_ref, right_ref, small_ref,
    w1, w2, big, probs, x_in, g_in, v_out, g_out, raw, normed, att_low, wide, acc, tmp,
    w_sem, raw_sem, v_send, v_recv, g_send, g_recv, f_send, f_recv, k_sem, kg_sem, kh_sem,
):
    dp, role = lax.axis_index("dp"), lax.axis_index("pipe")
    images = real // PATCHES
    share = micros // 4
    slab = raw.shape[1]
    total = tok_ref.shape[0]

    barrier = pltpu.get_barrier_semaphore()
    for n in range(1, 4):
        pl.semaphore_signal(barrier, inc=1, device_id=(dp, (role + n) % 4), device_id_type=MESH)

    load_1 = pltpu.make_async_copy(w1_ref, w1, w_sem.at[0])
    load_2 = pltpu.make_async_copy(w2_ref, w2, w_sem.at[1])
    load_1.start()

    def owner(m):
        return 3 - m // share

    def first_row(m):
        return owner(m) * (share * real) + (m % share) * real

    def slab_start(m):
        return pl.multiple_of(jnp.minimum(first_row(m) // 16 * 16, total - slab), 16)

    def load_slab(ref, m):
        return pltpu.make_async_copy(ref.at[pl.ds(slab_start(m), slab)], raw.at[m % 2], raw_sem.at[m % 2])

    def take_slab(ref, m, dst):
        load_slab(ref, m).wait()
        shift = first_row(m) - slab_start(m)
        moved = pltpu.roll(raw[m % 2].astype(F32), slab - shift, 0)[:rows]
        row = lax.broadcasted_iota(jnp.int32, (rows, 1), 0)
        dst[m] = jnp.where(row < real, moved, 0.0).astype(BF)

        @pl.when(m + 2 < micros)
        def _():
            load_slab(ref, m + 2).start()

    small_ref[...] = jnp.zeros_like(small_ref)

    def out_rows(m):
        return pl.ds(pl.multiple_of(m * rows, 16), rows)

    def keep_left(n, m, src):
        return pltpu.make_async_copy(src, left_ref.at[n, out_rows(m)], k_sem.at[n])

    def keep_wide(m, start, size):
        return pltpu.make_async_copy(
            wide.at[:, pl.ds(0, size)], right_ref.at[out_rows(m), pl.ds(start, size)], k_sem.at[2]
        )

    def again(m, copy):
        @pl.when(m > 0)
        def _():
            copy.wait()

    def keep_gout_left(m):
        return pltpu.make_async_copy(g_in.at[m], left_ref.at[1, out_rows(m)], kg_sem.at[m])

    def keep_gout_right(m):
        return pltpu.make_async_copy(g_in.at[m], right_ref.at[out_rows(m), pl.ds(3 * D, D)], kg_sem.at[m])

    def keep_hidden(m):
        return pltpu.make_async_copy(
            big.at[m, pl.ds(0, rows)], right_ref.at[out_rows(m), pl.ds(0, FF)], kh_sem.at[m]
        )

    def next_hop(m):
        return pltpu.make_async_remote_copy(
            src_ref=v_out.at[m % 2], dst_ref=x_in.at[m], send_sem=v_send.at[m], recv_sem=v_recv.at[m],
            device_id=(dp, (role + 1) % 4), device_id_type=MESH,
        )

    def back_hop(m):
        return pltpu.make_async_remote_copy(
            src_ref=g_out.at[m % 2], dst_ref=g_in.at[m], send_sem=g_send.at[m], recv_sem=g_recv.at[m],
            device_id=(dp, (role + 3) % 4), device_id_type=MESH,
        )

    def result_hop(n, src, ref, m):
        return pltpu.make_async_remote_copy(
            src_ref=src.at[m % 2], dst_ref=ref.at[m % share], send_sem=f_send.at[m],
            recv_sem=f_recv.at[n, m % share], device_id=(dp, owner(m)), device_id_type=MESH,
        )

    def result_here(src, ref, m):
        return pltpu.make_async_copy(src.at[m % 2], ref.at[m % share], f_send.at[m])

    def result_start(n, src, ref, m):
        @pl.when(owner(m) == role)
        def _():
            result_here(src, ref, m).start()

        @pl.when(owner(m) != role)
        def _():
            result_hop(n, src, ref, m).start()

    def result_wait(n, src, ref, m):
        @pl.when(owner(m) == role)
        def _():
            result_here(src, ref, m).wait()

        @pl.when(owner(m) != role)
        def _():
            result_hop(n, src, ref, m).wait_send()

    bias = par[0:1, :]
    gain, shift_row, bias_out = par[1:2, :D], par[1:2, D : 2 * D], par[1:2, 2 * D : 3 * D]
    image_row = lax.broadcasted_iota(jnp.int32, (PAD, 1), 0)

    def norm_forward(m, x):
        scaled, _ = norm_parts(x)
        again(m, keep_left(0, m, normed))
        normed[...] = (scaled * gain + shift_row).astype(BF)
        keep_left(0, m, normed).start()

    def norm_back(d_normed, m):
        scaled, inverse = norm_parts(x_in[m].astype(F32))
        small_ref[0:1, :] += jnp.sum(d_normed * scaled, 0, keepdims=True)
        small_ref[1:2, :] += jnp.sum(d_normed, 0, keepdims=True)
        d_scaled = d_normed * gain
        mean = jnp.mean(d_scaled, -1, keepdims=True)
        cross = jnp.mean(d_scaled * scaled, -1, keepdims=True)
        return (g_in[m].astype(F32) + inverse * (d_scaled - mean - scaled * cross)).astype(BF)

    def cut(src, n, c):
        part = src[PATCHES * n : PATCHES * n + PAD, c : c + D]
        return jnp.where(image_row < PATCHES, part, 0.0).astype(BF)

    def attention_forward(m, spatial):
        x = x_in[m].astype(F32)
        norm_forward(m, x)
        for c in range(0, 3 * D, D):
            tmp[0:rows, c : c + D] = dot(normed[...], w1[:, c : c + D], 1, 0) + bias[:, c : c + D]
        for i in range(images):
            for c in range(0, 3 * D, D):
                big[m, PAD * i : PAD * (i + 1), c : c + D] = cut(tmp, i, c)

        for start in range(0, images, GROUPS[spatial]):
            some = range(start, min(start + GROUPS[spatial], images))
            qs, ks, vs = (
                [big[m, PAD * i : PAD * (i + 1), n * D : (n + 1) * D] for i in some] for n in range(3)
            )
            if spatial:
                kept, parts = window_forward(qs, ks, vs)
                for i, p in zip(some, kept):
                    probs[m * images + i] = p
            else:
                kept, parts = channel_forward(qs, ks, vs)
                for i, p in zip(some, kept):
                    probs[m * images + i, 0:32, 0:D] = p
            for i, part in zip(some, parts):
                acc[PATCHES * i : PATCHES * i + PAD, :] = part
        acc[real:rows, :] = jnp.zeros((rows - real, D), F32)
        again(m, keep_left(1, m, att_low))
        att_low[...] = acc[0:rows, :].astype(BF)
        keep_left(1, m, att_low).start()
        branch = dot(att_low[...], w1[:, 3 * D :], 1, 0) + bias[:, 3 * D :]
        v_out[m % 2] = (x + branch).astype(BF)

    def attention_backward(m, spatial):
        keep_gout_right(m).start()
        g = g_in[m]
        small_ref[6:7, :] += jnp.sum(g.astype(F32), 0, keepdims=True)
        acc[0:rows, :] = dot(g, w1[:, 3 * D :], 1, 1)
        for start in range(0, images, GROUPS[spatial]):
            some = range(start, min(start + GROUPS[spatial], images))
            qs, ks, vs = (
                [big[m, PAD * i : PAD * (i + 1), n * D : (n + 1) * D] for i in some] for n in range(3)
            )
            d_atts = [cut(acc, i, 0) for i in some]
            if spatial:
                grads = window_backward(qs, ks, vs, [probs[m * images + i] for i in some], d_atts)
            else:
                kept = [probs[m * images + i, 0:32, 0:D] for i in some]
                grads = channel_backward(qs, ks, vs, kept, d_atts)
            for i, parts in zip(some, grads):
                for n in range(3):
                    tmp[PATCHES * i : PATCHES * i + PAD, n * D : (n + 1) * D] = parts[n]
        tmp[real:rows, :] = jnp.zeros((rows - real, 3 * D), F32)
        again(m, keep_wide(m, 0, 3 * D))
        for n in range(3):
            part = tmp[0:rows, n * D : (n + 1) * D]
            wide[:, n * D : (n + 1) * D] = part.astype(BF)
            small_ref[3 + n : 4 + n, :] += jnp.sum(part, 0, keepdims=True)
        keep_wide(m, 0, 3 * D).start()
        g_out[m % 2] = norm_back(dot(wide[:, : 3 * D], w1[:, : 3 * D], 1, 1), m)

    def feed_forward(m):
        x = x_in[m].astype(F32)
        norm_forward(m, x)
        again(m, keep_wide(m, FF, FF))
        for c in range(0, FF, CHUNK):
            hidden = dot(normed[...], w1[:, c : c + CHUNK], 1, 0) + bias[:, c : c + CHUNK]
            value, diff = gelu_pair(hidden)
            wide[:, c : c + CHUNK] = value.astype(BF)
            big[m, 0:rows, c : c + CHUNK] = diff.astype(BF)
        keep_wide(m, FF, FF).start()
        v_out[m % 2] = (x + bias_out + dot(wide[...], w2[...], 1, 0)).astype(BF)

    def feed_backward(m):
        keep_gout_left(m).start()
        small_ref[2:3, :] += jnp.sum(g_in[m].astype(F32), 0, keepdims=True)
        for n in range(FF // D):
            c = n * D
            d_act = dot(g_in[m], w2[c : c + D, :], 1, 1)
            d_hid = (d_act * big[m, 0:rows, c : c + D].astype(F32)).astype(BF)
            big[m, 0:rows, c : c + D] = d_hid
            small_ref[3 + n : 4 + n, :] += jnp.sum(d_hid.astype(F32), 0, keepdims=True)
        keep_hidden(m).start()
        g_out[m % 2] = norm_back(dot(big[m, 0:rows], w1[...], 1, 1), m)

    def forward(m, run, first, last):
        if first:
            take_slab(tok_ref, m, x_in)
        else:
            next_hop(m).wait_recv()

        @pl.when(m >= 2)
        def _():
            finish_forward(m - 2, last)

        run(m)
        if last is True:
            result_start(0, v_out, lo_ref, m)
        elif last is False:
            next_hop(m).start()
        else:

            @pl.when(last)
            def _():
                result_start(0, v_out, lo_ref, m)

            @pl.when(jnp.logical_not(last))
            def _():
                next_hop(m).start()

    def finish_forward(m, last):
        if last is False:
            next_hop(m).wait_send()
        else:

            @pl.when(last)
            def _():
                result_wait(0, v_out, lo_ref, m)

            @pl.when(jnp.logical_not(last))
            def _():
                next_hop(m).wait_send()

    def backward(m, run, first, last):
        if last is False:
            back_hop(m).wait_recv()
        else:

            @pl.when(last)
            def _():
                take_slab(cot_ref, m, g_in)

            @pl.when(jnp.logical_not(last))
            def _():
                back_hop(m).wait_recv()

        @pl.when(m >= 2)
        def _():
            finish_backward(m - 2, first)

        run(m)
        if first:
            result_start(1, g_out, ig_ref, m)
        else:
            back_hop(m).start()

    def finish_backward(m, first):
        if first:
            result_wait(1, g_out, ig_ref, m)
        else:
            back_hop(m).wait_send()

    def pipeline(run_forward, run_backward, lag, first, last):
        def step(s, carry):
            @pl.when(s < micros)
            def _():
                forward(s, run_forward, first, last)

            @pl.when(s >= lag)
            def _():
                backward(s - lag, run_backward, first, last)

            return carry

        lax.fori_loop(0, micros + lag, step, 0)
        for m in (micros - 2, micros - 1):
            finish_forward(m, last)
            finish_backward(m, first)

    @pl.when(role == 0)
    def _():
        load_slab(tok_ref, 0).start()
        load_slab(tok_ref, 1).start()

    @pl.when(role == 3)
    def _():
        load_slab(cot_ref, 0).start()
        load_slab(cot_ref, 1).start()

    @pl.when(role % 2 == 1)
    def _():
        load_2.start()

    load_1.wait()
    pl.semaphore_wait(barrier, 3)

    @pl.when(role == 0)
    def _():
        tmp[rows:, :] = jnp.zeros((tmp.shape[0] - rows, 3 * D), F32)
        acc[rows:, :] = jnp.zeros((acc.shape[0] - rows, D), F32)
        pipeline(
            functools.partial(attention_forward, spatial=True),
            functools.partial(attention_backward, spatial=True),
            micros, True, False,
        )

    @pl.when(role == 2)
    def _():
        tmp[rows:, :] = jnp.zeros((tmp.shape[0] - rows, 3 * D), F32)
        acc[rows:, :] = jnp.zeros((acc.shape[0] - rows, D), F32)
        pipeline(
            functools.partial(attention_forward, spatial=False),
            functools.partial(attention_backward, spatial=False),
            2, False, False,
        )

    @pl.when(role % 2 == 0)
    def _():
        keep_left(1, micros - 1, att_low).wait()
        keep_wide(micros - 1, 0, 3 * D).wait()

        def kept(m, carry):
            keep_gout_right(m).wait()
            return carry

        lax.fori_loop(0, micros, kept, 0)

    @pl.when(role % 2 == 1)
    def _():
        load_2.wait()
        pipeline(feed_forward, feed_backward, jnp.where(role == 3, 0, micros), False, role == 3)
        keep_wide(micros - 1, FF, FF).wait()

        def kept(m, carry):
            keep_gout_left(m).wait()
            keep_hidden(m).wait()
            return carry

        lax.fori_loop(0, micros, kept, 0)

    keep_left(0, micros - 1, normed).wait()

    def arrived(n, carry):
        @pl.when(role != 3)
        def _():
            result_hop(0, v_out, lo_ref, n).wait_recv()

        @pl.when(role != 0)
        def _():
            result_hop(1, g_out, ig_ref, n).wait_recv()

        return carry

    lax.fori_loop(0, share, arrived, 0)


def run_sections(tokens, cotangent, par, w1, w2, micros, rows, real):
    images = real // PATCHES
    tall = max((PATCHES * (images - 1) + PAD + 7) // 8 * 8, rows)
    share = micros // 4
    slab = min(rows + 16, tokens.shape[0])
    hbm = pl.BlockSpec(memory_space=pl.ANY)
    vmem = pl.BlockSpec(memory_space=pltpu.VMEM)
    dma = pltpu.SemaphoreType.DMA
    scratch = [
        pltpu.VMEM((D, FF), BF),
        pltpu.VMEM((FF, D), BF),
        pltpu.VMEM((micros, max(images * PAD, rows), FF), BF),
        pltpu.VMEM((micros * images, PAD, 3 * 512), BF),
        pltpu.VMEM((micros, rows, D), BF),
        pltpu.VMEM((micros, rows, D), BF),
        pltpu.VMEM((2, rows, D), BF),
        pltpu.VMEM((2, rows, D), BF),
        pltpu.VMEM((2, slab, D), BF),
        pltpu.VMEM((rows, D), BF),
        pltpu.VMEM((rows, D), BF),
        pltpu.VMEM((rows, FF), BF),
        pltpu.VMEM((tall, D), F32),
        pltpu.VMEM((tall, 3 * D), F32),
        dma((2,)), dma((2,)), dma((micros,)), dma((micros,)), dma((micros,)), dma((micros,)),
        dma((micros,)), dma((2, share)), dma((3,)), dma((micros,)), dma((micros,)),
    ]
    out_shape = (
        jax.ShapeDtypeStruct((share, rows, D), BF),
        jax.ShapeDtypeStruct((share, rows, D), BF),
        jax.ShapeDtypeStruct((2, micros * rows, D), BF),
        jax.ShapeDtypeStruct((micros * rows, 2 * FF), BF),
        jax.ShapeDtypeStruct((8, D), F32),
    )
    return pl.pallas_call(
        functools.partial(sections_kernel, micros, rows, real),
        out_shape=out_shape,
        in_specs=[hbm, hbm, vmem, hbm, hbm],
        out_specs=(hbm, hbm, hbm, hbm, vmem),
        scratch_shapes=scratch,
        compiler_params=pltpu.CompilerParams(
            collective_id=0, has_side_effects=True, vmem_limit_bytes=63 * 2**20
        ),
        cost_estimate=pl.CostEstimate(
            flops=2 * 4 * 2 * D * FF * micros * rows, bytes_accessed=60_000_000, transcendentals=0
        ),
        name="sections",
    )(tokens, cotangent, par, w1, w2)


LAG_X, LAG_Z, LAG_OUT = 0, 3, 6
RING = 4


def weights_kernel(
    inner, real,
    left_ref, right_ref, small, lo_ref, ig_ref,
    first_ref, second_ref, vec_ref, lo_out, ig_out,
    left, ring, part, from_x, from_z, vec_x, vec_z, halves, joined,
    l_sem, r_sem, x_send, x_recv, z_send, z_recv, v_send, v_recv, h_sem,
):
    dp, role = lax.axis_index("dp"), lax.axis_index("pipe")
    feed = role % 2
    outer, rest = dp // inner, dp % inner
    z, x = outer // 2, outer % 2
    lines = MEMBERS // 2
    per = FF // WIDE
    steps = per + per * feed

    def at(zz, xx):
        return ((zz * 2 + xx) * inner + rest, role)

    barrier = pltpu.get_barrier_semaphore()
    pl.semaphore_signal(barrier, inc=1, device_id=at(z, 1 - x), device_id_type=MESH)
    for i in range(1, lines):
        pl.semaphore_signal(barrier, inc=1, device_id=at((z + i) % lines, x), device_id_type=MESH)

    def load_left(n):
        return pltpu.make_async_copy(left_ref.at[n], left.at[n], l_sem.at[n])

    def load_right(k):
        cols = pl.ds(pl.multiple_of(k * WIDE, 128), WIDE)
        return pltpu.make_async_copy(right_ref.at[:, cols], ring.at[k % RING], r_sem.at[k % RING])

    load_left(0).start()
    load_right(0).start()
    for k in range(1, RING - 1):
        load_right(k).start()
    load_left(1).start()
    load_lo = pltpu.make_async_copy(lo_ref, halves.at[0], h_sem.at[0])
    load_ig = pltpu.make_async_copy(ig_ref, halves.at[1], h_sem.at[1])
    load_lo.start()
    load_ig.start()
    pl.semaphore_wait(barrier, lines)

    def to_x(k):
        return pltpu.make_async_remote_copy(
            src_ref=part.at[k, :, 1 - x], dst_ref=from_x.at[k], send_sem=x_send.at[k], recv_sem=x_recv.at[k],
            device_id=at(z, 1 - x), device_id_type=MESH,
        )

    def to_z(k, zz):
        return pltpu.make_async_remote_copy(
            src_ref=part.at[k, zz, x], dst_ref=from_z.at[k, z], send_sem=z_send.at[k, zz],
            recv_sem=z_recv.at[k, z], device_id=at(zz, x), device_id_type=MESH,
        )

    def arrived_z(k, zz):
        return pltpu.make_async_remote_copy(
            src_ref=part.at[k, zz, x], dst_ref=from_z.at[k, zz], send_sem=z_send.at[k, zz],
            recv_sem=z_recv.at[k, zz], device_id=at(zz, x), device_id_type=MESH,
        )

    vec_to_x = pltpu.make_async_remote_copy(
        src_ref=small, dst_ref=vec_x.at[0], send_sem=v_send.at[0], recv_sem=v_recv.at[0],
        device_id=at(z, 1 - x), device_id_type=MESH,
    )

    def vec_to_z(zz):
        return pltpu.make_async_remote_copy(
            src_ref=vec_x.at[1], dst_ref=vec_z.at[z], send_sem=v_send.at[1 + zz], recv_sem=v_recv.at[1 + z],
            device_id=at(zz, x), device_id_type=MESH,
        )

    def vec_arrived(zz):
        return pltpu.make_async_remote_copy(
            src_ref=vec_x.at[1], dst_ref=vec_z.at[zz], send_sem=v_send.at[1 + zz], recv_sem=v_recv.at[1 + zz],
            device_id=at(zz, x), device_id_type=MESH,
        )

    load_left(0).wait()
    edge = jnp.where(feed == 1, per, 3 * D // WIDE)

    def step(s, carry):
        @pl.when(s < steps)
        def _():
            @pl.when(s == edge)
            def _():
                load_left(1).wait()

            load_right(s).wait()

            @pl.when(s + RING - 1 < steps)
            def _():
                load_right(s + RING - 1).start()

            product = dot(left[s // edge], ring[s % RING], 0, 0)
            part[s] = product.astype(BF).reshape(lines, 2, BLOCK, WIDE)
            to_x(s).start()

        k2 = s - LAG_Z

        @pl.when((k2 >= 0) & (k2 < steps))
        def _():
            to_x(k2).wait_recv()
            part[k2, :, x] = (part[k2, :, x].astype(F32) + from_x[k2].astype(F32)).astype(BF)
            for i in range(1, lines):
                to_z(k2, (z + i) % lines).start()

        k3 = s - LAG_OUT

        @pl.when((k3 >= 0) & (k3 < steps))
        def _():
            total = part[k3, z, x].astype(F32)
            for i in range(1, lines):
                zz = (z + i) % lines
                arrived_z(k3, zz).wait_recv()
                total += from_z[k3, zz].astype(F32)
            place = pl.multiple_of((k3 % per) * WIDE, 128)

            @pl.when(k3 < per)
            def _():
                first_ref[:, pl.ds(place, WIDE)] = total

            @pl.when(k3 >= per)
            def _():
                second_ref[pl.ds(place, WIDE), :] = total.T

        @pl.when(s == 0)
        def _():
            vec_to_x.start()

            @pl.when(feed == 0)
            def _():
                second_ref[...] = jnp.zeros_like(second_ref)

        @pl.when(s == 2)
        def _():
            for n, load, dst in ((0, load_lo, lo_out), (1, load_ig, ig_out)):
                load.wait()
                for i in range(halves.shape[1]):
                    joined[real * i : real * (i + 1), :] = halves[n, i, :real].astype(F32)
                dst[...] = joined[: dst.shape[0], :].astype(BF)

        @pl.when(s == 4)
        def _():
            vec_to_x.wait_recv()
            vec_x[1] = small[...] + vec_x[0]
            for i in range(1, lines):
                vec_to_z((z + i) % lines).start()

        return carry

    lax.fori_loop(0, steps + LAG_OUT, step, 0)
    total = vec_x[1]
    for i in range(1, lines):
        zz = (z + i) % lines
        vec_arrived(zz).wait_recv()
        total += vec_z[zz]
        vec_to_z(zz).wait_send()
    vec_ref[...] = total
    vec_to_x.wait_send()

    def drain(k, carry):
        to_x(k).wait_send()
        for i in range(1, lines):
            to_z(k, (z + i) % lines).wait_send()
        return carry

    lax.fori_loop(0, steps, drain, 0)


def reduce_weights(left, right, small, lo, ig, inner, real):
    count = left.shape[1]
    lines = MEMBERS // 2
    per = FF // WIDE
    share = lo.shape[0]
    hbm = pl.BlockSpec(memory_space=pl.ANY)
    vmem = pl.BlockSpec(memory_space=pltpu.VMEM)
    dma = pltpu.SemaphoreType.DMA
    return pl.pallas_call(
        functools.partial(weights_kernel, inner, real),
        out_shape=(
            jax.ShapeDtypeStruct((BLOCK, FF), F32),
            jax.ShapeDtypeStruct((FF, BLOCK), F32),
            jax.ShapeDtypeStruct((8, D), F32),
            jax.ShapeDtypeStruct((share * real, D), BF),
            jax.ShapeDtypeStruct((share * real, D), BF),
        ),
        in_specs=[hbm, hbm, vmem, hbm, hbm],
        out_specs=(vmem, vmem, vmem, vmem, vmem),
        scratch_shapes=[
            pltpu.VMEM((2, count, D), BF),
            pltpu.VMEM((RING, count, WIDE), BF),
            pltpu.VMEM((2 * per, lines, 2, BLOCK, WIDE), BF),
            pltpu.VMEM((2 * per, lines, BLOCK, WIDE), BF),
            pltpu.VMEM((2 * per, lines, BLOCK, WIDE), BF),
            pltpu.VMEM((2, 8, D), F32),
            pltpu.VMEM((lines, 8, D), F32),
            pltpu.VMEM((2,) + lo.shape, BF),
            pltpu.VMEM(((share * real + 7) // 8 * 8, D), F32),
            dma((2,)), dma((RING,)), dma((2 * per,)), dma((2 * per,)),
            dma((2 * per, lines)), dma((2 * per, lines)), dma((1 + lines,)), dma((1 + lines,)), dma((2,)),
        ],
        compiler_params=pltpu.CompilerParams(
            collective_id=1, has_side_effects=True, vmem_limit_bytes=63 * 2**20
        ),
        cost_estimate=pl.CostEstimate(
            flops=2 * 2 * D * FF * count, bytes_accessed=40_000_000, transcendentals=0
        ),
        name="weights",
    )(left, right, small, lo, ig)


def on_device(tokens, cotangent, norm_gain, norm_shift, w_first, b_first, w_second, b_second):
    dp = lax.axis_index("dp")
    groups = lax.axis_size("dp")
    inner = groups // MEMBERS
    micros = MICROS
    real = tokens.shape[0] // micros
    rows = (real + 15) // 16 * 16
    line = jnp.concatenate([norm_gain, norm_shift, b_second, jnp.zeros((1, FF - 3 * D), F32)], 1)
    par = jnp.concatenate([b_first, line, jnp.zeros((6, FF), F32)], 0)
    lo, ig, left, right, small = run_sections(
        tokens, cotangent, par, w_first[0], w_second[0], micros, rows, real
    )
    g_first, g_second, vec, layer_out, input_grad = reduce_weights(left, right, small, lo, ig, inner, real)

    if inner > 1:
        members = [[o * inner + i for i in range(inner)] for o in range(MEMBERS)]

        def over_members(part, dim):
            return lax.psum_scatter(
                part, "dp", scatter_dimension=dim, axis_index_groups=members, tiled=True
            )

        g_first = over_members(g_first, 0)
        g_second = over_members(g_second, 1)
        vec = lax.psum(vec, "dp", axis_index_groups=members)

    def piece(vec):
        size = vec.shape[0] // groups
        return lax.dynamic_slice_in_dim(vec, dp * size, size, 0)[None]

    return (
        layer_out,
        input_grad,
        piece(vec[0]),
        piece(vec[1]),
        g_first[None],
        piece(vec[3:7].reshape(FF)),
        g_second[None],
        piece(vec[2]),
    )


def solution(mesh):
    in_specs = (
        P("dp", None), P("dp", None), P("pipe", None), P("pipe", None),
        P("pipe", None, None), P("pipe", None), P("pipe", None, None), P("pipe", None),
    )
    out_specs = (
        P(("dp", "pipe"), None), P(("dp", "pipe"), None), P("pipe", "dp"), P("pipe", "dp"),
        P("pipe", "dp", None), P("pipe", "dp"), P("pipe", None, "dp"), P("pipe", "dp"),
    )
    return jax.shard_map(
        on_device, mesh=mesh, in_specs=in_specs, out_specs=out_specs, check_vma=False
    )
```

```python
import functools

import jax
import jax.experimental.pallas as pl
import jax.experimental.pallas.tpu as pltpu
import jax.numpy as jnp
from jax import lax
from jax.sharding import PartitionSpec as P

D = 768
FF = 3072
PATCHES = 49
PAD = 64
EPS = 1e-05
SCALE = 32 ** (-0.5)
MICROS = 8
MEMBERS = 8
BLOCK = D // MEMBERS
CHUNK = 512
GROUPS = {True: 3, False: 6}
WIDE = 256
MESH = pl.DeviceIdType.MESH
BF = jnp.bfloat16
F32 = jnp.float32


def dot(a, b, ca, cb):
    return lax.dot_general(a, b, (((ca,), (cb,)), ((), ())), preferred_element_type=F32)


def gelu_pair(h):
    cdf = 0.5 + 0.5 * lax.erf(h * 0.7071067811865476)
    bell = jnp.exp(-0.5 * h * h)
    return h * cdf, cdf + h * (0.3989422804014327 * bell)


def norm_parts(x):
    center = x - jnp.mean(x, -1, keepdims=True)
    inverse = lax.rsqrt(jnp.mean(center * center, -1, keepdims=True) + EPS)
    return center * inverse, inverse


def head_masks(width):
    lane = lax.broadcasted_iota(jnp.int32, (1, width), 1) // 32
    return [lane == h for h in range(width // 32)]


def spread(block, masks):
    return jnp.concatenate([jnp.where(m, block, jnp.zeros_like(block)) for m in masks], 0)


def gather_heads(stacked, masks):
    total = None
    for h, m in enumerate(masks):
        part = jnp.where(m, stacked[PAD * h : PAD * (h + 1)], 0.0)
        total = part if total is None else total + part
    return total


def spread_turned(block):
    turned = block.T
    twice = jnp.concatenate([turned, turned], 1)
    lane = lax.broadcasted_iota(jnp.int32, (1, 2 * PAD), 1) // PAD
    none = jnp.zeros((32, 2 * PAD), block.dtype)
    rows = []
    for h in range(8):
        part = jnp.where(lane == h % 2, twice[32 * h : 32 * (h + 1)], none)
        rows.append(jnp.concatenate([part if c == h // 2 else none for c in range(4)], 1))
    return jnp.concatenate(rows, 0)


WIDE_STARTS = range(0, D, 256)
STARTS = range(0, D, 128)


def heads_apart(stacked, values):
    four = head_masks(128)
    parts = []
    for n, s in enumerate(STARTS):
        cols = slice(256 * (n % 2), 256 * (n % 2) + 256)
        parts.append(gather_heads(dot(stacked[n // 2][:, cols], values[:, s : s + 128], 0, 0), four))
    return parts


def window_forward(qs, ks, vs):
    every = range(len(qs))
    row = lax.broadcasted_iota(jnp.int32, (PAD, 1), 0)
    scores = [
        [dot(ks[i][:, s : s + 256], spread_turned(qs[i][:, s : s + 256]), 1, 0) for s in WIDE_STARTS]
        for i in every
    ]
    probs = []
    for i in every:
        blocks = []
        for block in scores[i]:
            block = jnp.where(row < PATCHES, block, -1e30)
            e = jnp.exp((block - jnp.max(block, 0, keepdims=True)) * SCALE)
            blocks.append((e * (1.0 / jnp.sum(e, 0, keepdims=True))).astype(BF))
        probs.append(blocks)
    parts = [jnp.concatenate(heads_apart(probs[i], vs[i]), 1) for i in every]
    return [jnp.concatenate(blocks, 1) for blocks in probs], parts


def window_backward(qs, ks, vs, probs, d_atts):
    eight = head_masks(256)
    every = range(len(qs))
    d_probs = [
        [dot(vs[i][:, s : s + 256], spread_turned(d_atts[i][:, s : s + 256]), 1, 0) for s in WIDE_STARTS]
        for i in every
    ]
    d_v = [
        [dot(probs[i][:, 2 * s : 2 * s + 512], spread(d_atts[i][:, s : s + 256], eight), 1, 0) for s in WIDE_STARTS]
        for i in every
    ]
    d_scores = []
    for i in every:
        blocks = []
        for n, s in enumerate(WIDE_STARTS):
            p = probs[i][:, 2 * s : 2 * s + 512].astype(F32)
            product = p * d_probs[i][n]
            blocks.append((product - p * jnp.sum(product, 0, keepdims=True)).astype(BF))
        d_scores.append(blocks)
    d_k = [
        [dot(d_scores[i][n], spread(qs[i][:, s : s + 256], eight), 1, 0) * SCALE for n, s in enumerate(WIDE_STARTS)]
        for i in every
    ]
    d_q = [[part * SCALE for part in heads_apart(d_scores[i], ks[i])] for i in every]
    return [[jnp.concatenate(parts[i], 1) for parts in (d_q, d_k, d_v)] for i in every]


def compress(block, masks):
    total = None
    for h, m in enumerate(masks):
        part = jnp.where(m, block[32 * h : 32 * h + 32], 0.0)
        total = part if total is None else total + part
    return total


def diagonal_turned(block):
    turned = jnp.concatenate([block.T] * 4, 1)
    r = lax.broadcasted_iota(jnp.int32, (128, 128), 0) // 32
    c = lax.broadcasted_iota(jnp.int32, (128, 128), 1) // 32
    return jnp.where(r == c, turned, jnp.zeros_like(turned))


def channel_forward(qs, ks, vs):
    four = head_masks(128)
    every = range(len(qs))
    scores = [[dot(ks[i][:, s : s + 128], qs[i][:, s : s + 128], 0, 0) for s in STARTS] for i in every]
    scores = [jnp.concatenate([compress(block, four) for block in scores[i]], 1) for i in every]
    es = [jnp.exp((block - jnp.max(block, 0, keepdims=True)) * SCALE) for block in scores]
    probs = [(e * (1.0 / jnp.sum(e, 0, keepdims=True))).astype(BF) for e in es]
    parts = [
        jnp.concatenate([dot(vs[i][:, s : s + 128], spread(probs[i][:, s : s + 128], four), 1, 0) for s in STARTS], 1)
        for i in every
    ]
    return probs, parts


def channel_backward(qs, ks, vs, probs, d_atts):
    four = head_masks(128)
    every = range(len(qs))
    d_probs = [[dot(vs[i][:, s : s + 128], d_atts[i][:, s : s + 128], 0, 0) for s in STARTS] for i in every]
    d_v = [
        [dot(d_atts[i][:, s : s + 128], diagonal_turned(probs[i][:, s : s + 128]), 1, 0) for s in STARTS]
        for i in every
    ]
    d_scores = []
    for i in every:
        block = jnp.concatenate([compress(block, four) for block in d_probs[i]], 1)
        p = probs[i].astype(F32)
        product = p * block
        d_scores.append((product - p * jnp.sum(product, 0, keepdims=True)).astype(BF))
    d_q = [
        [dot(ks[i][:, s : s + 128], spread(d_scores[i][:, s : s + 128], four), 1, 0) * SCALE for s in STARTS]
        for i in every
    ]
    d_k = [
        [dot(qs[i][:, s : s + 128], diagonal_turned(d_scores[i][:, s : s + 128]), 1, 0) * SCALE for s in STARTS]
        for i in every
    ]
    return [[jnp.concatenate(parts[i], 1) for parts in (d_q, d_k, d_v)] for i in every]


def sections_kernel(
    micros, rows, real,
    tok_ref, cot_ref, gain_ref, shift_ref, bias_ref, bias_out_ref, w1_ref, w2_ref,
    lo_ref, ig_ref, left_ref, right_ref, small_ref,
    w1, w2, big, probs, x_in, g_in, v_out, g_out, raw, normed, att_low, wide, acc, tmp,
    w_sem, raw_sem, v_send, v_recv, g_send, g_recv, f_send, f_recv, k_sem, kg_sem, kh_sem,
):
    dp, role = lax.axis_index("dp"), lax.axis_index("pipe")
    images = real // PATCHES
    share = micros // 4
    slab = raw.shape[1]
    total = tok_ref.shape[0]

    barrier = pltpu.get_barrier_semaphore()
    for n in range(1, 4):
        pl.semaphore_signal(barrier, inc=1, device_id=(dp, (role + n) % 4), device_id_type=MESH)

    load_1 = pltpu.make_async_copy(w1_ref, w1, w_sem.at[0])
    load_2 = pltpu.make_async_copy(w2_ref, w2, w_sem.at[1])
    load_1.start()

    def owner(m):
        return m // share

    def first_row(m):
        return m * real

    def slab_start(m):
        return pl.multiple_of(jnp.minimum(first_row(m) // 16 * 16, total - slab), 16)

    def load_slab(ref, m):
        return pltpu.make_async_copy(ref.at[pl.ds(slab_start(m), slab)], raw.at[m % 2], raw_sem.at[m % 2])

    def take_slab(ref, m, dst):
        load_slab(ref, m).wait()
        shift = first_row(m) - slab_start(m)
        moved = pltpu.roll(raw[m % 2].astype(F32), slab - shift, 0)[:rows]
        row = lax.broadcasted_iota(jnp.int32, (rows, 1), 0)
        dst[m] = jnp.where(row < real, moved, 0.0).astype(BF)

        @pl.when(m + 2 < micros)
        def _():
            load_slab(ref, m + 2).start()

    small_ref[...] = jnp.zeros_like(small_ref)

    def out_rows(m):
        return pl.ds(pl.multiple_of(m * rows, 16), rows)

    def keep_left(n, m, src):
        return pltpu.make_async_copy(src, left_ref.at[n, out_rows(m)], k_sem.at[n])

    def keep_wide(m, start, size):
        return pltpu.make_async_copy(
            wide.at[:, pl.ds(0, size)], right_ref.at[out_rows(m), pl.ds(start, size)], k_sem.at[2]
        )

    def again(m, copy):
        @pl.when(m > 0)
        def _():
            copy.wait()

    def keep_gout_left(m):
        return pltpu.make_async_copy(g_in.at[m], left_ref.at[1, out_rows(m)], kg_sem.at[m])

    def keep_gout_right(m):
        return pltpu.make_async_copy(g_in.at[m], right_ref.at[out_rows(m), pl.ds(3 * D, D)], kg_sem.at[m])

    def keep_hidden(m):
        return pltpu.make_async_copy(
            big.at[m, pl.ds(0, rows)], right_ref.at[out_rows(m), pl.ds(0, FF)], kh_sem.at[m]
        )

    def next_hop(m):
        return pltpu.make_async_remote_copy(
            src_ref=v_out.at[m % 2], dst_ref=x_in.at[m], send_sem=v_send.at[m], recv_sem=v_recv.at[m],
            device_id=(dp, (role + 1) % 4), device_id_type=MESH,
        )

    def back_hop(m):
        return pltpu.make_async_remote_copy(
            src_ref=g_out.at[m % 2], dst_ref=g_in.at[m], send_sem=g_send.at[m], recv_sem=g_recv.at[m],
            device_id=(dp, (role + 3) % 4), device_id_type=MESH,
        )

    def result_hop(m):
        return pltpu.make_async_remote_copy(
            src_ref=v_out.at[m % 2], dst_ref=lo_ref.at[m % share], send_sem=f_send.at[m],
            recv_sem=f_recv.at[m % share], device_id=(dp, owner(m)), device_id_type=MESH,
        )

    def result_here(m):
        return pltpu.make_async_copy(v_out.at[m % 2], lo_ref.at[m % share], f_send.at[m])

    def result_start(m):
        @pl.when(owner(m) == role)
        def _():
            result_here(m).start()

        @pl.when(owner(m) != role)
        def _():
            result_hop(m).start()

    def result_wait(m):
        @pl.when(owner(m) == role)
        def _():
            result_here(m).wait()

        @pl.when(owner(m) != role)
        def _():
            result_hop(m).wait_send()

    def grad_here(m):
        return pltpu.make_async_copy(g_out.at[m % 2], ig_ref.at[m], g_send.at[m])

    bias, bias_out = bias_ref[...], bias_out_ref[...]
    gain, shift_row = gain_ref[...], shift_ref[...]
    image_row = lax.broadcasted_iota(jnp.int32, (PAD, 1), 0)

    def norm_forward(m, x):
        scaled, _ = norm_parts(x)
        again(m, keep_left(0, m, normed))
        normed[...] = (scaled * gain + shift_row).astype(BF)
        keep_left(0, m, normed).start()

    def norm_back(d_normed, m):
        scaled, inverse = norm_parts(x_in[m].astype(F32))
        small_ref[0:1, :] += jnp.sum(d_normed * scaled, 0, keepdims=True)
        small_ref[1:2, :] += jnp.sum(d_normed, 0, keepdims=True)
        d_scaled = d_normed * gain
        mean = jnp.mean(d_scaled, -1, keepdims=True)
        cross = jnp.mean(d_scaled * scaled, -1, keepdims=True)
        return (g_in[m].astype(F32) + inverse * (d_scaled - mean - scaled * cross)).astype(BF)

    def cut(src, n, c):
        part = src[PATCHES * n : PATCHES * n + PAD, c : c + D]
        return jnp.where(image_row < PATCHES, part, 0.0).astype(BF)

    def attention_forward(m, spatial):
        x = x_in[m].astype(F32)
        norm_forward(m, x)
        for c in range(0, 3 * D, D):
            tmp[0:rows, c : c + D] = dot(normed[...], w1[:, c : c + D], 1, 0) + bias[:, c : c + D]
        for i in range(images):
            for c in range(0, 3 * D, D):
                big[m, PAD * i : PAD * (i + 1), c : c + D] = cut(tmp, i, c)

        for start in range(0, images, GROUPS[spatial]):
            some = range(start, min(start + GROUPS[spatial], images))
            qs, ks, vs = (
                [big[m, PAD * i : PAD * (i + 1), n * D : (n + 1) * D] for i in some] for n in range(3)
            )
            if spatial:
                kept, parts = window_forward(qs, ks, vs)
                for i, p in zip(some, kept):
                    probs[m * images + i] = p
            else:
                kept, parts = channel_forward(qs, ks, vs)
                for i, p in zip(some, kept):
                    probs[m * images + i, 0:32, 0:D] = p
            for i, part in zip(some, parts):
                acc[PATCHES * i : PATCHES * i + PAD, :] = part
        acc[real:rows, :] = jnp.zeros((rows - real, D), F32)
        again(m, keep_left(1, m, att_low))
        att_low[...] = acc[0:rows, :].astype(BF)
        keep_left(1, m, att_low).start()
        branch = dot(att_low[...], w1[:, 3 * D :], 1, 0) + bias[:, 3 * D :]
        v_out[m % 2] = (x + branch).astype(BF)

    def attention_backward(m, spatial):
        keep_gout_right(m).start()
        g = g_in[m]
        small_ref[6:7, :] += jnp.sum(g.astype(F32), 0, keepdims=True)
        acc[0:rows, :] = dot(g, w1[:, 3 * D :], 1, 1)
        for start in range(0, images, GROUPS[spatial]):
            some = range(start, min(start + GROUPS[spatial], images))
            qs, ks, vs = (
                [big[m, PAD * i : PAD * (i + 1), n * D : (n + 1) * D] for i in some] for n in range(3)
            )
            d_atts = [cut(acc, i, 0) for i in some]
            if spatial:
                grads = window_backward(qs, ks, vs, [probs[m * images + i] for i in some], d_atts)
            else:
                kept = [probs[m * images + i, 0:32, 0:D] for i in some]
                grads = channel_backward(qs, ks, vs, kept, d_atts)
            for i, parts in zip(some, grads):
                for n in range(3):
                    tmp[PATCHES * i : PATCHES * i + PAD, n * D : (n + 1) * D] = parts[n]
        tmp[real:rows, :] = jnp.zeros((rows - real, 3 * D), F32)
        again(m, keep_wide(m, 0, 3 * D))
        for n in range(3):
            part = tmp[0:rows, n * D : (n + 1) * D]
            wide[:, n * D : (n + 1) * D] = part.astype(BF)
            small_ref[3 + n : 4 + n, :] += jnp.sum(part, 0, keepdims=True)
        keep_wide(m, 0, 3 * D).start()
        g_out[m % 2] = norm_back(dot(wide[:, : 3 * D], w1[:, : 3 * D], 1, 1), m)

    def feed_forward(m):
        x = x_in[m].astype(F32)
        norm_forward(m, x)
        again(m, keep_wide(m, FF, FF))
        for c in range(0, FF, CHUNK):
            hidden = dot(normed[...], w1[:, c : c + CHUNK], 1, 0) + bias[:, c : c + CHUNK]
            value, diff = gelu_pair(hidden)
            wide[:, c : c + CHUNK] = value.astype(BF)
            big[m, 0:rows, c : c + CHUNK] = diff.astype(BF)
        keep_wide(m, FF, FF).start()
        v_out[m % 2] = (x + bias_out + dot(wide[...], w2[...], 1, 0)).astype(BF)

    def feed_backward(m):
        keep_gout_left(m).start()
        small_ref[2:3, :] += jnp.sum(g_in[m].astype(F32), 0, keepdims=True)
        for n in range(FF // D):
            c = n * D
            d_act = dot(g_in[m], w2[c : c + D, :], 1, 1)
            d_hid = (d_act * big[m, 0:rows, c : c + D].astype(F32)).astype(BF)
            big[m, 0:rows, c : c + D] = d_hid
            small_ref[3 + n : 4 + n, :] += jnp.sum(d_hid.astype(F32), 0, keepdims=True)
        keep_hidden(m).start()
        g_out[m % 2] = norm_back(dot(big[m, 0:rows], w1[...], 1, 1), m)

    def forward(m, run, first, last):
        if first:
            take_slab(tok_ref, m, x_in)
        else:
            next_hop(m).wait_recv()

        @pl.when(m >= 2)
        def _():
            finish_forward(m - 2, last)

        run(m)
        if last is True:
            result_start(m)
        elif last is False:
            next_hop(m).start()
        else:

            @pl.when(last)
            def _():
                result_start(m)

            @pl.when(jnp.logical_not(last))
            def _():
                next_hop(m).start()

    def finish_forward(m, last):
        if last is False:
            next_hop(m).wait_send()
        else:

            @pl.when(last)
            def _():
                result_wait(m)

            @pl.when(jnp.logical_not(last))
            def _():
                next_hop(m).wait_send()

    def backward(m, run, first, last):
        if last is False:
            back_hop(m).wait_recv()
        else:

            @pl.when(last)
            def _():
                take_slab(cot_ref, m, g_in)

            @pl.when(jnp.logical_not(last))
            def _():
                back_hop(m).wait_recv()

        @pl.when(m >= 2)
        def _():
            finish_backward(m - 2, first)

        run(m)
        if first:
            grad_here(m).start()
        else:
            back_hop(m).start()

    def finish_backward(m, first):
        if first:
            grad_here(m).wait()
        else:
            back_hop(m).wait_send()

    def pipeline(run_forward, run_backward, lag, first, last):
        def step(s, carry):
            @pl.when(s < micros)
            def _():
                forward(s, run_forward, first, last)

            @pl.when(s >= lag)
            def _():
                backward(s - lag, run_backward, first, last)

            return carry

        lax.fori_loop(0, micros + lag, step, 0)
        for m in (micros - 2, micros - 1):
            finish_forward(m, last)
            finish_backward(m, first)

    @pl.when(role == 0)
    def _():
        load_slab(tok_ref, 0).start()
        load_slab(tok_ref, 1).start()

    @pl.when(role == 3)
    def _():
        load_slab(cot_ref, 0).start()
        load_slab(cot_ref, 1).start()

    @pl.when(role % 2 == 1)
    def _():
        load_2.start()

    load_1.wait()
    pl.semaphore_wait(barrier, 3)

    @pl.when(role == 0)
    def _():
        tmp[rows:, :] = jnp.zeros((tmp.shape[0] - rows, 3 * D), F32)
        acc[rows:, :] = jnp.zeros((acc.shape[0] - rows, D), F32)
        pipeline(
            functools.partial(attention_forward, spatial=True),
            functools.partial(attention_backward, spatial=True),
            micros, True, False,
        )

    @pl.when(role == 2)
    def _():
        tmp[rows:, :] = jnp.zeros((tmp.shape[0] - rows, 3 * D), F32)
        acc[rows:, :] = jnp.zeros((acc.shape[0] - rows, D), F32)
        pipeline(
            functools.partial(attention_forward, spatial=False),
            functools.partial(attention_backward, spatial=False),
            2, False, False,
        )

    @pl.when(role % 2 == 0)
    def _():
        keep_left(1, micros - 1, att_low).wait()
        keep_wide(micros - 1, 0, 3 * D).wait()

        def kept(m, carry):
            keep_gout_right(m).wait()
            return carry

        lax.fori_loop(0, micros, kept, 0)

    @pl.when(role % 2 == 1)
    def _():
        load_2.wait()
        pipeline(feed_forward, feed_backward, jnp.where(role == 3, 0, micros), False, role == 3)
        keep_wide(micros - 1, FF, FF).wait()

        def kept(m, carry):
            keep_gout_left(m).wait()
            keep_hidden(m).wait()
            return carry

        lax.fori_loop(0, micros, kept, 0)

    keep_left(0, micros - 1, normed).wait()

    @pl.when(role != 3)
    def _():
        def arrived(n, carry):
            result_hop(n).wait_recv()
            return carry

        lax.fori_loop(0, share, arrived, 0)


def run_sections(tokens, cotangent, gain, shift, bias, bias_out, w1, w2, micros, rows, real):
    images = real // PATCHES
    tall = max((PATCHES * (images - 1) + PAD + 7) // 8 * 8, rows)
    share = micros // 4
    slab = min(rows + 16, tokens.shape[0])
    hbm = pl.BlockSpec(memory_space=pl.ANY)
    vmem = pl.BlockSpec(memory_space=pltpu.VMEM)
    dma = pltpu.SemaphoreType.DMA
    scratch = [
        pltpu.VMEM((D, FF), BF),
        pltpu.VMEM((FF, D), BF),
        pltpu.VMEM((micros, max(images * PAD, rows), FF), BF),
        pltpu.VMEM((micros * images, PAD, 3 * 512), BF),
        pltpu.VMEM((micros, rows, D), BF),
        pltpu.VMEM((micros, rows, D), BF),
        pltpu.VMEM((2, rows, D), BF),
        pltpu.VMEM((2, rows, D), BF),
        pltpu.VMEM((2, slab, D), BF),
        pltpu.VMEM((rows, D), BF),
        pltpu.VMEM((rows, D), BF),
        pltpu.VMEM((rows, FF), BF),
        pltpu.VMEM((tall, D), F32),
        pltpu.VMEM((tall, 3 * D), F32),
        dma((2,)), dma((2,)), dma((micros,)), dma((micros,)), dma((micros,)), dma((micros,)),
        dma((micros,)), dma((share,)), dma((3,)), dma((micros,)), dma((micros,)),
    ]
    out_shape = (
        jax.ShapeDtypeStruct((share, rows, D), BF),
        jax.ShapeDtypeStruct((micros, rows, D), BF),
        jax.ShapeDtypeStruct((2, micros * rows, D), BF),
        jax.ShapeDtypeStruct((micros * rows, 2 * FF), BF),
        jax.ShapeDtypeStruct((8, D), F32),
    )
    return pl.pallas_call(
        functools.partial(sections_kernel, micros, rows, real),
        out_shape=out_shape,
        in_specs=[hbm, hbm, vmem, vmem, vmem, vmem, hbm, hbm],
        out_specs=(hbm, hbm, hbm, hbm, vmem),
        scratch_shapes=scratch,
        compiler_params=pltpu.CompilerParams(
            collective_id=0, has_side_effects=True, vmem_limit_bytes=63 * 2**20
        ),
        cost_estimate=pl.CostEstimate(
            flops=2 * 4 * 2 * D * FF * micros * rows, bytes_accessed=60_000_000, transcendentals=0
        ),
        name="sections",
    )(tokens, cotangent, gain, shift, bias, bias_out, w1, w2)


X_LAG = 5
HOP = 3
RING = 4


def weights_kernel(
    inner, real,
    left_ref, right_ref, small, lo_ref, ig_ref,
    first_out, second_out, vec_ref, lo_out, ig_out,
    left, ring, part, from_x, from_z, vec_x, vec_z, lo_in, ig_in, joined, results, first_ref, second_ref,
    l_sem, r_sem, x_send, x_recv, z_send, z_recv, v_send, v_recv, h_sem, g_send, g_recv, o_sem,
):
    dp, role = lax.axis_index("dp"), lax.axis_index("pipe")
    feed = role % 2
    outer, rest = dp // inner, dp % inner
    z, x = outer // 2, outer % 2
    lines = MEMBERS // 2
    per = FF // WIDE
    steps = per + per * feed
    share = lo_in.shape[0]
    all_steps = steps + (lines - 1) * HOP + X_LAG

    def at(zz, xx):
        return ((zz * 2 + xx) * inner + rest, role)

    barrier = pltpu.get_barrier_semaphore()
    pl.semaphore_signal(barrier, inc=1, device_id=at(z, 1 - x), device_id_type=MESH)
    for i in range(1, lines):
        pl.semaphore_signal(barrier, inc=1, device_id=at((z + i) % lines, x), device_id_type=MESH)

    def load_left(n):
        return pltpu.make_async_copy(left_ref.at[n], left.at[n], l_sem.at[n])

    def load_right(k):
        cols = pl.ds(pl.multiple_of(k * WIDE, 128), WIDE)
        return pltpu.make_async_copy(right_ref.at[:, cols], ring.at[k % RING], r_sem.at[k % RING])

    @pl.when(role != 0)
    def _():
        pl.semaphore_signal(barrier, inc=1, device_id=(dp, 0), device_id_type=MESH)

    load_left(0).start()
    load_right(0).start()
    load_lo = pltpu.make_async_copy(lo_ref, lo_in, h_sem.at[0])
    load_ig = pltpu.make_async_copy(ig_ref.at[pl.ds(0, share)], ig_in, h_sem.at[1])

    def grads_to(n):
        return pltpu.make_async_remote_copy(
            src_ref=ig_ref.at[pl.ds(n * share, share)], dst_ref=ig_in, send_sem=g_send.at[n - 1], recv_sem=g_recv,
            device_id=(dp, n), device_id_type=MESH,
        )

    @pl.when(role == 0)
    def _():
        pl.semaphore_wait(barrier, lines + 3)
        load_ig.start()
        for n in range(1, 4):
            grads_to(n).start()

    @pl.when(role != 0)
    def _():
        pl.semaphore_wait(barrier, lines)

    def z_first(k):
        return jnp.where(feed == 1, k % 5 == 1, k == 0)

    def to_x(k):
        return pltpu.make_async_remote_copy(
            src_ref=part.at[k, :, 1 - x], dst_ref=from_x.at[k], send_sem=x_send.at[k], recv_sem=x_recv.at[k],
            device_id=at(z, 1 - x), device_id_type=MESH,
        )

    def block_to_x(k):
        return pltpu.make_async_remote_copy(
            src_ref=part.at[k, z, 1 - x], dst_ref=from_x.at[k, 0], send_sem=x_send.at[k], recv_sem=x_recv.at[k],
            device_id=at(z, 1 - x), device_id_type=MESH,
        )

    def hop(k, b, slot, target, whole):
        src = part.at[k, b] if whole else part.at[k, b, x]
        dst = from_z.at[k, slot] if whole else from_z.at[k, slot, 0]
        return pltpu.make_async_remote_copy(
            src_ref=src, dst_ref=dst, send_sem=z_send.at[k, b], recv_sem=z_recv.at[k, slot],
            device_id=at(target, x), device_id_type=MESH,
        )

    def up(k, b, whole):
        return hop(k, b, b, jnp.minimum(z + 1, lines - 1), whole)

    def down(k, b, whole):
        return hop(k, b, jnp.where(b == z - 1, lines, b), jnp.maximum(z - 1, 0), whole)

    def come(k, slot, whole):
        hop(k, 0, slot, z, whole).wait_recv()

    def add(k, b, slot, whole):
        come(k, slot, whole)
        if whole:
            part[k, b] = (part[k, b].astype(F32) + from_z[k, slot].astype(F32)).astype(BF)
        else:
            part[k, b, x] = (part[k, b, x].astype(F32) + from_z[k, slot, 0].astype(F32)).astype(BF)

    def in_range(k, whole):
        kind = z_first(k) if whole else jnp.logical_not(z_first(k))
        return (k >= 0) & (k < steps) & kind

    def put_first(k):
        place = pl.ds(pl.multiple_of((k % per) * WIDE, 128), WIDE)
        return pltpu.make_async_copy(first_ref.at[:, place], first_out.at[:, place], o_sem.at[k])

    def put_second(k):
        place = pl.ds(pl.multiple_of((k % per) * WIDE, 128), WIDE)
        return pltpu.make_async_copy(second_ref.at[:, place], second_out.at[:, place], o_sem.at[k])

    put_zeros = pltpu.make_async_copy(second_ref, second_out, o_sem.at[per])

    def write(k, total):
        place = pl.ds(pl.multiple_of((k % per) * WIDE, 128), WIDE)

        @pl.when(k < per)
        def _():
            first_ref[:, place] = total
            put_first(k).start()

        @pl.when(k >= per)
        def _():
            second_ref[:, place] = total
            put_second(k).start()

    def along_z(s, base, whole):
        k_up = s - base - HOP * z

        @pl.when(in_range(k_up, whole))
        def _():
            for b in range(1, lines):

                @pl.when(b > z)
                def _():
                    @pl.when(z > 0)
                    def _():
                        add(k_up, b, b, whole)

                    up(k_up, b, whole).start()

        k_down = s - base - HOP * (lines - 1 - z)

        @pl.when(in_range(k_down, whole))
        def _():
            for b in range(lines - 1):

                @pl.when(b < z)
                def _():
                    @pl.when(z < lines - 1)
                    def _():
                        add(k_down, b, b, whole)

                    down(k_down, b, whole).start()

        k_end = s - base - HOP * (lines - 1)

        @pl.when(in_range(k_end, whole))
        def _():
            @pl.when(z > 0)
            def _():
                add(k_end, z, z, whole)

            @pl.when(z < lines - 1)
            def _():
                add(k_end, z, lines, whole)

            if whole:
                block_to_x(k_end).start()
            else:
                write(k_end, part[k_end, z, x].astype(F32))

    vec_to_x = pltpu.make_async_remote_copy(
        src_ref=small, dst_ref=vec_x.at[0], send_sem=v_send.at[0], recv_sem=v_recv.at[0],
        device_id=at(z, 1 - x), device_id_type=MESH,
    )

    def vec_to_z(zz):
        return pltpu.make_async_remote_copy(
            src_ref=vec_x.at[1], dst_ref=vec_z.at[z], send_sem=v_send.at[1 + zz], recv_sem=v_recv.at[1 + z],
            device_id=at(zz, x), device_id_type=MESH,
        )

    def vec_arrived(zz):
        return pltpu.make_async_remote_copy(
            src_ref=vec_x.at[1], dst_ref=vec_z.at[zz], send_sem=v_send.at[1 + zz], recv_sem=v_recv.at[1 + zz],
            device_id=at(zz, x), device_id_type=MESH,
        )

    load_left(0).wait()
    for k in range(1, RING - 1):
        load_right(k).start()
    load_left(1).start()
    load_lo.start()
    edge = jnp.where(feed == 1, per, 3 * D // WIDE)

    def join(pieces, n):
        for i in range(share):
            joined[real * i : real * (i + 1), :] = pieces[i, :real].astype(F32)
        results[n] = joined[: results.shape[1], :].astype(BF)

    def step(s, carry):
        @pl.when(s < steps)
        def _():
            @pl.when(s == edge)
            def _():
                load_left(1).wait()

            load_right(s).wait()

            @pl.when(s + RING - 1 < steps)
            def _():
                load_right(s + RING - 1).start()

            product = dot(left[s // edge], ring[s % RING], 0, 0)
            part[s] = product.astype(BF).reshape(lines, 2, BLOCK, WIDE)

            @pl.when(jnp.logical_not(z_first(s)))
            def _():
                to_x(s).start()

        k_x = s - X_LAG

        @pl.when(in_range(k_x, False))
        def _():
            to_x(k_x).wait_recv()
            part[k_x, :, x] = (part[k_x, :, x].astype(F32) + from_x[k_x].astype(F32)).astype(BF)

        along_z(s, 0, True)
        along_z(s, X_LAG, False)
        k_out = s - (lines - 1) * HOP - X_LAG

        @pl.when(in_range(k_out, True))
        def _():
            block_to_x(k_out).wait_recv()
            write(k_out, part[k_out, z, x].astype(F32) + from_x[k_out, 0].astype(F32))

        @pl.when(s == 0)
        def _():
            vec_to_x.start()

            @pl.when(feed == 0)
            def _():
                second_ref[...] = jnp.zeros_like(second_ref)
                put_zeros.start()

        @pl.when(s == 2)
        def _():
            load_lo.wait()
            join(lo_in, 0)
            pltpu.make_async_copy(results.at[0], lo_out, h_sem.at[0]).start()

        @pl.when(s == all_steps - 2)
        def _():
            @pl.when(role == 0)
            def _():
                load_ig.wait()

            @pl.when(role != 0)
            def _():
                grads_to(1).wait_recv()

            join(ig_in, 1)
            pltpu.make_async_copy(results.at[1], ig_out, h_sem.at[1]).start()

        @pl.when(s == 4)
        def _():
            vec_to_x.wait_recv()
            vec_x[1] = small[...] + vec_x[0]
            for i in range(1, lines):
                vec_to_z((z + i) % lines).start()

        return carry

    lax.fori_loop(0, all_steps, step, 0)
    total = vec_x[1]
    for i in range(1, lines):
        zz = (z + i) % lines
        vec_arrived(zz).wait_recv()
        total += vec_z[zz]
        vec_to_z(zz).wait_send()
    vec_ref[...] = total
    vec_to_x.wait_send()

    def drain(k, carry):
        for whole in (False, True):

            @pl.when(in_range(k, whole))
            def _():
                (block_to_x(k) if whole else to_x(k)).wait_send()
                for b in range(lines):

                    @pl.when(b != z)
                    def _():
                        up(k, b, whole).wait_send()

        @pl.when(k < per)
        def _():
            put_first(k).wait()

        @pl.when(k >= per)
        def _():
            put_second(k).wait()

        return carry

    lax.fori_loop(0, steps, drain, 0)

    @pl.when(feed == 0)
    def _():
        put_zeros.wait()

    @pl.when(role == 0)
    def _():
        for n in range(1, 4):
            grads_to(n).wait_send()

    pltpu.make_async_copy(results.at[0], lo_out, h_sem.at[0]).wait()
    pltpu.make_async_copy(results.at[1], ig_out, h_sem.at[1]).wait()


def reduce_weights(left, right, small, lo, ig, inner, real):
    count = left.shape[1]
    lines = MEMBERS // 2
    per = FF // WIDE
    share = lo.shape[0]
    hbm = pl.BlockSpec(memory_space=pl.ANY)
    vmem = pl.BlockSpec(memory_space=pltpu.VMEM)
    dma = pltpu.SemaphoreType.DMA
    return pl.pallas_call(
        functools.partial(weights_kernel, inner, real),
        out_shape=(
            jax.ShapeDtypeStruct((BLOCK, FF), F32),
            jax.ShapeDtypeStruct((BLOCK, FF), F32),
            jax.ShapeDtypeStruct((8, D), F32),
            jax.ShapeDtypeStruct((share * real, D), BF),
            jax.ShapeDtypeStruct((share * real, D), BF),
        ),
        in_specs=[hbm, hbm, vmem, hbm, hbm],
        out_specs=(hbm, hbm, vmem, hbm, hbm),
        scratch_shapes=[
            pltpu.VMEM((2, count, D), BF),
            pltpu.VMEM((RING, count, WIDE), BF),
            pltpu.VMEM((2 * per, lines, 2, BLOCK, WIDE), BF),
            pltpu.VMEM((2 * per, lines, BLOCK, WIDE), BF),
            pltpu.VMEM((2 * per, lines + 1, 2, BLOCK, WIDE), BF),
            pltpu.VMEM((2, 8, D), F32),
            pltpu.VMEM((lines, 8, D), F32),
            pltpu.VMEM(lo.shape, BF),
            pltpu.VMEM(lo.shape, BF),
            pltpu.VMEM(((share * real + 7) // 8 * 8, D), F32),
            pltpu.VMEM((2, share * real, D), BF),
            pltpu.VMEM((BLOCK, FF), F32),
            pltpu.VMEM((BLOCK, FF), F32),
            dma((2,)), dma((RING,)), dma((2 * per,)), dma((2 * per,)),
            dma((2 * per, lines)), dma((2 * per, lines + 1)), dma((1 + lines,)), dma((1 + lines,)), dma((2,)),
            dma((3,)), dma(()), dma((2 * per,)),
        ],
        compiler_params=pltpu.CompilerParams(
            collective_id=1, has_side_effects=True, vmem_limit_bytes=63 * 2**20
        ),
        cost_estimate=pl.CostEstimate(
            flops=2 * 2 * D * FF * count, bytes_accessed=40_000_000, transcendentals=0
        ),
        name="weights",
    )(left, right, small, lo, ig)


def finish_kernel(
    groups, first, second, vec, lo, ig,
    first_out, second_out, lo_out, ig_out, gain_out, shift_out, bias_out, last_out,
    first_mid, second_mid, lo_mid, ig_mid, in_sem, out_sem,
):
    arrays = (
        (first, first_mid, first_out), (second, second_mid, second_out), (lo, lo_mid, lo_out), (ig, ig_mid, ig_out)
    )
    come = [pltpu.make_async_copy(src, mid, in_sem.at[n]) for n, (src, mid, _) in enumerate(arrays)]
    go = [pltpu.make_async_copy(mid, dst, out_sem.at[n]) for n, (_, mid, dst) in enumerate(arrays)]
    for copy in come:
        copy.start()
    dp = lax.axis_index("dp")
    size = D // groups
    turned = pltpu.roll(vec[...], lax.rem(D - dp * size, D), 1)
    gain_out[...] = turned[0:1, :size]
    shift_out[...] = turned[1:2, :size]
    last_out[...] = turned[2:3, :size]
    for n in range(4):
        @pl.when(dp // (groups // 4) == n)
        def _():
            shift = (dp % (groups // 4)) * (4 * size)
            bias_out[...] = pltpu.roll(vec[3 + n : 4 + n, :], lax.rem(D - shift, D), 1)[:, : 4 * size]

    for first_half, second_half in zip(come, go):
        first_half.wait()
        second_half.start()
    for copy in go:
        copy.wait()


def finish(first, second, vec, lo, ig, groups):
    hbm = pl.BlockSpec(memory_space=pl.ANY)
    vmem = pl.BlockSpec(memory_space=pltpu.VMEM)
    size = D // groups
    row = jax.ShapeDtypeStruct((1, size), F32)
    return pl.pallas_call(
        functools.partial(finish_kernel, groups),
        out_shape=(
            jax.ShapeDtypeStruct(first.shape, F32), jax.ShapeDtypeStruct(second.shape, F32),
            jax.ShapeDtypeStruct(lo.shape, BF), jax.ShapeDtypeStruct(ig.shape, BF),
            row, row, jax.ShapeDtypeStruct((1, 4 * size), F32), row,
        ),
        in_specs=[hbm, hbm, vmem, hbm, hbm],
        out_specs=(hbm, hbm, hbm, hbm, vmem, vmem, vmem, vmem),
        scratch_shapes=[
            pltpu.VMEM(first.shape, F32), pltpu.VMEM(second.shape, F32),
            pltpu.VMEM(lo.shape, BF), pltpu.VMEM(ig.shape, BF),
            pltpu.SemaphoreType.DMA((4,)), pltpu.SemaphoreType.DMA((4,)),
        ],
        name="finish",
    )(first, second, vec, lo, ig)


def on_device(tokens, cotangent, norm_gain, norm_shift, w_first, b_first, w_second, b_second):
    groups = lax.axis_size("dp")
    inner = groups // MEMBERS
    micros = MICROS
    real = tokens.shape[0] // micros
    rows = (real + 15) // 16 * 16
    lo, ig, left, right, small = run_sections(
        tokens, cotangent, norm_gain, norm_shift, b_first, b_second, w_first[0], w_second[0], micros, rows, real
    )
    g_first, g_second, vec, layer_out, input_grad = reduce_weights(left, right, small, lo, ig, inner, real)

    if inner > 1:
        members = [[o * inner + i for i in range(inner)] for o in range(MEMBERS)]

        def over_members(part, dim):
            return lax.psum_scatter(
                part, "dp", scatter_dimension=dim, axis_index_groups=members, tiled=True
            )

        g_first = over_members(g_first, 0)
        g_second = over_members(g_second, 0)
        vec = lax.psum(vec, "dp", axis_index_groups=members)

    g_first, g_second, layer_out, input_grad, g_gain, g_shift, g_bias, g_last = finish(
        g_first, g_second, vec, layer_out, input_grad, groups
    )
    return (layer_out, input_grad, g_gain, g_shift, g_first[None], g_bias, g_second.T[None], g_last)


def solution(mesh):
    in_specs = (
        P("dp", None), P("dp", None), P("pipe", None), P("pipe", None),
        P("pipe", None, None), P("pipe", None), P("pipe", None, None), P("pipe", None),
    )
    out_specs = (
        P(("dp", "pipe"), None), P(("dp", "pipe"), None), P("pipe", "dp"), P("pipe", "dp"),
        P("pipe", "dp", None), P("pipe", "dp"), P("pipe", None, "dp"), P("pipe", "dp"),
    )
    return jax.shard_map(
        on_device, mesh=mesh, in_specs=in_specs, out_specs=out_specs, check_vma=False
    )
```

```python
import functools

import jax
import jax.experimental.pallas as pl
import jax.experimental.pallas.tpu as pltpu
import jax.numpy as jnp
from jax import lax
from jax.sharding import PartitionSpec as P

D = 768
FF = 3072
PATCHES = 49
PAD = 64
EPS = 1e-05
SCALE = 32 ** (-0.5)
MICROS = 8
MEMBERS = 8
BLOCK = D // MEMBERS
CHUNK = 512
GROUPS = {True: 3, False: 6}
WIDE = 256
X_LAG = 5
HOP = 3
RING = 3
LINES = MEMBERS // 2
SLOTS = LINES + 1
PER = FF // WIDE
Z_FIRST = 5
MESH = pl.DeviceIdType.MESH
BF = jnp.bfloat16
F32 = jnp.float32


def dot(a, b, ca, cb):
    return lax.dot_general(a, b, (((ca,), (cb,)), ((), ())), preferred_element_type=F32)


def gelu_pair(h):
    cdf = 0.5 + 0.5 * lax.erf(h * 0.7071067811865476)
    bell = jnp.exp(-0.5 * h * h)
    return h * cdf, cdf + h * (0.3989422804014327 * bell)


def norm_parts(x):
    center = x - jnp.mean(x, -1, keepdims=True)
    inverse = lax.rsqrt(jnp.mean(center * center, -1, keepdims=True) + EPS)
    return center * inverse, inverse


def head_masks(width):
    lane = lax.broadcasted_iota(jnp.int32, (1, width), 1) // 32
    return [lane == h for h in range(width // 32)]


def spread(block, masks):
    return jnp.concatenate([jnp.where(m, block, jnp.zeros_like(block)) for m in masks], 0)


def gather_heads(stacked, masks):
    total = None
    for h, m in enumerate(masks):
        part = jnp.where(m, stacked[PAD * h : PAD * (h + 1)], 0.0)
        total = part if total is None else total + part
    return total


def spread_turned(block):
    turned = block.T
    twice = jnp.concatenate([turned, turned], 1)
    lane = lax.broadcasted_iota(jnp.int32, (1, 2 * PAD), 1) // PAD
    none = jnp.zeros((32, 2 * PAD), block.dtype)
    rows = []
    for h in range(8):
        part = jnp.where(lane == h % 2, twice[32 * h : 32 * (h + 1)], none)
        rows.append(jnp.concatenate([part if c == h // 2 else none for c in range(4)], 1))
    return jnp.concatenate(rows, 0)


WIDE_STARTS = range(0, D, 256)
STARTS = range(0, D, 128)


def heads_apart(stacked, values):
    four = head_masks(128)
    parts = []
    for n, s in enumerate(STARTS):
        cols = slice(256 * (n % 2), 256 * (n % 2) + 256)
        parts.append(gather_heads(dot(stacked[n // 2][:, cols], values[:, s : s + 128], 0, 0), four))
    return parts


def window_forward(qs, ks, vs):
    every = range(len(qs))
    row = lax.broadcasted_iota(jnp.int32, (PAD, 1), 0)
    scores = [
        [dot(ks[i][:, s : s + 256], spread_turned(qs[i][:, s : s + 256]), 1, 0) for s in WIDE_STARTS]
        for i in every
    ]
    probs = []
    for i in every:
        blocks = []
        for block in scores[i]:
            block = jnp.where(row < PATCHES, block, -1e30)
            e = jnp.exp((block - jnp.max(block, 0, keepdims=True)) * SCALE)
            blocks.append((e * (1.0 / jnp.sum(e, 0, keepdims=True))).astype(BF))
        probs.append(blocks)
    parts = [jnp.concatenate(heads_apart(probs[i], vs[i]), 1) for i in every]
    return probs, parts


def window_backward(qs, ks, vs, probs, d_atts):
    eight = head_masks(256)
    every = range(len(qs))
    d_probs = [
        [dot(vs[i][:, s : s + 256], spread_turned(d_atts[i][:, s : s + 256]), 1, 0) for s in WIDE_STARTS]
        for i in every
    ]
    d_v = [
        [dot(probs[i][n], spread(d_atts[i][:, s : s + 256], eight), 1, 0) for n, s in enumerate(WIDE_STARTS)]
        for i in every
    ]
    d_scores = []
    for i in every:
        blocks = []
        for n in range(len(WIDE_STARTS)):
            p = probs[i][n].astype(F32)
            product = p * d_probs[i][n]
            blocks.append((product - p * jnp.sum(product, 0, keepdims=True)).astype(BF))
        d_scores.append(blocks)
    d_k = [
        [dot(d_scores[i][n], spread(qs[i][:, s : s + 256], eight), 1, 0) * SCALE for n, s in enumerate(WIDE_STARTS)]
        for i in every
    ]
    d_q = [[part * SCALE for part in heads_apart(d_scores[i], ks[i])] for i in every]
    return [[jnp.concatenate(parts[i], 1) for parts in (d_q, d_k, d_v)] for i in every]


def compress(block, masks):
    total = None
    for h, m in enumerate(masks):
        part = jnp.where(m, block[32 * h : 32 * h + 32], 0.0)
        total = part if total is None else total + part
    return total


def diagonal_turned(block):
    turned = jnp.concatenate([block.T] * 4, 1)
    r = lax.broadcasted_iota(jnp.int32, (128, 128), 0) // 32
    c = lax.broadcasted_iota(jnp.int32, (128, 128), 1) // 32
    return jnp.where(r == c, turned, jnp.zeros_like(turned))


def channel_forward(qs, ks, vs):
    four = head_masks(128)
    every = range(len(qs))
    scores = [[dot(ks[i][:, s : s + 128], qs[i][:, s : s + 128], 0, 0) for s in STARTS] for i in every]
    scores = [jnp.concatenate([compress(block, four) for block in scores[i]], 1) for i in every]
    es = [jnp.exp((block - jnp.max(block, 0, keepdims=True)) * SCALE) for block in scores]
    probs = [(e * (1.0 / jnp.sum(e, 0, keepdims=True))).astype(BF) for e in es]
    parts = [
        jnp.concatenate([dot(vs[i][:, s : s + 128], spread(probs[i][:, s : s + 128], four), 1, 0) for s in STARTS], 1)
        for i in every
    ]
    return probs, parts


def channel_backward(qs, ks, vs, probs, d_atts):
    four = head_masks(128)
    every = range(len(qs))
    d_probs = [[dot(vs[i][:, s : s + 128], d_atts[i][:, s : s + 128], 0, 0) for s in STARTS] for i in every]
    d_v = [
        [dot(d_atts[i][:, s : s + 128], diagonal_turned(probs[i][:, s : s + 128]), 1, 0) for s in STARTS]
        for i in every
    ]
    d_scores = []
    for i in every:
        block = jnp.concatenate([compress(block, four) for block in d_probs[i]], 1)
        p = probs[i].astype(F32)
        product = p * block
        d_scores.append((product - p * jnp.sum(product, 0, keepdims=True)).astype(BF))
    d_q = [
        [dot(ks[i][:, s : s + 128], spread(d_scores[i][:, s : s + 128], four), 1, 0) * SCALE for s in STARTS]
        for i in every
    ]
    d_k = [
        [dot(qs[i][:, s : s + 128], diagonal_turned(d_scores[i][:, s : s + 128]), 1, 0) * SCALE for s in STARTS]
        for i in every
    ]
    return [[jnp.concatenate(parts[i], 1) for parts in (d_q, d_k, d_v)] for i in every]


def layer_kernel(
    micros, rows, real, inner,
    tok_ref, cot_ref, gain_ref, shift_ref, bias_ref, bias_out_ref, w1_ref, w2_ref,
    lo_ref, ig_ref, active_ref, first_out, second_out, vec_ref,
    w1, w2, big, flat, x_in, g_in, normed, v_out, g_out, raw, wide, acc, tmp, from_z, small_ref, vec_x, vec_z,
    w_sem, raw_sem, v_send, v_recv, g_send, g_recv, f_send, f_recv, i_recv, k_sem,
    r_sem, x_send, x_recv, z_send, z_recv, vec_send, vec_recv, o_sem, ready,
):
    dp, role = lax.axis_index("dp"), lax.axis_index("pipe")
    feed = role % 2
    outer, rest = dp // inner, dp % inner
    z, x = outer // 2, outer % 2
    count = micros * rows

    def at(zz, xx):
        return ((zz * 2 + xx) * inner + rest, role)

    images = real // PATCHES
    share = micros // 4
    slab = raw.shape[1]
    total = tok_ref.shape[0]

    barrier = pltpu.get_barrier_semaphore()
    for n in range(1, 4):
        pl.semaphore_signal(barrier, inc=1, device_id=(dp, (role + n) % 4), device_id_type=MESH)
    pl.semaphore_signal(barrier, inc=1, device_id=at(z, 1 - x), device_id_type=MESH)
    for n in range(1, LINES):
        pl.semaphore_signal(barrier, inc=1, device_id=at((z + n) % LINES, x), device_id_type=MESH)

    load_1 = pltpu.make_async_copy(w1_ref, w1, w_sem.at[0])
    load_2 = pltpu.make_async_copy(w2_ref, w2, w_sem.at[1])
    load_1.start()

    def owner(m):
        return m // share

    def first_row(m):
        return m * real

    def slab_start(m):
        return pl.multiple_of(jnp.minimum(first_row(m) // 16 * 16, total - slab), 16)

    def load_slab(ref, m):
        return pltpu.make_async_copy(ref.at[pl.ds(slab_start(m), slab)], raw.at[m % 2], raw_sem.at[m % 2])

    def take_slab(ref, m, dst):
        load_slab(ref, m).wait()
        shift = first_row(m) - slab_start(m)
        moved = pltpu.roll(raw[m % 2].astype(F32), slab - shift, 0)[:rows]
        row = lax.broadcasted_iota(jnp.int32, (rows, 1), 0)
        dst[m] = jnp.where(row < real, moved, 0.0).astype(BF)

        @pl.when(m + 2 < micros)
        def _():
            load_slab(ref, m + 2).start()

    small_ref[...] = jnp.zeros_like(small_ref)

    def keep_active(m):
        return pltpu.make_async_copy(wide, active_ref.at[m], k_sem)

    def again(m, copy):
        @pl.when(m > 0)
        def _():
            copy.wait()

    def next_hop(m):
        return pltpu.make_async_remote_copy(
            src_ref=v_out.at[m % 2], dst_ref=x_in.at[m], send_sem=v_send.at[m], recv_sem=v_recv.at[m],
            device_id=(dp, (role + 1) % 4), device_id_type=MESH,
        )

    def back_hop(m):
        return pltpu.make_async_remote_copy(
            src_ref=g_out.at[m % 2], dst_ref=g_in.at[m], send_sem=g_send.at[m], recv_sem=g_recv.at[m],
            device_id=(dp, (role + 3) % 4), device_id_type=MESH,
        )

    def result_hop(m, back):
        src, ref, recv = (g_out, ig_ref, i_recv) if back else (v_out, lo_ref, f_recv)
        return pltpu.make_async_remote_copy(
            src_ref=src.at[m % 2], dst_ref=ref.at[m % share], send_sem=f_send.at[m],
            recv_sem=recv.at[m % share], device_id=(dp, owner(m)), device_id_type=MESH,
        )

    def result_here(m, back):
        src, ref = (g_out, ig_ref) if back else (v_out, lo_ref)
        return pltpu.make_async_copy(src.at[m % 2], ref.at[m % share], f_send.at[m])

    def result_start(m, back):
        @pl.when(owner(m) == role)
        def _():
            result_here(m, back).start()

        @pl.when(owner(m) != role)
        def _():
            result_hop(m, back).start()

    def result_wait(m, back):
        @pl.when(owner(m) == role)
        def _():
            result_here(m, back).wait()

        @pl.when(owner(m) != role)
        def _():
            result_hop(m, back).wait_send()

    bias, bias_out = bias_ref[...], bias_out_ref[...]
    gain, shift_row = gain_ref[...], shift_ref[...]
    image_row = lax.broadcasted_iota(jnp.int32, (PAD, 1), 0)

    def norm_forward(m, x):
        scaled, _ = norm_parts(x)
        normed[m] = (scaled * gain + shift_row).astype(BF)

    def norm_back(d_normed, m):
        scaled, inverse = norm_parts(x_in[m].astype(F32))
        small_ref[0:1, :] += jnp.sum(d_normed * scaled, 0, keepdims=True)
        small_ref[1:2, :] += jnp.sum(d_normed, 0, keepdims=True)
        d_scaled = d_normed * gain
        mean = jnp.mean(d_scaled, -1, keepdims=True)
        cross = jnp.mean(d_scaled * scaled, -1, keepdims=True)
        return (g_in[m].astype(F32) + inverse * (d_scaled - mean - scaled * cross)).astype(BF)

    def cut(src, n, c):
        part = src[PATCHES * n : PATCHES * n + PAD, c : c + D]
        return jnp.where(image_row < PATCHES, part, 0.0).astype(BF)

    def place(i, n):
        return (3 * i + n) // 4 * PAD, (3 * i + n) % 4 * D

    def projected(m, some, n):
        parts = []
        for i in some:
            r, c = place(i, n)
            parts.append(big[m, r : r + PAD, c : c + D])
        return parts

    def probs_at(m, i, j, size):
        return pl.ds(pl.multiple_of(((m * images + i) * 6 + j) * PAD, PAD), size)

    def out_rows(m):
        return pl.ds(pl.multiple_of(m * rows, 16), rows)

    def attention_forward(m, spatial):
        x = x_in[m].astype(F32)
        norm_forward(m, x)
        for c in range(0, 3 * D, D):
            tmp[0:rows, c : c + D] = dot(normed[m], w1[:, c : c + D], 1, 0) + bias[:, c : c + D]
        for i in range(images):
            for n in range(3):
                r, c = place(i, n)
                big[m, r : r + PAD, c : c + D] = cut(tmp, i, n * D)

        for start in range(0, images, GROUPS[spatial]):
            some = range(start, min(start + GROUPS[spatial], images))
            qs, ks, vs = (projected(m, some, n) for n in range(3))
            if spatial:
                kept, parts = window_forward(qs, ks, vs)
                for i, blocks in zip(some, kept):
                    for j in range(6):
                        flat[probs_at(m, i, j, PAD), :] = blocks[j // 2][:, 256 * (j % 2) : 256 * (j % 2) + 256]
            else:
                kept, parts = channel_forward(qs, ks, vs)
                for i, block in zip(some, kept):
                    for j in range(3):
                        flat[probs_at(m, i, j, 32), :] = block[:, 256 * j : 256 * (j + 1)]
            for i, part in zip(some, parts):
                acc[PATCHES * i : PATCHES * i + PAD, :] = part
        acc[real:rows, :] = jnp.zeros((rows - real, D), F32)
        att_low = acc[0:rows, :].astype(BF)
        w2[out_rows(m), :] = att_low
        branch = dot(att_low, w1[:, 3 * D :], 1, 0) + bias[:, 3 * D :]
        v_out[m % 2] = (x + branch).astype(BF)

    def attention_backward(m, spatial):
        g = g_in[m]
        small_ref[6:7, :] += jnp.sum(g.astype(F32), 0, keepdims=True)
        acc[0:rows, :] = dot(g, w1[:, 3 * D :], 1, 1)
        for start in range(0, images, GROUPS[spatial]):
            some = range(start, min(start + GROUPS[spatial], images))
            qs, ks, vs = (projected(m, some, n) for n in range(3))
            d_atts = [cut(acc, i, 0) for i in some]
            if spatial:
                kept = [
                    [
                        jnp.concatenate([flat[probs_at(m, i, 2 * n + a, PAD), :] for a in range(2)], 1)
                        for n in range(3)
                    ]
                    for i in some
                ]
                grads = window_backward(qs, ks, vs, kept, d_atts)
            else:
                kept = [
                    jnp.concatenate([flat[probs_at(m, i, j, 32), :] for j in range(3)], 1) for i in some
                ]
                grads = channel_backward(qs, ks, vs, kept, d_atts)
            for i, parts in zip(some, grads):
                for n in range(3):
                    tmp[PATCHES * i : PATCHES * i + PAD, n * D : (n + 1) * D] = parts[n]
        tmp[real:rows, :] = jnp.zeros((rows - real, 3 * D), F32)
        for n in range(3):
            part = tmp[0:rows, n * D : (n + 1) * D]
            big[m, 0:rows, n * D : (n + 1) * D] = part.astype(BF)
            small_ref[3 + n : 4 + n, :] += jnp.sum(part, 0, keepdims=True)
        g_out[m % 2] = norm_back(dot(big[m, 0:rows, : 3 * D], w1[:, : 3 * D], 1, 1), m)

    def feed_forward(m):
        x = x_in[m].astype(F32)
        norm_forward(m, x)
        again(m, keep_active(m))
        for c in range(0, FF, CHUNK):
            hidden = dot(normed[m], w1[:, c : c + CHUNK], 1, 0) + bias[:, c : c + CHUNK]
            value, diff = gelu_pair(hidden)
            wide[:, c : c + CHUNK] = value.astype(BF)
            big[m, 0:rows, c : c + CHUNK] = diff.astype(BF)
        keep_active(m).start()
        v_out[m % 2] = (x + bias_out + dot(wide[...], w2[...], 1, 0)).astype(BF)

    def feed_backward(m):
        small_ref[2:3, :] += jnp.sum(g_in[m].astype(F32), 0, keepdims=True)
        for n in range(FF // D):
            c = n * D
            d_act = dot(g_in[m], w2[c : c + D, :], 1, 1)
            d_hid = (d_act * big[m, 0:rows, c : c + D].astype(F32)).astype(BF)
            big[m, 0:rows, c : c + D] = d_hid
            small_ref[3 + n : 4 + n, :] += jnp.sum(d_hid.astype(F32), 0, keepdims=True)
        g_out[m % 2] = norm_back(dot(big[m, 0:rows], w1[...], 1, 1), m)

    def forward(m, run, first, last):
        if first:
            take_slab(tok_ref, m, x_in)
        else:
            next_hop(m).wait_recv()

        @pl.when(m >= 2)
        def _():
            finish_forward(m - 2, last)

        run(m)
        if last is True:
            result_start(m, False)
        elif last is False:
            next_hop(m).start()
        else:

            @pl.when(last)
            def _():
                result_start(m, False)

            @pl.when(jnp.logical_not(last))
            def _():
                next_hop(m).start()

    def finish_forward(m, last):
        if last is False:
            next_hop(m).wait_send()
        else:

            @pl.when(last)
            def _():
                result_wait(m, False)

            @pl.when(jnp.logical_not(last))
            def _():
                next_hop(m).wait_send()

    def backward(m, run, first, last):
        if last is False:
            back_hop(m).wait_recv()
        else:

            @pl.when(last)
            def _():
                take_slab(cot_ref, m, g_in)

            @pl.when(jnp.logical_not(last))
            def _():
                back_hop(m).wait_recv()

        @pl.when(m >= 2)
        def _():
            finish_backward(m - 2, first)

        run(m)
        if first:
            result_start(m, True)
        else:
            back_hop(m).start()

    def finish_backward(m, first):
        if first:
            result_wait(m, True)
        else:
            back_hop(m).wait_send()

    def pipeline(run_forward, run_backward, lag, first, last):
        def step(s, carry):
            @pl.when(s < micros)
            def _():
                forward(s, run_forward, first, last)

            @pl.when(s >= lag)
            def _():
                backward(s - lag, run_backward, first, last)

            return carry

        lax.fori_loop(0, micros + lag, step, 0)

    @pl.when(role == 0)
    def _():
        load_slab(tok_ref, 0).start()
        load_slab(tok_ref, 1).start()

    @pl.when(role == 3)
    def _():
        load_slab(cot_ref, 0).start()
        load_slab(cot_ref, 1).start()

    @pl.when(role % 2 == 1)
    def _():
        load_2.start()

    load_1.wait()
    pl.semaphore_wait(barrier, 3 + LINES)

    @pl.when(role == 0)
    def _():
        tmp[rows:, :] = jnp.zeros((tmp.shape[0] - rows, 3 * D), F32)
        acc[rows:, :] = jnp.zeros((acc.shape[0] - rows, D), F32)
        pipeline(
            functools.partial(attention_forward, spatial=True),
            functools.partial(attention_backward, spatial=True),
            micros, True, False,
        )

    @pl.when(role == 2)
    def _():
        tmp[rows:, :] = jnp.zeros((tmp.shape[0] - rows, 3 * D), F32)
        acc[rows:, :] = jnp.zeros((acc.shape[0] - rows, D), F32)
        pipeline(
            functools.partial(attention_forward, spatial=False),
            functools.partial(attention_backward, spatial=False),
            2, False, False,
        )

    @pl.when(feed == 1)
    def _():
        load_2.wait()
        pipeline(feed_forward, feed_backward, jnp.where(role == 3, 0, micros), False, role == 3)
        keep_active(micros - 1).wait()

    steps = PER + PER * feed
    all_steps = steps + (LINES - 1) * HOP + X_LAG
    pl.semaphore_signal(ready, inc=1, device_id=at(z, 1 - x), device_id_type=MESH)

    def columns(k):
        return pl.ds(pl.multiple_of(k * WIDE, WIDE), WIDE)

    def load_active(k):
        j = k - PER
        return pltpu.make_async_copy(
            active_ref.at[:, :, columns(j)], x_in.at[:, :, columns(j % RING)], r_sem.at[j % RING]
        )

    @pl.when(feed == 1)
    def _():
        for j in range(RING):
            load_active(PER + j).start()

    def chunk_rows(k, xx, zz, size):
        return pl.ds(pl.multiple_of(((k * 2 + xx) * LINES + zz) * BLOCK, 32), size * BLOCK)

    def multiply(k):
        def put(left, right):
            product = dot(left.reshape(count, D), right.reshape(count, WIDE), 0, 0).astype(BF)
            product = product.reshape(LINES, 2, BLOCK, WIDE)
            for xx in range(2):
                flat[chunk_rows(k, xx, 0, LINES), :] = product[:, xx].reshape(LINES * BLOCK, WIDE)

        @pl.when((feed == 1) & (k < PER) | (feed == 0) & (k < 3 * D // WIDE))
        def _():
            put(normed[...], big[:, 0:rows, columns(k)])

        @pl.when((feed == 1) & (k >= PER))
        def _():
            load_active(k).wait()
            put(g_in[...], x_in[:, :, columns((k - PER) % RING)])

            @pl.when(k + RING < steps)
            def _():
                load_active(k + RING).start()

        @pl.when((feed == 0) & (k >= 3 * D // WIDE))
        def _():
            put(w2[0:count, :], g_in[:, :, columns(k - 3 * D // WIDE)])

    def z_first(k):
        return jnp.where(feed == 1, k % Z_FIRST == 1, k == 0)

    def extra(k):
        return 2 * PER + k // Z_FIRST

    def x_place(k, size):
        return w1.at[pl.ds(pl.multiple_of(k % 2 * (LINES * BLOCK), 32), size * BLOCK), columns(k // 2)]

    def along_x(k, src, size):
        return pltpu.make_async_remote_copy(
            src_ref=flat.at[src], dst_ref=x_place(k, size), send_sem=x_send.at[k], recv_sem=x_recv.at[k],
            device_id=at(z, 1 - x), device_id_type=MESH,
        )

    def to_x(k):
        return along_x(k, chunk_rows(k, 1 - x, 0, LINES), LINES)

    def block_to_x(k):
        return along_x(k, chunk_rows(k, 1 - x, z, 1), 1)

    def hop(k, b, slot, target, other):
        xx, row = (1 - x, extra(k)) if other else (x, k)
        return pltpu.make_async_remote_copy(
            src_ref=flat.at[chunk_rows(k, xx, b, 1)], dst_ref=from_z.at[row * SLOTS + slot],
            send_sem=z_send.at[row, b], recv_sem=z_recv.at[row, slot],
            device_id=at(target, x), device_id_type=MESH,
        )

    def up(k, b, other):
        return hop(k, b, b, jnp.minimum(z + 1, LINES - 1), other)

    def down(k, b, other):
        return hop(k, b, jnp.where(b == z - 1, LINES, b), jnp.maximum(z - 1, 0), other)

    def add(k, b, slot, whole):
        for other in (False, True)[: 1 + whole]:
            hop(k, 0, slot, z, other).wait_recv()
            xx, row = (1 - x, extra(k)) if other else (x, k)
            here = chunk_rows(k, xx, b, 1)
            flat[here, :] = (flat[here, :].astype(F32) + from_z[row * SLOTS + slot].astype(F32)).astype(BF)

    def in_range(k, whole):
        kind = z_first(k) if whole else jnp.logical_not(z_first(k))
        return (k >= 0) & (k < steps) & kind

    def result_place(k):
        return tmp.at[pl.ds(pl.multiple_of(k % 3 * BLOCK, 8), BLOCK), columns(k // 3)]

    def put_first(k):
        return pltpu.make_async_copy(result_place(k), first_out.at[:, columns(k)], o_sem.at[k])

    def put_second(k):
        return pltpu.make_async_copy(result_place(k), second_out.at[:, columns(k - PER)], o_sem.at[k])

    def write(k, total):
        result_place(k)[...] = total

        @pl.when(k < PER)
        def _():
            put_first(k).start()

        @pl.when(k >= PER)
        def _():
            put_second(k).start()

    def along_z(s, base, whole):
        halves = (False, True)[: 1 + whole]
        k_up = s - base - HOP * z

        @pl.when(in_range(k_up, whole))
        def _():
            for b in range(1, LINES):

                @pl.when(b > z)
                def _():
                    @pl.when(z > 0)
                    def _():
                        add(k_up, b, b, whole)

                    for other in halves:
                        up(k_up, b, other).start()

        k_down = s - base - HOP * (LINES - 1 - z)

        @pl.when(in_range(k_down, whole))
        def _():
            for b in range(LINES - 1):

                @pl.when(b < z)
                def _():
                    @pl.when(z < LINES - 1)
                    def _():
                        add(k_down, b, b, whole)

                    for other in halves:
                        down(k_down, b, other).start()

        k_end = s - base - HOP * (LINES - 1)

        @pl.when(in_range(k_end, whole))
        def _():
            @pl.when(z > 0)
            def _():
                add(k_end, z, z, whole)

            @pl.when(z < LINES - 1)
            def _():
                add(k_end, z, LINES, whole)

            if whole:
                block_to_x(k_end).start()
            else:
                write(k_end, flat[chunk_rows(k_end, x, z, 1), :].astype(F32))

    vec_to_x = pltpu.make_async_remote_copy(
        src_ref=small_ref, dst_ref=vec_x.at[0], send_sem=vec_send.at[0], recv_sem=vec_recv.at[0],
        device_id=at(z, 1 - x), device_id_type=MESH,
    )

    def vec_to_z(zz, slot):
        return pltpu.make_async_remote_copy(
            src_ref=vec_x.at[1], dst_ref=vec_z.at[slot], send_sem=vec_send.at[1 + zz],
            recv_sem=vec_recv.at[1 + slot], device_id=at(zz, x), device_id_type=MESH,
        )

    multiply(0)
    pl.semaphore_wait(ready, 1)

    def sums(s, carry):
        @pl.when(in_range(s, False))
        def _():
            to_x(s).start()

        @pl.when(s + 1 < steps)
        def _():
            multiply(s + 1)

        k_x = s - X_LAG

        @pl.when(in_range(k_x, False))
        def _():
            to_x(k_x).wait_recv()
            here = chunk_rows(k_x, x, 0, LINES)
            flat[here, :] = (flat[here, :].astype(F32) + x_place(k_x, LINES)[...].astype(F32)).astype(BF)

        along_z(s, 0, True)
        along_z(s, X_LAG, False)
        k_out = s - (LINES - 1) * HOP - X_LAG

        @pl.when(in_range(k_out, True))
        def _():
            block_to_x(k_out).wait_recv()
            write(k_out, flat[chunk_rows(k_out, x, z, 1), :].astype(F32) + x_place(k_out, 1)[...].astype(F32))

        @pl.when(s == 0)
        def _():
            vec_to_x.start()

        @pl.when(s == 4)
        def _():
            vec_to_x.wait_recv()
            vec_x[1] = small_ref[...] + vec_x[0]
            for i in range(1, LINES):
                vec_to_z((z + i) % LINES, z).start()

        return carry

    lax.fori_loop(0, all_steps, sums, 0)
    total = vec_x[1]
    for i in range(1, LINES):
        zz = (z + i) % LINES
        vec_to_z(zz, zz).wait_recv()
        total += vec_z[zz]
        vec_to_z(zz, z).wait_send()
    vec_ref[...] = total
    vec_to_x.wait_send()

    def drain(k, carry):
        for whole in (False, True):

            @pl.when(in_range(k, whole))
            def _():
                (block_to_x(k) if whole else to_x(k)).wait_send()
                for b in range(LINES):

                    @pl.when(b != z)
                    def _():
                        for other in (False, True)[: 1 + whole]:
                            up(k, b, other).wait_send()

        @pl.when(k < PER)
        def _():
            put_first(k).wait()

        @pl.when(k >= PER)
        def _():
            put_second(k).wait()

        return carry

    lax.fori_loop(0, steps, drain, 0)

    for m in (micros - 2, micros - 1):

        @pl.when(role == 3)
        def _():
            result_wait(m, False)

        @pl.when(role != 3)
        def _():
            next_hop(m).wait_send()

        @pl.when(role == 0)
        def _():
            result_wait(m, True)

        @pl.when(role != 0)
        def _():
            back_hop(m).wait_send()

    for n in range(share):

        @pl.when(role != 3)
        def _():
            result_hop(n, False).wait_recv()

        @pl.when(role != 0)
        def _():
            result_hop(n, True).wait_recv()


def run_layer(tokens, cotangent, gain, shift, bias, bias_out, w1, w2, micros, rows, real, inner):
    images = real // PATCHES
    tall = max((PATCHES * (images - 1) + PAD + 7) // 8 * 8, rows)
    share = micros // 4
    slab = min(rows + 16, tokens.shape[0])
    deep = max((3 * images + 3) // 4 * PAD, rows)
    hbm = pl.BlockSpec(memory_space=pl.ANY)
    vmem = pl.BlockSpec(memory_space=pltpu.VMEM)
    dma = pltpu.SemaphoreType.DMA
    chunks = 2 * PER
    extras = (chunks + Z_FIRST - 1) // Z_FIRST
    scratch = [
        pltpu.VMEM((D, FF), BF),
        pltpu.VMEM((FF, D), BF),
        pltpu.VMEM((micros, deep, FF), BF),
        pltpu.VMEM((max(micros * images * 6 * PAD, chunks * MEMBERS * BLOCK), WIDE), BF),
        pltpu.VMEM((micros, rows, D), BF),
        pltpu.VMEM((micros, rows, D), BF),
        pltpu.VMEM((micros, rows, D), BF),
        pltpu.VMEM((2, rows, D), BF),
        pltpu.VMEM((2, rows, D), BF),
        pltpu.VMEM((2, slab, D), BF),
        pltpu.VMEM((rows, FF), BF),
        pltpu.VMEM((tall, D), F32),
        pltpu.VMEM((tall, 3 * D), F32),
        pltpu.VMEM(((chunks + extras) * SLOTS, BLOCK, WIDE), BF),
        pltpu.VMEM((8, D), F32),
        pltpu.VMEM((2, 8, D), F32),
        pltpu.VMEM((LINES, 8, D), F32),
        dma((2,)), dma((2,)), dma((micros,)), dma((micros,)), dma((micros,)), dma((micros,)),
        dma((micros,)), dma((share,)), dma((share,)), dma(()),
        dma((RING,)), dma((chunks,)), dma((chunks,)), dma((chunks + extras, LINES)), dma((chunks + extras, SLOTS)),
        dma((1 + LINES,)), dma((1 + LINES,)), dma((chunks,)), pltpu.SemaphoreType.REGULAR,
    ]
    out_shape = (
        jax.ShapeDtypeStruct((share, rows, D), BF),
        jax.ShapeDtypeStruct((share, rows, D), BF),
        jax.ShapeDtypeStruct((micros, rows, FF), BF),
        jax.ShapeDtypeStruct((BLOCK, FF), F32),
        jax.ShapeDtypeStruct((BLOCK, FF), F32),
        jax.ShapeDtypeStruct((8, D), F32),
    )
    return pl.pallas_call(
        functools.partial(layer_kernel, micros, rows, real, inner),
        out_shape=out_shape,
        in_specs=[hbm, hbm, vmem, vmem, vmem, vmem, hbm, hbm],
        out_specs=(hbm, hbm, hbm, hbm, hbm, vmem),
        scratch_shapes=scratch,
        compiler_params=pltpu.CompilerParams(
            collective_id=0, has_side_effects=True, vmem_limit_bytes=64 * 2**20 - 2**17
        ),
        cost_estimate=pl.CostEstimate(
            flops=2 * 6 * 2 * D * FF * micros * rows, bytes_accessed=60_000_000, transcendentals=0
        ),
        name="layer",
    )(tokens, cotangent, gain, shift, bias, bias_out, w1, w2)


def finish_kernel(
    groups, real, first, second, vec, lo, ig,
    first_out, second_out, lo_out, ig_out, gain_out, shift_out, bias_out, last_out,
    first_mid, second_mid, pieces, whole, joined, in_sem, out_sem,
):
    dp, role = lax.axis_index("dp"), lax.axis_index("pipe")
    feed = role % 2
    come = [
        pltpu.make_async_copy(src, dst, in_sem.at[n])
        for n, (src, dst) in enumerate(
            ((lo, pieces.at[0]), (ig, pieces.at[1]), (first, first_mid), (second, second_mid))
        )
    ]
    go = [
        pltpu.make_async_copy(src, dst, out_sem.at[n])
        for n, (src, dst) in enumerate(
            ((whole.at[0], lo_out), (whole.at[1], ig_out), (first_mid, first_out), (second_mid, second_out))
        )
    ]
    for n in range(3):
        come[n].start()

    @pl.when(feed == 1)
    def _():
        come[3].start()

    @pl.when(feed == 0)
    def _():
        second_mid[...] = jnp.zeros_like(second_mid)
        go[3].start()

    size = D // groups
    turned = pltpu.roll(vec[...], lax.rem(D - dp * size, D), 1)
    gain_out[...] = turned[0:1, :size]
    shift_out[...] = turned[1:2, :size]
    last_out[...] = turned[2:3, :size]
    for n in range(4):
        @pl.when(dp // (groups // 4) == n)
        def _():
            shift = (dp % (groups // 4)) * (4 * size)
            bias_out[...] = pltpu.roll(vec[3 + n : 4 + n, :], lax.rem(D - shift, D), 1)[:, : 4 * size]

    for n in range(2):
        come[n].wait()
        for i in range(pieces.shape[1]):
            joined[real * i : real * (i + 1), :] = pieces[n, i, :real].astype(F32)
        whole[n] = joined[: whole.shape[1], :].astype(BF)
        go[n].start()
    come[2].wait()
    go[2].start()

    @pl.when(feed == 1)
    def _():
        come[3].wait()
        go[3].start()

    for copy in go:
        copy.wait()


def finish(first, second, vec, lo, ig, groups, real):
    hbm = pl.BlockSpec(memory_space=pl.ANY)
    vmem = pl.BlockSpec(memory_space=pltpu.VMEM)
    size = D // groups
    share = lo.shape[0]
    row = jax.ShapeDtypeStruct((1, size), F32)
    flat = jax.ShapeDtypeStruct((share * real, D), BF)
    return pl.pallas_call(
        functools.partial(finish_kernel, groups, real),
        out_shape=(
            jax.ShapeDtypeStruct(first.shape, F32), jax.ShapeDtypeStruct(second.shape, F32), flat, flat,
            row, row, jax.ShapeDtypeStruct((1, 4 * size), F32), row,
        ),
        in_specs=[hbm, hbm, vmem, hbm, hbm],
        out_specs=(hbm, hbm, hbm, hbm, vmem, vmem, vmem, vmem),
        scratch_shapes=[
            pltpu.VMEM(first.shape, F32), pltpu.VMEM(second.shape, F32),
            pltpu.VMEM((2,) + lo.shape, BF), pltpu.VMEM((2, share * real, D), BF),
            pltpu.VMEM(((share * real + 7) // 8 * 8, D), F32),
            pltpu.SemaphoreType.DMA((4,)), pltpu.SemaphoreType.DMA((4,)),
        ],
        compiler_params=pltpu.CompilerParams(vmem_limit_bytes=60 * 2**20),
        name="finish",
    )(first, second, vec, lo, ig)


def on_device(tokens, cotangent, norm_gain, norm_shift, w_first, b_first, w_second, b_second):
    groups = lax.axis_size("dp")
    inner = groups // MEMBERS
    micros = MICROS
    real = tokens.shape[0] // micros
    rows = (real + 15) // 16 * 16
    lo, ig, _, g_first, g_second, vec = run_layer(
        tokens, cotangent, norm_gain, norm_shift, b_first, b_second, w_first[0], w_second[0],
        micros, rows, real, inner,
    )

    if inner > 1:
        members = [[o * inner + i for i in range(inner)] for o in range(MEMBERS)]

        def over_members(part, dim):
            return lax.psum_scatter(
                part, "dp", scatter_dimension=dim, axis_index_groups=members, tiled=True
            )

        g_first = over_members(g_first, 0)
        g_second = over_members(g_second, 0)
        vec = lax.psum(vec, "dp", axis_index_groups=members)

    g_first, g_second, layer_out, input_grad, g_gain, g_shift, g_bias, g_last = finish(
        g_first, g_second, vec, lo, ig, groups, real
    )
    return (layer_out, input_grad, g_gain, g_shift, g_first[None], g_bias, g_second.T[None], g_last)


def solution(mesh):
    in_specs = (
        P("dp", None), P("dp", None), P("pipe", None), P("pipe", None),
        P("pipe", None, None), P("pipe", None), P("pipe", None, None), P("pipe", None),
    )
    out_specs = (
        P(("dp", "pipe"), None), P(("dp", "pipe"), None), P("pipe", "dp"), P("pipe", "dp"),
        P("pipe", "dp", None), P("pipe", "dp"), P("pipe", None, "dp"), P("pipe", "dp"),
    )
    return jax.shard_map(
        on_device, mesh=mesh, in_specs=in_specs, out_specs=out_specs, check_vma=False
    )
```

```python
import functools

import jax
import jax.experimental.pallas as pl
import jax.experimental.pallas.tpu as pltpu
import jax.numpy as jnp
from jax import lax
from jax.sharding import PartitionSpec as P

D = 768
FF = 3072
PATCHES = 49
PAD = 64
EPS = 1e-05
SCALE = 32 ** (-0.5)
MICROS = 8
MEMBERS = 8
BLOCK = D // MEMBERS
CHUNK = 512
GROUPS = {True: 3, False: 6}
WIDE = 256
X_LAG = 5
HOP = 3
RING = 3
LINES = MEMBERS // 2
SLOTS = LINES + 1
PER = FF // WIDE
Z_FIRST = 6
MESH = pl.DeviceIdType.MESH
BF = jnp.bfloat16
F32 = jnp.float32


def dot(a, b, ca, cb):
    return lax.dot_general(a, b, (((ca,), (cb,)), ((), ())), preferred_element_type=F32)


def gelu_pair(h):
    cdf = 0.5 + 0.5 * lax.erf(h * 0.7071067811865476)
    bell = jnp.exp(-0.5 * h * h)
    return h * cdf, cdf + h * (0.3989422804014327 * bell)


def norm_parts(x):
    center = x - jnp.mean(x, -1, keepdims=True)
    inverse = lax.rsqrt(jnp.mean(center * center, -1, keepdims=True) + EPS)
    return center * inverse, inverse


def head_masks(width):
    lane = lax.broadcasted_iota(jnp.int32, (1, width), 1) // 32
    return [lane == h for h in range(width // 32)]


def spread(block, masks):
    return jnp.concatenate([jnp.where(m, block, jnp.zeros_like(block)) for m in masks], 0)


def gather_heads(stacked, masks):
    total = None
    for h, m in enumerate(masks):
        part = jnp.where(m, stacked[PAD * h : PAD * (h + 1)], 0.0)
        total = part if total is None else total + part
    return total


def spread_turned(block):
    turned = block.T
    twice = jnp.concatenate([turned, turned], 1)
    lane = lax.broadcasted_iota(jnp.int32, (1, 2 * PAD), 1) // PAD
    none = jnp.zeros((32, 2 * PAD), block.dtype)
    rows = []
    for h in range(8):
        part = jnp.where(lane == h % 2, twice[32 * h : 32 * (h + 1)], none)
        rows.append(jnp.concatenate([part if c == h // 2 else none for c in range(4)], 1))
    return jnp.concatenate(rows, 0)


WIDE_STARTS = range(0, D, 256)
STARTS = range(0, D, 128)


def heads_apart(stacked, values):
    four = head_masks(128)
    parts = []
    for n, s in enumerate(STARTS):
        cols = slice(256 * (n % 2), 256 * (n % 2) + 256)
        parts.append(gather_heads(dot(stacked[n // 2][:, cols], values[:, s : s + 128], 0, 0), four))
    return parts


def window_forward(qs, ks, vs):
    every = range(len(qs))
    row = lax.broadcasted_iota(jnp.int32, (PAD, 1), 0)
    scores = [
        [dot(ks[i][:, s : s + 256], spread_turned(qs[i][:, s : s + 256]), 1, 0) for s in WIDE_STARTS]
        for i in every
    ]
    probs = []
    for i in every:
        blocks = []
        for block in scores[i]:
            block = jnp.where(row < PATCHES, block, -1e30)
            e = jnp.exp((block - jnp.max(block, 0, keepdims=True)) * SCALE)
            blocks.append((e * (1.0 / jnp.sum(e, 0, keepdims=True))).astype(BF))
        probs.append(blocks)
    parts = [jnp.concatenate(heads_apart(probs[i], vs[i]), 1) for i in every]
    return probs, parts


def window_backward(qs, ks, vs, probs, d_atts):
    eight = head_masks(256)
    every = range(len(qs))
    d_probs = [
        [dot(vs[i][:, s : s + 256], spread_turned(d_atts[i][:, s : s + 256]), 1, 0) for s in WIDE_STARTS]
        for i in every
    ]
    d_v = [
        [dot(probs[i][n], spread(d_atts[i][:, s : s + 256], eight), 1, 0) for n, s in enumerate(WIDE_STARTS)]
        for i in every
    ]
    d_scores = []
    for i in every:
        blocks = []
        for n in range(len(WIDE_STARTS)):
            p = probs[i][n].astype(F32)
            product = p * d_probs[i][n]
            blocks.append((product - p * jnp.sum(product, 0, keepdims=True)).astype(BF))
        d_scores.append(blocks)
    d_k = [
        [dot(d_scores[i][n], spread(qs[i][:, s : s + 256], eight), 1, 0) * SCALE for n, s in enumerate(WIDE_STARTS)]
        for i in every
    ]
    d_q = [[part * SCALE for part in heads_apart(d_scores[i], ks[i])] for i in every]
    return [[jnp.concatenate(parts[i], 1) for parts in (d_q, d_k, d_v)] for i in every]


def compress(block, masks):
    total = None
    for h, m in enumerate(masks):
        part = jnp.where(m, block[32 * h : 32 * h + 32], 0.0)
        total = part if total is None else total + part
    return total


def diagonal_turned(block):
    turned = jnp.concatenate([block.T] * 4, 1)
    r = lax.broadcasted_iota(jnp.int32, (128, 128), 0) // 32
    c = lax.broadcasted_iota(jnp.int32, (128, 128), 1) // 32
    return jnp.where(r == c, turned, jnp.zeros_like(turned))


def channel_forward(qs, ks, vs):
    four = head_masks(128)
    every = range(len(qs))
    scores = [[dot(ks[i][:, s : s + 128], qs[i][:, s : s + 128], 0, 0) for s in STARTS] for i in every]
    scores = [jnp.concatenate([compress(block, four) for block in scores[i]], 1) for i in every]
    es = [jnp.exp((block - jnp.max(block, 0, keepdims=True)) * SCALE) for block in scores]
    probs = [(e * (1.0 / jnp.sum(e, 0, keepdims=True))).astype(BF) for e in es]
    parts = [
        jnp.concatenate([dot(vs[i][:, s : s + 128], spread(probs[i][:, s : s + 128], four), 1, 0) for s in STARTS], 1)
        for i in every
    ]
    return probs, parts


def channel_backward(qs, ks, vs, probs, d_atts):
    four = head_masks(128)
    every = range(len(qs))
    d_probs = [[dot(vs[i][:, s : s + 128], d_atts[i][:, s : s + 128], 0, 0) for s in STARTS] for i in every]
    d_v = [
        [dot(d_atts[i][:, s : s + 128], diagonal_turned(probs[i][:, s : s + 128]), 1, 0) for s in STARTS]
        for i in every
    ]
    d_scores = []
    for i in every:
        block = jnp.concatenate([compress(block, four) for block in d_probs[i]], 1)
        p = probs[i].astype(F32)
        product = p * block
        d_scores.append((product - p * jnp.sum(product, 0, keepdims=True)).astype(BF))
    d_q = [
        [dot(ks[i][:, s : s + 128], spread(d_scores[i][:, s : s + 128], four), 1, 0) * SCALE for s in STARTS]
        for i in every
    ]
    d_k = [
        [dot(qs[i][:, s : s + 128], diagonal_turned(d_scores[i][:, s : s + 128]), 1, 0) * SCALE for s in STARTS]
        for i in every
    ]
    return [[jnp.concatenate(parts[i], 1) for parts in (d_q, d_k, d_v)] for i in every]


def layer_kernel(
    micros, rows, real, inner,
    tok_ref, cot_ref, gain_ref, shift_ref, bias_ref, bias_out_ref, w1_ref, w2_ref,
    lo_ref, ig_ref, active_ref, first_out, second_out, vec_ref,
    w1, w2, big, flat, x_in, g_in, normed, v_out, g_out, raw, wide, acc, tmp, from_z, small_ref, vec_x, vec_z,
    w_sem, raw_sem, v_send, v_recv, g_send, g_recv, f_send, f_recv, i_recv, k_sem,
    r_sem, x_send, x_recv, z_send, z_recv, vec_send, vec_recv, o_sem, ready,
):
    dp, role = lax.axis_index("dp"), lax.axis_index("pipe")
    feed = role % 2
    outer, rest = dp // inner, dp % inner
    z, x = outer // 2, outer % 2
    count = micros * rows

    def at(zz, xx):
        return ((zz * 2 + xx) * inner + rest, role)

    images = real // PATCHES
    share = micros // 4
    slab = raw.shape[0]
    total = tok_ref.shape[0]

    barrier = pltpu.get_barrier_semaphore()
    for n in range(1, 4):
        pl.semaphore_signal(barrier, inc=1, device_id=(dp, (role + n) % 4), device_id_type=MESH)
    pl.semaphore_signal(barrier, inc=1, device_id=at(z, 1 - x), device_id_type=MESH)
    for n in range(1, LINES):
        pl.semaphore_signal(barrier, inc=1, device_id=at((z + n) % LINES, x), device_id_type=MESH)

    load_1 = pltpu.make_async_copy(w1_ref, w1, w_sem.at[0])
    load_2 = pltpu.make_async_copy(w2_ref, w2, w_sem.at[1])
    load_1.start()

    def owner(m):
        return m // share

    def first_row(m):
        return m * real

    def slab_start(m):
        return pl.multiple_of(jnp.minimum(first_row(m) // 16 * 16, total - slab), 16)

    def load_slab(ref, m):
        return pltpu.make_async_copy(ref.at[pl.ds(slab_start(m), slab)], raw, raw_sem)

    def take_slab(ref, m, dst):
        load_slab(ref, m).wait()
        shift = first_row(m) - slab_start(m)
        moved = pltpu.roll(raw[...].astype(F32), slab - shift, 0)[:rows]
        row = lax.broadcasted_iota(jnp.int32, (rows, 1), 0)
        dst[m] = jnp.where(row < real, moved, 0.0).astype(BF)

        @pl.when(m + 1 < micros)
        def _():
            load_slab(ref, m + 1).start()

    small_ref[...] = jnp.zeros_like(small_ref)

    def keep_active(m):
        return pltpu.make_async_copy(wide, active_ref.at[m], k_sem)

    def again(m, copy):
        @pl.when(m > 0)
        def _():
            copy.wait()

    def next_hop(m):
        return pltpu.make_async_remote_copy(
            src_ref=v_out.at[m % 2], dst_ref=x_in.at[m], send_sem=v_send.at[m], recv_sem=v_recv.at[m],
            device_id=(dp, (role + 1) % 4), device_id_type=MESH,
        )

    def back_hop(m):
        return pltpu.make_async_remote_copy(
            src_ref=g_out.at[m % 2], dst_ref=g_in.at[m], send_sem=g_send.at[m], recv_sem=g_recv.at[m],
            device_id=(dp, (role + 3) % 4), device_id_type=MESH,
        )

    def result_hop(m, back):
        src, ref, recv = (g_out, ig_ref, i_recv) if back else (v_out, lo_ref, f_recv)
        return pltpu.make_async_remote_copy(
            src_ref=src.at[m % 2], dst_ref=ref.at[m % share], send_sem=f_send.at[m],
            recv_sem=recv.at[m % share], device_id=(dp, owner(m)), device_id_type=MESH,
        )

    def result_here(m, back):
        src, ref = (g_out, ig_ref) if back else (v_out, lo_ref)
        return pltpu.make_async_copy(src.at[m % 2], ref.at[m % share], f_send.at[m])

    def result_start(m, back):
        @pl.when(owner(m) == role)
        def _():
            result_here(m, back).start()

        @pl.when(owner(m) != role)
        def _():
            result_hop(m, back).start()

    def result_wait(m, back):
        @pl.when(owner(m) == role)
        def _():
            result_here(m, back).wait()

        @pl.when(owner(m) != role)
        def _():
            result_hop(m, back).wait_send()

    bias, bias_out = bias_ref[...], bias_out_ref[...]
    gain, shift_row = gain_ref[...], shift_ref[...]
    image_row = lax.broadcasted_iota(jnp.int32, (PAD, 1), 0)

    def norm_forward(m, x):
        scaled, _ = norm_parts(x)
        normed[m] = (scaled * gain + shift_row).astype(BF)

    def norm_back(d_normed, m):
        scaled, inverse = norm_parts(x_in[m].astype(F32))
        small_ref[0:1, :] += jnp.sum(d_normed * scaled, 0, keepdims=True)
        small_ref[1:2, :] += jnp.sum(d_normed, 0, keepdims=True)
        d_scaled = d_normed * gain
        mean = jnp.mean(d_scaled, -1, keepdims=True)
        cross = jnp.mean(d_scaled * scaled, -1, keepdims=True)
        return (g_in[m].astype(F32) + inverse * (d_scaled - mean - scaled * cross)).astype(BF)

    def cut(src, n, c):
        part = src[PATCHES * n : PATCHES * n + PAD, c : c + D]
        return jnp.where(image_row < PATCHES, part, 0.0).astype(BF)

    def place(i, n):
        return (3 * i + n) // 4 * PAD, (3 * i + n) % 4 * D

    def projected(m, some, n):
        parts = []
        for i in some:
            r, c = place(i, n)
            parts.append(big[m, r : r + PAD, c : c + D])
        return parts

    def probs_at(m, i, j, size):
        return pl.ds(pl.multiple_of(((m * images + i) * 6 + j) * PAD, PAD), size)

    def out_rows(m):
        return pl.ds(pl.multiple_of(m * rows, 16), rows)

    def attention_forward(m, spatial):
        x = x_in[m].astype(F32)
        norm_forward(m, x)
        for c in range(0, 3 * D, D):
            tmp[0:rows, c : c + D] = dot(normed[m], w1[:, c : c + D], 1, 0) + bias[:, c : c + D]
        for i in range(images):
            for n in range(3):
                r, c = place(i, n)
                big[m, r : r + PAD, c : c + D] = cut(tmp, i, n * D)

        for start in range(0, images, GROUPS[spatial]):
            some = range(start, min(start + GROUPS[spatial], images))
            qs, ks, vs = (projected(m, some, n) for n in range(3))
            if spatial:
                kept, parts = window_forward(qs, ks, vs)
                for i, blocks in zip(some, kept):
                    for j in range(6):
                        flat[probs_at(m, i, j, PAD), :] = blocks[j // 2][:, 256 * (j % 2) : 256 * (j % 2) + 256]
            else:
                kept, parts = channel_forward(qs, ks, vs)
                for i, block in zip(some, kept):
                    for j in range(3):
                        flat[probs_at(m, i, j, 32), :] = block[:, 256 * j : 256 * (j + 1)]
            for i, part in zip(some, parts):
                acc[PATCHES * i : PATCHES * i + PAD, :] = part
        acc[real:rows, :] = jnp.zeros((rows - real, D), F32)
        att_low = acc[0:rows, :].astype(BF)
        w2[out_rows(m), :] = att_low
        branch = dot(att_low, w1[:, 3 * D :], 1, 0) + bias[:, 3 * D :]
        v_out[m % 2] = (x + branch).astype(BF)

    def attention_backward(m, spatial):
        g = g_in[m]
        small_ref[6:7, :] += jnp.sum(g.astype(F32), 0, keepdims=True)
        acc[0:rows, :] = dot(g, w1[:, 3 * D :], 1, 1)
        for start in range(0, images, GROUPS[spatial]):
            some = range(start, min(start + GROUPS[spatial], images))
            qs, ks, vs = (projected(m, some, n) for n in range(3))
            d_atts = [cut(acc, i, 0) for i in some]
            if spatial:
                kept = [
                    [
                        jnp.concatenate([flat[probs_at(m, i, 2 * n + a, PAD), :] for a in range(2)], 1)
                        for n in range(3)
                    ]
                    for i in some
                ]
                grads = window_backward(qs, ks, vs, kept, d_atts)
            else:
                kept = [
                    jnp.concatenate([flat[probs_at(m, i, j, 32), :] for j in range(3)], 1) for i in some
                ]
                grads = channel_backward(qs, ks, vs, kept, d_atts)
            for i, parts in zip(some, grads):
                for n in range(3):
                    tmp[PATCHES * i : PATCHES * i + PAD, n * D : (n + 1) * D] = parts[n]
        tmp[real:rows, :] = jnp.zeros((rows - real, 3 * D), F32)
        for n in range(3):
            part = tmp[0:rows, n * D : (n + 1) * D]
            big[m, 0:rows, n * D : (n + 1) * D] = part.astype(BF)
            small_ref[3 + n : 4 + n, :] += jnp.sum(part, 0, keepdims=True)
        g_out[m % 2] = norm_back(dot(big[m, 0:rows, : 3 * D], w1[:, : 3 * D], 1, 1), m)

    def feed_forward(m):
        x = x_in[m].astype(F32)
        norm_forward(m, x)
        again(m, keep_active(m))
        def hidden_at(c):
            return dot(normed[m], w1[:, c : c + CHUNK], 1, 0) + bias[:, c : c + CHUNK]

        coming = hidden_at(0)
        total = x + bias_out
        for c in range(0, FF, CHUNK):
            hidden = coming
            if c + CHUNK < FF:
                coming = hidden_at(c + CHUNK)
            value, diff = gelu_pair(hidden)
            value = value.astype(BF)
            wide[:, c : c + CHUNK] = value
            big[m, 0:rows, c : c + CHUNK] = diff.astype(BF)
            total += dot(value, w2[c : c + CHUNK, :], 1, 0)
        keep_active(m).start()
        v_out[m % 2] = total.astype(BF)

    def feed_backward(m):
        small_ref[2:3, :] += jnp.sum(g_in[m].astype(F32), 0, keepdims=True)
        for n in range(FF // D):
            c = n * D
            d_act = dot(g_in[m], w2[c : c + D, :], 1, 1)
            d_hid = (d_act * big[m, 0:rows, c : c + D].astype(F32)).astype(BF)
            big[m, 0:rows, c : c + D] = d_hid
            small_ref[3 + n : 4 + n, :] += jnp.sum(d_hid.astype(F32), 0, keepdims=True)
        g_out[m % 2] = norm_back(dot(big[m, 0:rows], w1[...], 1, 1), m)

    def forward(m, run, first, last):
        if first:
            take_slab(tok_ref, m, x_in)
        else:
            next_hop(m).wait_recv()

        @pl.when(m >= 2)
        def _():
            finish_forward(m - 2, last)

        run(m)
        if last is True:
            result_start(m, False)
        elif last is False:
            next_hop(m).start()
        else:

            @pl.when(last)
            def _():
                result_start(m, False)

            @pl.when(jnp.logical_not(last))
            def _():
                next_hop(m).start()

    def finish_forward(m, last):
        if last is False:
            next_hop(m).wait_send()
        else:

            @pl.when(last)
            def _():
                result_wait(m, False)

            @pl.when(jnp.logical_not(last))
            def _():
                next_hop(m).wait_send()

    def backward(m, run, first, last):
        if last is False:
            back_hop(m).wait_recv()
        else:

            @pl.when(last)
            def _():
                take_slab(cot_ref, m, g_in)

            @pl.when(jnp.logical_not(last))
            def _():
                back_hop(m).wait_recv()

        @pl.when(m >= 2)
        def _():
            finish_backward(m - 2, first)

        run(m)
        if first:
            result_start(m, True)
        else:
            back_hop(m).start()

    def finish_backward(m, first):
        if first:
            result_wait(m, True)
        else:
            back_hop(m).wait_send()

    def pipeline(run_forward, run_backward, lag, first, last):
        def step(s, carry):
            @pl.when(s < micros)
            def _():
                forward(s, run_forward, first, last)

            @pl.when(s >= lag)
            def _():
                backward(s - lag, run_backward, first, last)

            return carry

        lax.fori_loop(0, micros + lag, step, 0)

    @pl.when(role == 0)
    def _():
        load_slab(tok_ref, 0).start()

    @pl.when(role == 3)
    def _():
        load_slab(cot_ref, 0).start()

    @pl.when(role % 2 == 1)
    def _():
        load_2.start()

    load_1.wait()
    pl.semaphore_wait(barrier, 3 + LINES)

    @pl.when(role == 0)
    def _():
        tmp[rows:, :] = jnp.zeros((tmp.shape[0] - rows, 3 * D), F32)
        acc[rows:, :] = jnp.zeros((acc.shape[0] - rows, D), F32)
        pipeline(
            functools.partial(attention_forward, spatial=True),
            functools.partial(attention_backward, spatial=True),
            micros, True, False,
        )

    @pl.when(role == 2)
    def _():
        tmp[rows:, :] = jnp.zeros((tmp.shape[0] - rows, 3 * D), F32)
        acc[rows:, :] = jnp.zeros((acc.shape[0] - rows, D), F32)
        pipeline(
            functools.partial(attention_forward, spatial=False),
            functools.partial(attention_backward, spatial=False),
            2, False, False,
        )

    @pl.when(feed == 1)
    def _():
        load_2.wait()
        pipeline(feed_forward, feed_backward, jnp.where(role == 3, 0, micros), False, role == 3)
        keep_active(micros - 1).wait()

    steps = PER + PER * feed
    all_steps = steps + (LINES - 1) * HOP + X_LAG
    pl.semaphore_signal(ready, inc=1, device_id=at(z, 1 - x), device_id_type=MESH)

    def columns(k):
        return pl.ds(pl.multiple_of(k * WIDE, WIDE), WIDE)

    def load_active(k):
        j = k - PER
        return pltpu.make_async_copy(
            active_ref.at[:, :, columns(j)], x_in.at[:, :, columns(j % RING)], r_sem.at[j % RING]
        )

    @pl.when(feed == 1)
    def _():
        for j in range(RING):
            load_active(PER + j).start()

    def chunk_rows(k, xx, zz, size):
        return pl.ds(pl.multiple_of(((k * 2 + xx) * LINES + zz) * BLOCK, 32), size * BLOCK)

    def multiply(k):
        def put(left, right):
            product = dot(left.reshape(count, D), right.reshape(count, WIDE), 0, 0).astype(BF)
            product = product.reshape(LINES, 2, BLOCK, WIDE)
            for xx in range(2):
                flat[chunk_rows(k, xx, 0, LINES), :] = product[:, xx].reshape(LINES * BLOCK, WIDE)

        @pl.when((feed == 1) & (k < PER) | (feed == 0) & (k < 3 * D // WIDE))
        def _():
            put(normed[...], big[:, 0:rows, columns(k)])

        @pl.when((feed == 1) & (k >= PER))
        def _():
            load_active(k).wait()
            put(g_in[...], x_in[:, :, columns((k - PER) % RING)])

            @pl.when(k + RING < steps)
            def _():
                load_active(k + RING).start()

        @pl.when((feed == 0) & (k >= 3 * D // WIDE))
        def _():
            put(w2[0:count, :], g_in[:, :, columns(k - 3 * D // WIDE)])

    def z_first(k):
        return jnp.where(feed == 1, k % Z_FIRST == 1, k == 0)

    def extra(k):
        return 2 * PER + k // Z_FIRST

    def x_place(k, size):
        return w1.at[pl.ds(pl.multiple_of(k % 2 * (LINES * BLOCK), 32), size * BLOCK), columns(k // 2)]

    def along_x(k, src, size):
        return pltpu.make_async_remote_copy(
            src_ref=flat.at[src], dst_ref=x_place(k, size), send_sem=x_send.at[k], recv_sem=x_recv.at[k],
            device_id=at(z, 1 - x), device_id_type=MESH,
        )

    def to_x(k):
        return along_x(k, chunk_rows(k, 1 - x, 0, LINES), LINES)

    def block_to_x(k):
        return along_x(k, chunk_rows(k, 1 - x, z, 1), 1)

    def hop(k, b, slot, target, other):
        xx, row = (1 - x, extra(k)) if other else (x, k)
        return pltpu.make_async_remote_copy(
            src_ref=flat.at[chunk_rows(k, xx, b, 1)], dst_ref=from_z.at[row * SLOTS + slot],
            send_sem=z_send.at[row, b], recv_sem=z_recv.at[row, slot],
            device_id=at(target, x), device_id_type=MESH,
        )

    def up(k, b, other):
        return hop(k, b, b, jnp.minimum(z + 1, LINES - 1), other)

    def down(k, b, other):
        return hop(k, b, jnp.where(b == z - 1, LINES, b), jnp.maximum(z - 1, 0), other)

    def add(k, b, slot, whole):
        for other in (False, True)[: 1 + whole]:
            hop(k, 0, slot, z, other).wait_recv()
            xx, row = (1 - x, extra(k)) if other else (x, k)
            here = chunk_rows(k, xx, b, 1)
            flat[here, :] = (flat[here, :].astype(F32) + from_z[row * SLOTS + slot].astype(F32)).astype(BF)

    def in_range(k, whole):
        kind = z_first(k) if whole else jnp.logical_not(z_first(k))
        return (k >= 0) & (k < steps) & kind

    def result_place(k):
        return tmp.at[pl.ds(pl.multiple_of(k % 3 * BLOCK, 8), BLOCK), columns(k // 3)]

    def put_first(k):
        return pltpu.make_async_copy(result_place(k), first_out.at[:, columns(k)], o_sem.at[k])

    def put_second(k):
        return pltpu.make_async_copy(result_place(k), second_out.at[:, columns(k - PER)], o_sem.at[k])

    def write(k, total):
        result_place(k)[...] = total

        @pl.when(k < PER)
        def _():
            put_first(k).start()

        @pl.when(k >= PER)
        def _():
            put_second(k).start()

    def along_z(s, base, whole):
        halves = (False, True)[: 1 + whole]
        k_up = s - base - HOP * z

        @pl.when(in_range(k_up, whole))
        def _():
            for b in range(1, LINES):

                @pl.when(b > z)
                def _():
                    @pl.when(z > 0)
                    def _():
                        add(k_up, b, b, whole)

                    for other in halves:
                        up(k_up, b, other).start()

        k_down = s - base - HOP * (LINES - 1 - z)

        @pl.when(in_range(k_down, whole))
        def _():
            for b in range(LINES - 1):

                @pl.when(b < z)
                def _():
                    @pl.when(z < LINES - 1)
                    def _():
                        add(k_down, b, b, whole)

                    for other in halves:
                        down(k_down, b, other).start()

        k_end = s - base - HOP * (LINES - 1)

        @pl.when(in_range(k_end, whole))
        def _():
            @pl.when(z > 0)
            def _():
                add(k_end, z, z, whole)

            @pl.when(z < LINES - 1)
            def _():
                add(k_end, z, LINES, whole)

            if whole:
                block_to_x(k_end).start()
            else:
                write(k_end, flat[chunk_rows(k_end, x, z, 1), :].astype(F32))

    vec_to_x = pltpu.make_async_remote_copy(
        src_ref=small_ref, dst_ref=vec_x.at[0], send_sem=vec_send.at[0], recv_sem=vec_recv.at[0],
        device_id=at(z, 1 - x), device_id_type=MESH,
    )

    def vec_to_z(zz, slot):
        return pltpu.make_async_remote_copy(
            src_ref=vec_x.at[1], dst_ref=vec_z.at[slot], send_sem=vec_send.at[1 + zz],
            recv_sem=vec_recv.at[1 + slot], device_id=at(zz, x), device_id_type=MESH,
        )

    multiply(0)
    pl.semaphore_wait(ready, 1)

    def sums(s, carry):
        @pl.when(in_range(s, False))
        def _():
            to_x(s).start()

        @pl.when(s + 1 < steps)
        def _():
            multiply(s + 1)

        k_x = s - X_LAG

        @pl.when(in_range(k_x, False))
        def _():
            to_x(k_x).wait_recv()
            here = chunk_rows(k_x, x, 0, LINES)
            flat[here, :] = (flat[here, :].astype(F32) + x_place(k_x, LINES)[...].astype(F32)).astype(BF)

        along_z(s, 0, True)
        along_z(s, X_LAG, False)
        k_out = s - (LINES - 1) * HOP - X_LAG

        @pl.when(in_range(k_out, True))
        def _():
            block_to_x(k_out).wait_recv()
            write(k_out, flat[chunk_rows(k_out, x, z, 1), :].astype(F32) + x_place(k_out, 1)[...].astype(F32))

        @pl.when(s == 0)
        def _():
            vec_to_x.start()

        @pl.when(s == 4)
        def _():
            vec_to_x.wait_recv()
            vec_x[1] = small_ref[...] + vec_x[0]
            for i in range(1, LINES):
                vec_to_z((z + i) % LINES, z).start()

        return carry

    lax.fori_loop(0, all_steps, sums, 0)
    total = vec_x[1]
    for i in range(1, LINES):
        zz = (z + i) % LINES
        vec_to_z(zz, zz).wait_recv()
        total += vec_z[zz]
        vec_to_z(zz, z).wait_send()
    vec_ref[...] = total
    vec_to_x.wait_send()

    def drain(k, carry):
        for whole in (False, True):

            @pl.when(in_range(k, whole))
            def _():
                (block_to_x(k) if whole else to_x(k)).wait_send()
                for b in range(LINES):

                    @pl.when(b != z)
                    def _():
                        for other in (False, True)[: 1 + whole]:
                            up(k, b, other).wait_send()

        @pl.when(k < PER)
        def _():
            put_first(k).wait()

        @pl.when(k >= PER)
        def _():
            put_second(k).wait()

        return carry

    lax.fori_loop(0, steps, drain, 0)

    for m in (micros - 2, micros - 1):

        @pl.when(role == 3)
        def _():
            result_wait(m, False)

        @pl.when(role != 3)
        def _():
            next_hop(m).wait_send()

        @pl.when(role == 0)
        def _():
            result_wait(m, True)

        @pl.when(role != 0)
        def _():
            back_hop(m).wait_send()

    for n in range(share):

        @pl.when(role != 3)
        def _():
            result_hop(n, False).wait_recv()

        @pl.when(role != 0)
        def _():
            result_hop(n, True).wait_recv()


def run_layer(tokens, cotangent, gain, shift, bias, bias_out, w1, w2, micros, rows, real, inner):
    images = real // PATCHES
    tall = max((PATCHES * (images - 1) + PAD + 7) // 8 * 8, rows)
    share = micros // 4
    slab = min(rows + 16, tokens.shape[0])
    deep = max((3 * images + 3) // 4 * PAD, rows)
    hbm = pl.BlockSpec(memory_space=pl.ANY)
    vmem = pl.BlockSpec(memory_space=pltpu.VMEM)
    dma = pltpu.SemaphoreType.DMA
    chunks = 2 * PER
    extras = (chunks + Z_FIRST - 1) // Z_FIRST
    scratch = [
        pltpu.VMEM((D, FF), BF),
        pltpu.VMEM((FF, D), BF),
        pltpu.VMEM((micros, deep, FF), BF),
        pltpu.VMEM((max(micros * images * 6 * PAD, chunks * MEMBERS * BLOCK), WIDE), BF),
        pltpu.VMEM((micros, rows, D), BF),
        pltpu.VMEM((micros, rows, D), BF),
        pltpu.VMEM((micros, rows, D), BF),
        pltpu.VMEM((2, rows, D), BF),
        pltpu.VMEM((2, rows, D), BF),
        pltpu.VMEM((slab, D), BF),
        pltpu.VMEM((rows, FF), BF),
        pltpu.VMEM((tall, D), F32),
        pltpu.VMEM((tall, 3 * D), F32),
        pltpu.VMEM(((chunks + extras) * SLOTS, BLOCK, WIDE), BF),
        pltpu.VMEM((8, D), F32),
        pltpu.VMEM((2, 8, D), F32),
        pltpu.VMEM((LINES, 8, D), F32),
        dma((2,)), dma(()), dma((micros,)), dma((micros,)), dma((micros,)), dma((micros,)),
        dma((micros,)), dma((share,)), dma((share,)), dma(()),
        dma((RING,)), dma((chunks,)), dma((chunks,)), dma((chunks + extras, LINES)), dma((chunks + extras, SLOTS)),
        dma((1 + LINES,)), dma((1 + LINES,)), dma((chunks,)), pltpu.SemaphoreType.REGULAR,
    ]
    out_shape = (
        jax.ShapeDtypeStruct((share, rows, D), BF),
        jax.ShapeDtypeStruct((share, rows, D), BF),
        jax.ShapeDtypeStruct((micros, rows, FF), BF),
        jax.ShapeDtypeStruct((BLOCK, FF), F32),
        jax.ShapeDtypeStruct((BLOCK, FF), F32),
        jax.ShapeDtypeStruct((8, D), F32),
    )
    return pl.pallas_call(
        functools.partial(layer_kernel, micros, rows, real, inner),
        out_shape=out_shape,
        in_specs=[hbm, hbm, vmem, vmem, vmem, vmem, hbm, hbm],
        out_specs=(hbm, hbm, hbm, hbm, hbm, vmem),
        scratch_shapes=scratch,
        compiler_params=pltpu.CompilerParams(
            collective_id=0, has_side_effects=True, vmem_limit_bytes=64 * 2**20 - 2**17
        ),
        cost_estimate=pl.CostEstimate(
            flops=2 * 6 * 2 * D * FF * micros * rows, bytes_accessed=60_000_000, transcendentals=0
        ),
        name="layer",
    )(tokens, cotangent, gain, shift, bias, bias_out, w1, w2)


def finish_kernel(
    groups, real, first, second, vec, lo, ig,
    first_out, second_out, lo_out, ig_out, gain_out, shift_out, bias_out, last_out,
    first_mid, second_mid, pieces, whole, joined, in_sem, out_sem,
):
    dp, role = lax.axis_index("dp"), lax.axis_index("pipe")
    feed = role % 2
    come = [
        pltpu.make_async_copy(src, dst, in_sem.at[n])
        for n, (src, dst) in enumerate(
            ((first, first_mid), (second, second_mid), (lo, pieces.at[0]), (ig, pieces.at[1]))
        )
    ]
    go = [
        pltpu.make_async_copy(src, dst, out_sem.at[n])
        for n, (src, dst) in enumerate(
            ((first_mid, first_out), (second_mid, second_out), (whole.at[0], lo_out), (whole.at[1], ig_out))
        )
    ]
    come[0].start()

    @pl.when(feed == 1)
    def _():
        come[1].start()

    come[2].start()
    come[3].start()

    @pl.when(feed == 0)
    def _():
        second_mid[...] = jnp.zeros_like(second_mid)
        go[1].start()

    size = D // groups
    turned = pltpu.roll(vec[...], lax.rem(D - dp * size, D), 1)
    gain_out[...] = turned[0:1, :size]
    shift_out[...] = turned[1:2, :size]
    last_out[...] = turned[2:3, :size]
    for n in range(4):
        @pl.when(dp // (groups // 4) == n)
        def _():
            shift = (dp % (groups // 4)) * (4 * size)
            bias_out[...] = pltpu.roll(vec[3 + n : 4 + n, :], lax.rem(D - shift, D), 1)[:, : 4 * size]

    come[0].wait()
    go[0].start()

    @pl.when(feed == 1)
    def _():
        come[1].wait()
        go[1].start()

    for n in range(2):
        come[2 + n].wait()
        for i in range(pieces.shape[1]):
            joined[real * i : real * (i + 1), :] = pieces[n, i, :real].astype(F32)
        whole[n] = joined[: whole.shape[1], :].astype(BF)
        go[2 + n].start()
    for copy in go:
        copy.wait()


def finish(first, second, vec, lo, ig, groups, real):
    hbm = pl.BlockSpec(memory_space=pl.ANY)
    vmem = pl.BlockSpec(memory_space=pltpu.VMEM)
    size = D // groups
    share = lo.shape[0]
    row = jax.ShapeDtypeStruct((1, size), F32)
    flat = jax.ShapeDtypeStruct((share * real, D), BF)
    return pl.pallas_call(
        functools.partial(finish_kernel, groups, real),
        out_shape=(
            jax.ShapeDtypeStruct(first.shape, F32), jax.ShapeDtypeStruct(second.shape, F32), flat, flat,
            row, row, jax.ShapeDtypeStruct((1, 4 * size), F32), row,
        ),
        in_specs=[hbm, hbm, vmem, hbm, hbm],
        out_specs=(hbm, hbm, hbm, hbm, vmem, vmem, vmem, vmem),
        scratch_shapes=[
            pltpu.VMEM(first.shape, F32), pltpu.VMEM(second.shape, F32),
            pltpu.VMEM((2,) + lo.shape, BF), pltpu.VMEM((2, share * real, D), BF),
            pltpu.VMEM(((share * real + 7) // 8 * 8, D), F32),
            pltpu.SemaphoreType.DMA((4,)), pltpu.SemaphoreType.DMA((4,)),
        ],
        compiler_params=pltpu.CompilerParams(vmem_limit_bytes=60 * 2**20),
        name="finish",
    )(first, second, vec, lo, ig)


def on_device(tokens, cotangent, norm_gain, norm_shift, w_first, b_first, w_second, b_second):
    groups = lax.axis_size("dp")
    inner = groups // MEMBERS
    micros = MICROS
    real = tokens.shape[0] // micros
    rows = (real + 15) // 16 * 16
    lo, ig, _, g_first, g_second, vec = run_layer(
        tokens, cotangent, norm_gain, norm_shift, b_first, b_second, w_first[0], w_second[0],
        micros, rows, real, inner,
    )

    if inner > 1:
        members = [[o * inner + i for i in range(inner)] for o in range(MEMBERS)]

        def over_members(part, dim):
            return lax.psum_scatter(
                part, "dp", scatter_dimension=dim, axis_index_groups=members, tiled=True
            )

        g_first = over_members(g_first, 0)
        g_second = over_members(g_second, 0)
        vec = lax.psum(vec, "dp", axis_index_groups=members)

    g_first, g_second, layer_out, input_grad, g_gain, g_shift, g_bias, g_last = finish(
        g_first, g_second, vec, lo, ig, groups, real
    )
    return (layer_out, input_grad, g_gain, g_shift, g_first[None], g_bias, g_second.T[None], g_last)


def solution(mesh):
    in_specs = (
        P("dp", None), P("dp", None), P("pipe", None), P("pipe", None),
        P("pipe", None, None), P("pipe", None), P("pipe", None, None), P("pipe", None),
    )
    out_specs = (
        P(("dp", "pipe"), None), P(("dp", "pipe"), None), P("pipe", "dp"), P("pipe", "dp"),
        P("pipe", "dp", None), P("pipe", "dp"), P("pipe", None, "dp"), P("pipe", "dp"),
    )
    return jax.shard_map(
        on_device, mesh=mesh, in_specs=in_specs, out_specs=out_specs, check_vma=False
    )
```
